32 devices in a mesh: dp: 8 (over z, x), expert: 4 (over y, core).
Axes of the slice: x: 2, y: 2, z: 4, core: 2. Of those that a mesh axis runs over, the one named last changes fastest.
Arguments:
- tokens: bfloat16 [4, 2048, 768], P('expert', 'dp'), may hold values from -6 to 6
- norm_attn: float32 [768], replicated, may hold values from 0.5 to 1.5
- query_key_value_weight: bfloat16 [768, 2304], replicated, may hold values from -0.21875 to 0.21875
- attention_output_weight: bfloat16 [768, 768], replicated, may hold values from -1.75 to 1.75
- norm_ffn: float32 [768], replicated, may hold values from 0.5 to 1.5
- router: bfloat16 [768, 8], replicated, may hold values from -0.15625 to 0.15625
- expert_in: bfloat16 [768, 8, 4096], P(None, 'expert'), may hold values from -0.21875 to 0.21875
- expert_out: bfloat16 [2048, 8, 768], P(None, 'expert'), may hold values from -0.125 to 0.125
- shared_gate_up_weight: bfloat16 [768, 4096], replicated, may hold values from -0.21875 to 0.21875
- shared_down_weight: bfloat16 [2048, 768], replicated, may hold values from -0.125 to 0.125
- block_lengths: int32 [4, 16], P('expert'), may hold values from 1 to 256, 2048 in all within a row
- routes: int32 [4, 2048, 2], P('expert', 'dp'), may hold values from 0 to 7, all different within a row
- cotangent: bfloat16 [4, 2048, 768], P('expert', 'dp'), may hold values from -6 to 6
Outputs:
- mixed: bfloat16 [4, 2048, 768], P('expert', 'dp')
- input_grad: float32 [4, 2048, 768], P('expert', 'dp')
- norm_attn_grad: float32 [768], P('dp')
- qkv_weight_grad: float32 [768, 2304], P('dp', 'expert')
- out_weight_grad: float32 [768, 768], P('dp', 'expert')
- norm_ffn_grad: float32 [768], P('dp')
- router_grad: float32 [768, 8], P('dp', 'expert')
- expert_in_grad: float32 [768, 8, 4096], P('dp', 'expert')
- expert_out_grad: float32 [2048, 8, 768], P('dp', 'expert')
- shared_in_grad: float32 [768, 4096], P('dp', 'expert')
- shared_out_grad: float32 [2048, 768], P('dp', 'expert')
The draws below stay inside these ranges and needn't reach their ends.
Inputs may be any that keep to these rules, and one draw needn't show every extreme that they name: `block_lengths`: each sequence's 16 block lengths sum to 2048, and the longest is 256. `routes`: each token names 2 different experts.
All inputs are finite; a program needn't handle non-finite values.
Results may differ from the reference program's by a relative error of at most 0.028.
Values may be sent and summed in bfloat16 or wider, within the bound.
No kernel may reach another device: no remote copies, remote signals or barrier semaphores. Data moves between devices by JAX's collectives and lax.ppermute only.
A program may use at most 256 MiB of HBM per device.

```python
import math
import jax
import jax.numpy as jnp
import numpy as np
from jax import lax

D = 768
HEADS = 12
HEAD_DIM = 64
FF = 2048
SHARED_FF = 2048
TOP = 2
BLOCK = 256
TOK_DEV = 256
EXPERTS = 8
LENGTH = 2048
SEQS = 4
BLOCKS = 16
CAP = 80
N_DP = 8


def with_spikes(values, own_key, source, target, blocks, factor):
    owner, partner = [(jnp.arange(values.shape[position]) // (values.shape[position] // blocks)).reshape([-1 if axis == position else 1 for axis in range(values.ndim)]) for position in (source, target)]
    chosen = jax.random.permutation(own_key, blocks)[partner]
    strong = (owner == chosen) | (owner == (partner + blocks // 2) % blocks)
    return jnp.where(strong, factor * values, values)


def shard_levels(stream_key, extent, shards, low, high):
    gain, own = 1.0, jax.random.fold_in(stream_key, 6)
    for axis_at, shards_of in shards:
        draws = jnp.exp(jax.random.uniform(jax.random.fold_in(own, axis_at), (shards_of,), jnp.float32, low / len(shards), high / len(shards)))
        gain = gain * jnp.repeat(draws, extent[axis_at] // shards_of).reshape([-1 if axis == axis_at else 1 for axis in range(len(extent))])
    return gain


def picks_of(own_key, rows, number_of, top, lift):
    sequence = jax.random.permutation(jax.random.fold_in(own_key, 1), number_of)
    favour = sequence
    for power in range(3):
        favour = favour * favour // number_of
    favour = favour * lift // number_of
    tickets = jax.random.randint(jax.random.fold_in(own_key, 2), (rows, number_of), 0, 4096) + favour
    fixed_rows = jax.random.permutation(jax.random.fold_in(own_key, 3), rows)[jnp.arange(number_of) % rows]
    tickets = jnp.where(jnp.arange(rows)[:, None] == fixed_rows[None, :], 1 << 14, tickets)
    score = tickets * number_of + jnp.arange(number_of)
    return lax.top_k(score.astype(jnp.int32), top)[1].astype(jnp.int32)


def split_up(number_of, total, bound, skew):
    weights = [(1 << 20) // math.isqrt(rank ** skew) + 1 for rank in range(2, number_of + 1)]
    surplus, counts = total - bound - (number_of - 1), [1] * (number_of - 1)
    while surplus > 0:
        candidates = [i for i in range(number_of - 1) if counts[i] < bound]
        pool, budget = sum([weights[i] for i in candidates]), surplus
        for i in candidates:
            more = min(bound - counts[i], max(1, budget * weights[i] // pool), surplus)
            counts[i] = counts[i] + more
            surplus = surplus - more
    return np.array([bound] + counts)


def uneven(stream_key, count, total, reach, lean):
    if count == 2:
        one = jax.random.randint(stream_key, (), max(1, total - reach), min(reach, total - 1) + 1)
        return jnp.stack([one, total - one])
    tallies = jnp.asarray(split_up(count, total, reach, lean), jnp.int32)
    pairs = (count - 1) // 2
    giver, sink = tallies[1:1 + 2 * pairs:2], tallies[2:2 + 2 * pairs:2]
    margin = jnp.minimum(giver - 1, reach - sink)
    moved = jax.random.randint(jax.random.fold_in(stream_key, 1), (pairs,), 0, 1 << 20) % (margin + 1)
    tallies = tallies.at[1:1 + 2 * pairs:2].set(giver - moved).at[2:2 + 2 * pairs:2].set(sink + moved)
    return tallies[jax.random.permutation(jax.random.fold_in(stream_key, 2), count)]


def normal_values(rng, dims, width, most, cuts=(), held_as=jnp.bfloat16):
    array = width * jax.random.normal(rng, dims, jnp.float32)
    if cuts:
        array = array * shard_levels(rng, dims, cuts, -0.22, 0.18)
    return jnp.clip(array, -most, most).astype(held_as)


def heavy_noise(rng, extent, scale, bound, shards, heavy, kind=jnp.bfloat16):
    array = scale * jax.random.normal(rng, extent, jnp.float32)
    if shards:
        array = array * shard_levels(rng, extent, shards, -0.22, 0.18)
    return jnp.clip(with_spikes(array, jax.random.fold_in(rng, 3), *heavy), -bound, bound).astype(kind)


def setup_inputs(seed: int = 0) -> dict:
    keys = jax.random.split(jax.random.key(seed), 14)
    return {
        "tokens": normal_values(keys[0], (SEQS, LENGTH, D), 1.0, 6.0, ((0, 4), (1, 8))),
        "norm_attn": jnp.clip(1.0 + 0.1 * jax.random.normal(keys[1], (D,), jnp.float32), 0.5, 1.5),
        "query_key_value_weight": normal_values(keys[2], (D, 3 * D), D ** -0.5, 0.21875),
        "attention_output_weight": normal_values(keys[3], (D, D), (D // 64) ** -0.5, 1.75),
        "norm_ffn": jnp.clip(1.0 + 0.1 * jax.random.normal(keys[4], (D,), jnp.float32), 0.5, 1.5),
        "router": normal_values(keys[5], (D, EXPERTS), (2 * D) ** -0.5, 0.15625),
        "expert_in": normal_values(keys[6], (D, EXPERTS, 2 * FF), D ** -0.5, 0.21875, ((1, 4),)),
        "expert_out": normal_values(keys[7], (FF, EXPERTS, D), FF ** -0.5, 0.125, ((1, 4),)),
        "shared_gate_up_weight": normal_values(keys[8], (D, 2 * SHARED_FF), D ** -0.5, 0.21875),
        "shared_down_weight": normal_values(keys[9], (SHARED_FF, D), SHARED_FF ** -0.5, 0.125),
        "block_lengths": jax.vmap(lambda own: uneven(own, BLOCKS, LENGTH, BLOCK, 1))(jax.random.split(keys[10], SEQS)).reshape((SEQS, BLOCKS)).astype(jnp.int32),
        "routes": picks_of(keys[11], SEQS * LENGTH, EXPERTS, TOP, 2048).reshape((SEQS, LENGTH, TOP)),
        "cotangent": heavy_noise(keys[12], (SEQS, LENGTH, D), 1.0, 6.0, ((0, 4), (1, 8)), (1, 2, 8, 2.0)),
    }


EPS = 1e-06
NEG = -1e+30
PRECISE_MATMUL = lax.Precision.HIGHEST

@jax.custom_vjp
def low(v):
    return lax.optimization_barrier(v.astype(jnp.bfloat16)).astype(jnp.float32)

@jax.custom_vjp
def low_back(v):
    return v

def low_keep(v):
    return (low(v), None)

def low_pass(kept, grad):
    return (grad,)

def back_keep(v):
    return (v, None)

def back_low(kept, grad):
    return (low(grad),)
low.defvjp(low_keep, low_pass)
low_back.defvjp(back_keep, back_low)

def rope_table(positions):
    half_dim = HEAD_DIM // 2
    frequency = 10000.0 ** (-jnp.arange(half_dim, dtype=jnp.float32) * 2.0 / HEAD_DIM)
    angles = positions.astype(jnp.float32)[:, None] * frequency[None, :]
    return (jnp.cos(angles)[:, None, :], jnp.sin(angles)[:, None, :])

def rotate(values, cosine, sine_table):
    half_dim = HEAD_DIM // 2
    first_half = values[..., :half_dim]
    second = values[..., half_dim:]
    return jnp.concatenate([first_half * cosine - second * sine_table, second * cosine + first_half * sine_table], axis=-1)

def rms_norm(hidden, gain_vector):
    return hidden * lax.rsqrt(lax.optimization_barrier(jnp.mean(hidden * hidden, axis=-1, keepdims=True)) + EPS) * gain_vector

def swiglu(pre_act, split_at):
    gate_half = pre_act[..., :split_at]
    return gate_half * jax.nn.sigmoid(gate_half) * pre_act[..., split_at:]

def masked_softmax(scores, visible):
    scores = jnp.where(visible, scores, NEG)
    shifted = scores - lax.optimization_barrier(jnp.max(scores, axis=-1, keepdims=True))
    powers = jnp.exp(shifted)
    return powers / lax.optimization_barrier(jnp.sum(powers, axis=-1, keepdims=True))

def attend(queries, key_heads, values, block_id):
    key_span = min(512, LENGTH)

    def one_block(inputs):
        query_block, query_ids = inputs
        scores = low_back(jnp.einsum('qhd,khd->hqk', query_block, key_heads, precision=PRECISE_MATMUL))
        visible = (query_ids[:, None] >= block_id[None, :])[None]
        weights_low = low(masked_softmax(scores, visible))
        return jnp.einsum('hqk,khd->qhd', weights_low, values, precision=PRECISE_MATMUL)
    result = lax.map(jax.checkpoint(one_block), (queries.reshape(LENGTH // key_span, key_span, HEADS, HEAD_DIM), block_id.reshape(LENGTH // key_span, key_span)))
    return result.reshape(LENGTH, HEADS, HEAD_DIM)

def forward(tokens, norm_attn, query_key_value_weight, attention_output_weight, norm_ffn, router, expert_in, expert_out, shared_gate_up_weight, shared_down_weight, block_id, routes):
    normalized_rows = low(rms_norm(tokens, norm_attn))
    projected_rows = low_back(jnp.einsum('ajx,xi->aji', normalized_rows, query_key_value_weight, precision=PRECISE_MATMUL))
    head_shape = (SEQS, LENGTH, HEADS, HEAD_DIM)
    cosine, sine_table = rope_table(jnp.arange(LENGTH, dtype=jnp.int32))
    queries = low(rotate(projected_rows[..., :D].reshape(head_shape), cosine, sine_table) * HEAD_DIM ** (-0.5))
    key_heads = low(rotate(projected_rows[..., D:2 * D].reshape(head_shape), cosine, sine_table))
    values = low(projected_rows[..., 2 * D:].reshape(head_shape))
    attention_result = lax.map(lambda entry: attend(entry[0], entry[1], entry[2], entry[3]), (queries, key_heads, values, block_id))
    attention_result = low_back(low(attention_result.reshape(SEQS, LENGTH, D)))
    residual_between = tokens + low_back(jnp.einsum('ajx,xi->aji', attention_result, attention_output_weight, precision=PRECISE_MATMUL))
    combined_input = low(rms_norm(residual_between, norm_ffn))
    router_scores = low_back(jnp.einsum('ajx,xi->aji', combined_input, router, precision=PRECISE_MATMUL))
    groups = SEQS * N_DP
    grouped = combined_input.reshape(groups, TOK_DEV, D)
    route_groups = routes.reshape(groups, TOK_DEV, TOP)
    picked = jnp.take_along_axis(router_scores.reshape(groups, TOK_DEV, EXPERTS), route_groups, axis=-1)
    shifted = picked - lax.optimization_barrier(jnp.max(picked, axis=-1, keepdims=True))
    powers = jnp.exp(shifted)
    gate_weights = powers / lax.optimization_barrier(jnp.sum(powers, axis=-1, keepdims=True))
    flat_routes = route_groups.reshape(groups, TOK_DEV * TOP)
    route_hot = (flat_routes[..., None] == jnp.arange(EXPERTS, dtype=jnp.int32)).astype(jnp.int32)
    earlier = jnp.cumsum(route_hot, axis=1).astype(jnp.int32) - route_hot
    slot_index = lax.optimization_barrier(jnp.sum(earlier * route_hot, axis=-1)).astype(jnp.int32)
    target = jnp.where(slot_index < CAP, flat_routes * CAP + slot_index, -1)
    dispatch = (target[..., None] == jnp.arange(EXPERTS * CAP, dtype=jnp.int32)).astype(jnp.float32)
    repeated = jnp.repeat(grouped, TOP, axis=1)
    expert_rows = low_back(jnp.einsum('grc,grd->cgd', dispatch, repeated, precision=PRECISE_MATMUL)).reshape(EXPERTS, CAP * groups, D)
    gate_up = low_back(jnp.einsum('erd,def->erf', expert_rows, expert_in, precision=PRECISE_MATMUL))
    activated = low(swiglu(gate_up, FF))
    result = low_back(low(jnp.einsum('erf,fed->erd', activated, expert_out, precision=PRECISE_MATMUL)))
    back_rows = jnp.einsum('grc,cgd->grd', dispatch, result.reshape(EXPERTS * CAP, groups, D), precision=PRECISE_MATMUL)
    routed = lax.optimization_barrier(jnp.sum(gate_weights[..., None] * back_rows.reshape(groups, TOK_DEV, TOP, D), axis=2)).reshape(SEQS, LENGTH, D)
    shared_preactivation = low_back(jnp.einsum('ani,ic->anc', combined_input, shared_gate_up_weight, precision=PRECISE_MATMUL))
    shared_activation = low(swiglu(shared_preactivation, SHARED_FF))
    shared_feedforward_output = jnp.einsum('har,rn->han', shared_activation, shared_down_weight, precision=PRECISE_MATMUL)
    return residual_between + routed + shared_feedforward_output

def reference(tokens, norm_attn, query_key_value_weight, attention_output_weight, norm_ffn, router, expert_in, expert_out, shared_gate_up_weight, shared_down_weight, block_lengths, routes, cotangent):
    bounds = jnp.cumsum(block_lengths, axis=1).astype(jnp.int32)
    places = jnp.arange(LENGTH, dtype=jnp.int32)
    block_id = lax.optimization_barrier(jnp.sum((bounds[:, None, :] <= places[None, :, None]).astype(jnp.int32), axis=2)).astype(jnp.int32)
    floats = (tokens.astype(jnp.float32), norm_attn.astype(jnp.float32), query_key_value_weight.astype(jnp.float32), attention_output_weight.astype(jnp.float32), norm_ffn.astype(jnp.float32), router.astype(jnp.float32), expert_in.astype(jnp.float32), expert_out.astype(jnp.float32), shared_gate_up_weight.astype(jnp.float32), shared_down_weight.astype(jnp.float32))

    def closed(*entries):
        return forward(*entries, block_id, routes)
    mixed, pullback = jax.vjp(closed, *floats)
    gradients = pullback(cotangent.astype(jnp.float32))
    return (mixed.astype(jnp.bfloat16), gradients[0], gradients[1], gradients[2], gradients[3], gradients[4], gradients[5], gradients[6], gradients[7], gradients[8], gradients[9])
```

```python
import functools

import jax
import jax.numpy as jnp
from jax import lax
from jax.experimental import pallas as pl
from jax.experimental.pallas import tpu as pltpu
from jax.sharding import Mesh
from jax.sharding import PartitionSpec as P

HEADS = 12
HEAD_DIM = 64
TOP = 2
EPS = 1e-06
NEG = -1e30
F32 = jnp.float32
BF16 = jnp.bfloat16
STEPS = 8
DP = ("g", "r")
EX = ("y", "c")


def rope_table(positions):
    half_dim = HEAD_DIM // 2
    frequency = 10000.0 ** (-jnp.arange(half_dim, dtype=F32) * 2.0 / HEAD_DIM)
    angles = positions.astype(F32)[:, None] * frequency[None, :]
    return (jnp.cos(angles)[:, None, :], jnp.sin(angles)[:, None, :])


def rotate(values, cosine, sine_table, direction):
    half_dim = HEAD_DIM // 2
    first_half = values[..., :half_dim]
    second = values[..., half_dim:]
    return jnp.concatenate(
        [
            first_half * cosine - direction * second * sine_table,
            second * cosine + direction * first_half * sine_table,
        ],
        axis=-1,
    )


def block_ids(bounds, positions):
    return jnp.sum((bounds[None, :] <= positions[:, None]).astype(jnp.int32), axis=1)


def rms_scale(hidden):
    return lax.rsqrt(jnp.mean(hidden * hidden, axis=-1, keepdims=True) + EPS)


def rms_back(hidden, scale_rows, gain_vector, upstream):
    normed_grad = upstream * gain_vector
    inner_mean = jnp.mean(normed_grad * hidden, axis=-1, keepdims=True)
    return scale_rows * normed_grad - hidden * scale_rows**3 * inner_mean


def masked_scores(queries, key_heads, query_ids, key_ids):
    scores = jnp.einsum("qhd,khd->hqk", queries, key_heads, preferred_element_type=F32)
    visible = query_ids[:, None] >= key_ids[None, :]
    return (jnp.where(visible[None], scores, NEG), visible)


def score_grads(queries, grad_out, log_total, row_delta, key_heads, values, query_ids, key_ids):
    scores, visible = masked_scores(queries, key_heads, query_ids, key_ids)
    weights_full = jnp.where(visible[None], jnp.exp(scores - log_total.T[:, :, None]), 0.0)
    grad_weights = jnp.einsum("qhd,khd->hqk", grad_out, values, preferred_element_type=F32)
    grad_scores = (weights_full * (grad_weights - row_delta.T[:, :, None])).astype(BF16)
    return (weights_full.astype(BF16), grad_scores)


class Place:
    def __init__(self):
        self.groups, self.lanes = lax.axis_size("g"), lax.axis_size("r")
        self.rows_y = lax.axis_size("y")
        self.dp = self.groups * self.lanes
        self.experts = self.rows_y * 2
        self.g, self.r = lax.axis_index("g"), lax.axis_index("r")
        self.y, self.c = lax.axis_index("y"), lax.axis_index("c")
        self.low, self.high = self.g % 2, self.g // 2

    def own(self, b):
        g, r = b // self.lanes, b % self.lanes
        low, high = g % 2, g // 2
        if self.lanes == 2:
            return r ^ self.r, low * 2 + high
        return low ^ self.low, high * self.lanes + r

    def flat(self, b):
        g, r = b // self.lanes, b % self.lanes
        if self.lanes == 2:
            return r * 4 + (g % 2) * 2 + g // 2
        return (g % 2 * 2 + g // 2) * self.lanes + r

    def expert_table(self, width):
        sub = STEPS // 4
        order = []
        for pos in range(STEPS):
            half, rest = pos // 4, pos % 4
            if self.lanes == 2:
                low, high, part = rest // 2, rest % 2, half ^ self.r
            else:
                low, high, part = half ^ self.low, rest // 2, rest % 2
            order.append((high * 2 + low) * sub + part)
        block = width // self.dp
        rows = []
        for b in range(self.dp):
            half, rest = self.own(b)
            rows.append(half * (width // 2) + rest * block)
        return jnp.stack([jnp.asarray(v, jnp.int32) for v in order + [0] * STEPS + rows])

    def shared_table(self, width):
        per = 16 // self.experts
        order, columns = [], []
        sub = STEPS // 4
        for pos in range(STEPS):
            half, rest = pos // 4, pos % 4
            j = (rest // per * 2 + (half ^ self.c)) * per + rest % per
            order.append(j)
            g, part = j // sub, j % sub
            if self.lanes == 2:
                columns.append(part * 4 + g % 2 * 2 + g // 2)
            else:
                columns.append((g % 2 * 2 + g // 2) * sub + part)
        block = width // self.dp
        rows = [self.flat(b) * block for b in range(self.dp)]
        own = width // self.experts
        turned = [
            (e % 2 ^ self.c) * (width // 2) + e // 2 * own for e in range(self.experts)
        ]
        return jnp.stack(
            [jnp.asarray(v, jnp.int32) for v in order + columns + rows + turned]
        )


def nt(a, b):
    return lax.dot_general(a, b, (((1,), (1,)), ((), ())), preferred_element_type=F32)


def nn(a, b):
    return lax.dot_general(a, b, (((1,), (0,)), ((), ())), preferred_element_type=F32)


def ffn_kernel(shared, dp, experts, table, x_ref, dy_ref, gate_ref, up_ref, down_ref, *refs):
    if shared:
        result, back, in_keep, in_send, out_keep, out_send, stage, turned, turned_dy = refs
    else:
        both, in_keep, in_send, out_keep, out_send, stage, turned, result, back = refs
    step = pl.program_id(0)
    width = x_ref.shape[1]
    rows = x_ref.shape[0]

    @pl.when(step == 0)
    def _():
        whole = x_ref[...].astype(F32).T
        block = width // dp
        for b in range(dp):
            start = pl.multiple_of(table[2 * STEPS + b], 8)
            stage[pl.ds(start, block), :] = whole[b * block : (b + 1) * block]
        turned[...] = stage[...].astype(BF16)
        if shared:
            whole = dy_ref[...].astype(F32).T
            block = width // experts
            for e in range(experts):
                start = pl.multiple_of(table[2 * STEPS + dp + e], 8)
                stage[pl.ds(start, block), :] = whole[e * block : (e + 1) * block]
            turned_dy[...] = stage[...].astype(BF16)
        result[...] = jnp.zeros_like(result)
        back[...] = jnp.zeros_like(back)

    x, dy = x_ref[...], dy_ref[...]
    w_gate, w_up, w_down = gate_ref[0], up_ref[0], down_ref[0]
    gate, up = nn(x, w_gate), nn(x, w_up)
    grad = nt(dy, w_down)
    sig = jax.nn.sigmoid(gate)
    silu = gate * sig
    act = (silu * up).astype(BF16)
    grad_gate = (grad * up * (sig * (1.0 + gate * (1.0 - sig)))).astype(BF16)
    grad_up = (grad * silu).astype(BF16)
    result[...] += nn(act, w_down)
    back[...] += nt(grad_gate, w_gate) + nt(grad_up, w_up)
    xt = turned[...]
    half = width // 2
    for k, upper in enumerate((grad_gate, grad_up)):
        grad_in = nn(xt, upper).astype(BF16)
        if shared:

            @pl.when(step < STEPS // 2)
            def _():
                in_keep[k] = grad_in

            @pl.when(step >= STEPS // 2)
            def _():
                in_send[k] = grad_in

        else:
            in_keep[k] = grad_in[:half]
            in_send[k] = grad_in[half:]
    if shared:
        grad_out = nn(turned_dy[...], act).astype(BF16)
        out_keep[...] = grad_out[:half]
        out_send[...] = grad_out[half:]
    else:
        grad_out = lax.dot_general(
            act, dy, (((0,), (0,)), ((), ())), preferred_element_type=F32
        ).astype(BF16)

        @pl.when(step < STEPS // 2)
        def _():
            out_keep[...] = grad_out

        @pl.when(step >= STEPS // 2)
        def _():
            out_send[...] = grad_out

        @pl.when(step == STEPS - 1)
        def _():
            both[:, :width] = result[...].astype(BF16)
            both[:, width:] = back[...].astype(BF16)


def ffn(shared, place, table, x, dy, w_in, w_out, e):
    rows, width = x.shape
    hidden = w_out.shape[1]
    chunk = hidden // STEPS
    near, far = STEPS // 2 - 1, STEPS // 2
    sds = jax.ShapeDtypeStruct
    first = lambda i, t: (0, 0, jnp.minimum(i, near))
    second = lambda i, t: (0, 0, jnp.maximum(i - far, 0))
    if shared:
        out_shape = (
            sds((rows, width), F32),
            sds((rows, width), F32),
            sds((2, width, hidden // 2), BF16),
            sds((2, width, hidden // 2), BF16),
            sds((width // 2, hidden), BF16),
            sds((width // 2, hidden), BF16),
        )
        out_specs = (
            pl.BlockSpec((rows, width), lambda i, t: (0, 0)),
            pl.BlockSpec((rows, width), lambda i, t: (0, 0)),
            pl.BlockSpec((2, width, chunk), first),
            pl.BlockSpec((2, width, chunk), second),
            pl.BlockSpec((width // 2, chunk), lambda i, t: (0, t[STEPS + i])),
            pl.BlockSpec((width // 2, chunk), lambda i, t: (0, t[STEPS + i])),
        )
        extra = [pltpu.VMEM((width, rows), BF16)]
    else:
        out_shape = (
            sds((rows, 2 * width), BF16),
            sds((2, width // 2, hidden), BF16),
            sds((2, width // 2, hidden), BF16),
            sds((hidden // 2, width), BF16),
            sds((hidden // 2, width), BF16),
        )
        out_specs = (
            pl.BlockSpec((rows, 2 * width), lambda i, t: (0, 0)),
            pl.BlockSpec((2, width // 2, chunk), lambda i, t: (0, 0, t[i])),
            pl.BlockSpec((2, width // 2, chunk), lambda i, t: (0, 0, t[i])),
            pl.BlockSpec((chunk, width), lambda i, t: (jnp.minimum(i, near), 0)),
            pl.BlockSpec((chunk, width), lambda i, t: (jnp.maximum(i - far, 0), 0)),
        )
        extra = [pltpu.VMEM((rows, width), F32), pltpu.VMEM((rows, width), F32)]
    return pl.pallas_call(
        functools.partial(ffn_kernel, shared, place.dp, place.experts),
        out_shape=out_shape,
        grid_spec=pltpu.PrefetchScalarGridSpec(
            num_scalar_prefetch=1,
            grid=(STEPS,),
            in_specs=[
                pl.BlockSpec((rows, width), lambda i, t: (0, 0)),
                pl.BlockSpec((rows, width), lambda i, t: (0, 0)),
                pl.BlockSpec((1, width, chunk), lambda i, t: (e, 0, t[i])),
                pl.BlockSpec((1, width, chunk), lambda i, t: (e, 0, STEPS + t[i])),
                pl.BlockSpec((1, chunk, width), lambda i, t: (e, t[i], 0)),
            ],
            out_specs=out_specs,
            scratch_shapes=[pltpu.VMEM((width, rows), F32), pltpu.VMEM((width, rows), BF16)]
            + extra,
        ),
        compiler_params=pltpu.CompilerParams(vmem_limit_bytes=48 * 1024 * 1024),
        cost_estimate=pl.CostEstimate(
            flops=2 * 9 * rows * width * hidden,
            bytes_accessed=12 * width * hidden,
            transcendentals=rows * hidden,
        ),
    )(table, x, dy, w_in, w_in, w_out)


def swap(a, axis, bit=1):
    size = lax.axis_size(axis)
    return lax.ppermute(a, axis, [(i, i ^ bit) for i in range(size)])


def add(a, b, kind=BF16):
    return (a.astype(F32) + b.astype(F32)).astype(kind)


def half_of(a, dim, index):
    size = a.shape[dim] // 2
    return lax.dynamic_slice_in_dim(a, index * size, size, dim)


def exchange(keep, came, dim, mine):
    return [add(half_of(keep, dim, i), half_of(came, dim, i)) for i in (mine, 1 - mine)]


def scatter(a, axis, dim):
    return lax.psum_scatter(a, axis, scatter_dimension=dim, tiled=True)


def reduce_experts(place, keep, send, dim):
    if place.lanes == 2:
        came = swap(send, "r")
        keep, send = exchange(keep, came, dim, place.low)
        came = swap(send, "g", 1)
        keep, send = exchange(keep, came, dim, place.high)
        return add(keep, swap(send, "g", 2), F32)
    came = swap(send, "g", 1)
    keep, send = exchange(keep, came, dim, place.high)
    return scatter(add(keep, swap(send, "g", 2)), "r", dim).astype(F32)


def reduce_tokens(place, keep, came, dim):
    if place.lanes == 2:
        keep, send = exchange(keep, came, dim, place.r)
        came = swap(send, "r")
    keep, send = exchange(keep, came, dim, place.low)
    came = swap(send, "g", 1)
    keep, send = exchange(keep, came, dim, place.high)
    came = swap(send, "g", 2)
    if place.lanes == 2:
        return add(keep, came, F32)
    return scatter(add(keep, came), "r", dim).astype(F32)


def reduce_shared_in(place, keep, send):
    came = swap(send, "c")
    if place.rows_y == 2:
        keep, send = [
            add(lax.dynamic_index_in_dim(keep, i, 0, False), lax.dynamic_index_in_dim(came, i, 0, False))
            for i in (place.y, 1 - place.y)
        ]
        return reduce_tokens(place, keep, swap(send, "y"), 0)
    total = add(keep, came)
    two, width, columns = total.shape
    parts = place.rows_y // 2
    total = total.reshape(two, width, parts, columns // parts).transpose(0, 2, 1, 3)
    mine = scatter(total.reshape(two * parts, width, columns // parts), "y", 0)[0]
    return reduce_tokens(place, mine, jnp.zeros_like(mine), 0)


def reduce_shared_out(place, keep, send):
    came = swap(send, "c")
    if place.rows_y == 2:
        keep, send = exchange(keep, came, 0, place.y)
        return reduce_tokens(place, keep, swap(send, "y"), 1)
    mine = scatter(add(keep, came), "y", 0)
    return reduce_tokens(place, mine, jnp.zeros_like(mine), 1)


def to_flat(place, x):
    rows, width = x.shape
    x = x.reshape(rows, 2, 2, place.lanes, width // place.dp)
    order = (0, 3, 2, 1, 4) if place.lanes == 2 else (0, 2, 1, 3, 4)
    return x.transpose(order).reshape(rows, width)


def weight_grad(place, left, right):
    rows, columns = right.shape
    own = columns // place.experts
    parts = right.reshape(rows, place.rows_y, 2, own)
    keep, send = [
        lax.dot_general(
            left,
            lax.dynamic_index_in_dim(parts, i, 2, False).reshape(rows, columns // 2),
            (((0,), (0,)), ((), ())),
            preferred_element_type=F32,
        ).astype(BF16)
        for i in (place.c, 1 - place.c)
    ]
    came = swap(send, "c")
    width = left.shape[1]
    if place.rows_y == 2:
        keep, send = [
            add(
                lax.dynamic_slice_in_dim(keep, i * own, own, 1),
                lax.dynamic_slice_in_dim(came, i * own, own, 1),
            )
            for i in (place.y, 1 - place.y)
        ]
        return reduce_tokens(place, keep, swap(send, "y"), 0)
    total = add(keep, came).reshape(width, place.rows_y, own).transpose(1, 0, 2)
    mine = scatter(total, "y", 0)[0]
    return reduce_tokens(place, mine, jnp.zeros_like(mine), 0)


def local(
    tokens,
    norm_attn,
    query_key_value_weight,
    attention_output_weight,
    norm_ffn,
    router,
    expert_in,
    expert_out,
    shared_gate_up_weight,
    shared_down_weight,
    block_lengths,
    routes,
    cotangent,
):
    place = Place()
    hidden = tokens[0].astype(F32)
    row_count, model_width = hidden.shape
    shard_index = lax.axis_index(DP)
    length = row_count * place.dp
    positions = shard_index * row_count + jnp.arange(row_count, dtype=jnp.int32)
    bounds = jnp.cumsum(block_lengths[0])
    query_ids = block_ids(bounds, positions)
    key_ids = block_ids(bounds, jnp.arange(length, dtype=jnp.int32))
    cosine, sine_table = rope_table(positions)
    head_shape = (row_count, HEADS, HEAD_DIM)
    scale_one = rms_scale(hidden)
    normalized_rows = (hidden * scale_one * norm_attn).astype(BF16)
    projected_rows = jnp.dot(
        normalized_rows, query_key_value_weight, preferred_element_type=F32
    )
    queries = (
        rotate(projected_rows[:, :model_width].reshape(head_shape), cosine, sine_table, 1.0)
        * HEAD_DIM ** (-0.5)
    ).astype(BF16)
    key_heads = rotate(
        projected_rows[:, model_width : 2 * model_width].reshape(head_shape),
        cosine,
        sine_table,
        1.0,
    ).astype(BF16)
    values = projected_rows[:, 2 * model_width :].reshape(head_shape).astype(BF16)
    all_keys, all_values = (
        lax.all_gather(key_heads.reshape(row_count, model_width), DP, axis=0, tiled=True),
        lax.all_gather(values.reshape(row_count, model_width), DP, axis=0, tiled=True),
    )
    expert_in = jnp.transpose(expert_in, (1, 0, 2))
    expert_out = jnp.transpose(expert_out, (1, 0, 2))
    key_span = min(512, length)
    blocks = length // key_span
    key_blocks = all_keys.reshape(blocks, key_span, HEADS, HEAD_DIM)
    value_blocks = all_values.reshape(blocks, key_span, HEADS, HEAD_DIM)
    id_blocks = key_ids.reshape(blocks, key_span)

    def stat_step(running, inputs):
        largest, row_total = running
        key_block, id_block = inputs
        scores, visible = masked_scores(queries, key_block, query_ids, id_block)
        newest = jnp.maximum(largest, jnp.max(scores, axis=-1))
        row_total = row_total * jnp.exp(largest - newest) + jnp.sum(
            jnp.where(visible[None], jnp.exp(scores - newest[:, :, None]), 0.0), axis=-1
        )
        return ((newest, row_total), None)

    start_max = jnp.full((HEADS, row_count), NEG, F32)
    (largest, row_total), _ = lax.scan(
        stat_step, (start_max, jnp.zeros((HEADS, row_count), F32)), (key_blocks, id_blocks)
    )
    log_total = (largest + jnp.log(row_total)).T

    def out_step(running, inputs):
        key_block, value_block, id_block = inputs
        scores, visible = masked_scores(queries, key_block, query_ids, id_block)
        weights_low = jnp.where(
            visible[None], jnp.exp(scores - log_total.T[:, :, None]), 0.0
        ).astype(BF16)
        return (
            running
            + jnp.einsum("hqk,khd->qhd", weights_low, value_block, preferred_element_type=F32),
            None,
        )

    attention_result, _ = lax.scan(
        out_step, jnp.zeros(head_shape, F32), (key_blocks, value_blocks, id_blocks)
    )
    attended_low = attention_result.reshape(row_count, model_width).astype(BF16)
    residual_between = hidden + jnp.dot(
        attended_low, attention_output_weight, preferred_element_type=F32
    )
    scale_two = rms_scale(residual_between)
    combined_input = (residual_between * scale_two * norm_ffn).astype(BF16)
    experts_total = router.shape[1]
    local_experts = expert_in.shape[0]
    groups = place.experts
    capacity = row_count * TOP * 5 // (4 * experts_total)
    router_scores = jnp.dot(combined_input, router, preferred_element_type=F32)
    chosen = routes[0]
    column = jnp.arange(experts_total, dtype=jnp.int32)
    pick_hot = (chosen[:, :, None] == column[None, None, :]).astype(F32)
    picked = jnp.sum(pick_hot * router_scores[:, None, :], axis=-1)
    gate_weights = jax.nn.softmax(picked, axis=-1)
    column_expert = column % groups * local_experts + column // groups
    flat_routes = chosen.reshape(row_count * TOP)
    route_hot = (flat_routes[:, None] == column_expert[None, :]).astype(jnp.int32)
    earlier = jnp.cumsum(route_hot, axis=0) - route_hot
    slot_index = jnp.sum(earlier * route_hot, axis=1)
    target = jnp.where(
        slot_index < capacity, jnp.sum(route_hot * column[None, :], axis=1) * capacity + slot_index, -1
    ).reshape(row_count, TOP)
    seats = jnp.arange(experts_total * capacity, dtype=jnp.int32)
    hot = [(target[:, k : k + 1] == seats[None, :]).astype(BF16) for k in range(TOP)]
    upstream = cotangent[0]
    grad_upper = upstream.astype(F32)

    def dispatch(matrix, rows):
        return lax.dot_general(
            matrix, rows, (((0,), (0,)), ((), ())), preferred_element_type=F32
        )

    def trade(rows):
        return lax.all_to_all(rows, EX, split_axis=1, concat_axis=1, tiled=True)

    seat_shape = (local_experts, groups, capacity, model_width)
    every = hot[0] + hot[1]
    send_rows = dispatch(every, combined_input).astype(BF16)
    seat_gates = jnp.sum(
        sum(
            (target[:, k : k + 1] == seats[None, :]) * gate_weights[:, k : k + 1] for k in range(TOP)
        ),
        axis=0,
    )
    grad_send = (dispatch(every, upstream) * seat_gates[:, None]).astype(BF16)
    arrived = trade(send_rows.reshape(seat_shape)).reshape(
        local_experts, groups * capacity, model_width
    )
    grad_arrived = trade(grad_send.reshape(seat_shape)).reshape(
        local_experts, groups * capacity, model_width
    )
    shared_result, grad_mixed, *shared_grads = ffn(
        True,
        place,
        place.shared_table(model_width),
        combined_input,
        upstream,
        shared_gate_up_weight[None],
        shared_down_weight[None],
        0,
    )
    table = place.expert_table(model_width)
    came_back, in_grads, out_grads = [], [], []
    for e in range(local_experts):
        both, in_keep, in_send, out_keep, out_send = ffn(
            False, place, table, arrived[e], grad_arrived[e], expert_in, expert_out, e
        )
        came_back.append(
            lax.all_to_all(
                both.reshape(groups, capacity, 2 * model_width),
                EX,
                split_axis=0,
                concat_axis=0,
                tiled=True,
            ).reshape(groups * capacity, 2 * model_width)
        )
        in_grads.append(reduce_experts(place, in_keep, in_send, 1))
        out_grads.append(reduce_experts(place, out_keep, out_send, 0))
    sum_shared_in = reduce_shared_in(place, *shared_grads[:2])
    sum_shared_out = reduce_shared_out(place, *shared_grads[2:])
    returned = jnp.concatenate(came_back, axis=0)
    back_rows = [
        jnp.dot(h, returned[:, :model_width], preferred_element_type=F32) for h in hot
    ]
    routed = sum(gate_weights[:, k : k + 1] * back_rows[k] for k in range(TOP))
    output = (residual_between + routed + shared_result).astype(BF16)[None]
    grad_gates = jnp.stack([jnp.sum(b * grad_upper, axis=-1) for b in back_rows], axis=1)
    grad_picked = gate_weights * (
        grad_gates - jnp.sum(gate_weights * grad_gates, axis=-1, keepdims=True)
    )
    grad_logits = jnp.sum(pick_hot * grad_picked[:, :, None], axis=1).astype(BF16)
    grad_router = jnp.einsum("td,te->de", combined_input, grad_logits, preferred_element_type=F32)
    grad_mixed = (
        grad_mixed
        + jnp.einsum("te,de->td", grad_logits, router, preferred_element_type=F32)
        + jnp.dot(every, returned[:, model_width:], preferred_element_type=F32)
    )
    grad_norm_ffn = jnp.sum(grad_mixed * residual_between * scale_two, axis=0)
    grad_middle = grad_upper + rms_back(residual_between, scale_two, norm_ffn, grad_mixed)
    grad_attn_low = grad_middle.astype(BF16)
    grad_attended = (
        jnp.einsum(
            "te,de->td", grad_attn_low, attention_output_weight, preferred_element_type=F32
        )
        .astype(BF16)
        .reshape(head_shape)
    )
    row_delta = jnp.sum(grad_attended.astype(F32) * attention_result, axis=-1)

    def back_step(grad_queries, inputs):
        key_block, value_block, id_block = inputs
        weights_low, grad_scores = score_grads(
            queries,
            grad_attended,
            log_total,
            row_delta,
            key_block,
            value_block,
            query_ids,
            id_block,
        )
        grad_queries = grad_queries + jnp.einsum(
            "hqk,khd->qhd", grad_scores, key_block, preferred_element_type=F32
        )
        grad_key_part = jnp.einsum(
            "hqk,qhd->khd", grad_scores, queries, preferred_element_type=F32
        ).reshape(key_span, model_width)
        grad_value_part = jnp.einsum(
            "hqk,qhd->khd", weights_low, grad_attended, preferred_element_type=F32
        ).reshape(key_span, model_width)
        return (grad_queries, jnp.concatenate([grad_key_part, grad_value_part], axis=1))

    grad_queries, key_terms = lax.scan(
        back_step, jnp.zeros(head_shape, F32), (key_blocks, value_blocks, id_blocks)
    )
    own_terms = lax.psum_scatter(
        key_terms.reshape(length, 2 * model_width).astype(BF16),
        DP,
        scatter_dimension=0,
        tiled=True,
    ).astype(F32)
    grad_keys = own_terms[:, :model_width].reshape(head_shape)
    grad_values = own_terms[:, model_width:].reshape(head_shape)
    grad_queries = rotate(grad_queries * HEAD_DIM ** (-0.5), cosine, sine_table, -1.0)
    grad_keys = rotate(grad_keys, cosine, sine_table, -1.0)
    grad_projected = jnp.concatenate(
        [
            grad_queries.reshape(row_count, model_width),
            grad_keys.reshape(row_count, model_width),
            grad_values.reshape(row_count, model_width),
        ],
        axis=1,
    ).astype(BF16)
    grad_normed = jnp.einsum(
        "te,de->td", grad_projected, query_key_value_weight, preferred_element_type=F32
    )
    grad_norm_attn = jnp.sum(grad_normed * hidden * scale_one, axis=0)
    grad_input = grad_middle + rms_back(hidden, scale_one, norm_attn, grad_normed)
    sum_qkv = weight_grad(place, to_flat(place, normalized_rows), grad_projected)
    sum_out = weight_grad(place, to_flat(place, attended_low), grad_attn_low)
    small = jnp.concatenate([grad_norm_ffn[:, None], grad_router], axis=1)
    small = lax.psum(small, DP + EX)
    own = model_width // place.dp
    small = lax.dynamic_slice_in_dim(small, shard_index * own, own, 0)
    sum_router = lax.dynamic_slice_in_dim(
        small[:, 1:], lax.axis_index(EX) * local_experts, local_experts, 1
    )
    sum_norm_attn = lax.dynamic_slice_in_dim(
        lax.psum(grad_norm_attn, DP + EX), shard_index * own, own, 0
    )
    part_in = jnp.stack([g.transpose(1, 0, 2).reshape(own, -1) for g in in_grads], axis=1)
    part_out = jnp.stack(out_grads, axis=1)
    return (
        output,
        grad_input[None],
        sum_norm_attn,
        sum_qkv,
        sum_out,
        small[:, 0],
        sum_router,
        part_in,
        part_out,
        sum_shared_in,
        sum_shared_out.T,
    )


def solution(mesh):
    dp, experts = mesh.shape["dp"], mesh.shape["expert"]
    finer = Mesh(mesh.devices.reshape(4, dp // 4, experts // 2, 2), ("g", "r", "y", "c"))
    whole = P()
    return jax.shard_map(
        local,
        mesh=finer,
        in_specs=(
            P(EX, DP, None),
            whole,
            whole,
            whole,
            whole,
            whole,
            P(None, EX, None),
            P(None, EX, None),
            whole,
            whole,
            P(EX, None),
            P(EX, DP, None),
            P(EX, DP, None),
        ),
        out_specs=(
            P(EX, DP, None),
            P(EX, DP, None),
            P(DP),
            P(DP, EX),
            P(DP, EX),
            P(DP),
            P(DP, EX),
            P(DP, EX, None),
            P(DP, EX, None),
            P(DP, EX),
            P(DP, EX),
        ),
        check_vma=False,
    )
```

```python
import functools

import jax
import jax.numpy as jnp
from jax import lax
from jax.experimental import pallas as pl
from jax.experimental.pallas import tpu as pltpu
from jax.sharding import Mesh
from jax.sharding import PartitionSpec as P

HEADS = 12
HEAD_DIM = 64
TOP = 2
EPS = 1e-06
NEG = -1e30
F32 = jnp.float32
BF16 = jnp.bfloat16
STEPS = 8
DP = ("g", "r")
EX = ("y", "c")


def rope_table(positions):
    lane = jnp.arange(2 * HEAD_DIM, dtype=jnp.int32) % HEAD_DIM
    half_dim = HEAD_DIM // 2
    frequency = 10000.0 ** (-(lane % half_dim).astype(F32) * 2.0 / HEAD_DIM)
    angles = positions.astype(F32)[:, None] * frequency[None, :]
    return jnp.cos(angles), jnp.sin(angles) * jnp.where(lane < half_dim, -1.0, 1.0)


def rms_scale(hidden):
    return lax.rsqrt(jnp.mean(hidden * hidden, axis=-1, keepdims=True) + EPS)


def rms_back(hidden, scale_rows, gain_vector, upstream):
    normed_grad = upstream * gain_vector
    inner_mean = jnp.mean(normed_grad * hidden, axis=-1, keepdims=True)
    return scale_rows * normed_grad - hidden * scale_rows**3 * inner_mean


class Place:
    def __init__(self):
        self.groups, self.lanes = lax.axis_size("g"), lax.axis_size("r")
        self.rows_y = lax.axis_size("y")
        self.dp = self.groups * self.lanes
        self.experts = self.rows_y * 2
        self.g, self.r = lax.axis_index("g"), lax.axis_index("r")
        self.y, self.c = lax.axis_index("y"), lax.axis_index("c")
        self.low, self.high = self.g % 2, self.g // 2

    def own(self, b):
        g, r = b // self.lanes, b % self.lanes
        low, high = g % 2, g // 2
        if self.lanes == 2:
            return r ^ self.r, low * 2 + high
        return low ^ self.low, high * self.lanes + r

    def flat(self, b):
        g, r = b // self.lanes, b % self.lanes
        if self.lanes == 2:
            return r * 4 + (g % 2) * 2 + g // 2
        return (g % 2 * 2 + g // 2) * self.lanes + r

    def expert_table(self, width):
        sub = STEPS // 4
        order = []
        for pos in range(STEPS):
            half, rest = pos // 4, pos % 4
            if self.lanes == 2:
                low, high, part = rest // 2, rest % 2, half ^ self.r
            else:
                low, high, part = half ^ self.low, rest // 2, rest % 2
            order.append((high * 2 + low) * sub + part)
        block = width // self.dp
        rows = []
        for b in range(self.dp):
            half, rest = self.own(b)
            rows.append(half * (width // 2) + rest * block)
        return jnp.stack([jnp.asarray(v, jnp.int32) for v in order + [0] * STEPS + rows])

    def shared_table(self, width):
        per = 16 // self.experts
        order, columns = [], []
        sub = STEPS // 4
        for pos in range(STEPS):
            half, rest = pos // 4, pos % 4
            j = (rest // per * 2 + (half ^ self.c)) * per + rest % per
            order.append(j)
            g, part = j // sub, j % sub
            if self.lanes == 2:
                columns.append(part * 4 + g % 2 * 2 + g // 2)
            else:
                columns.append((g % 2 * 2 + g // 2) * sub + part)
        block = width // self.dp
        rows = [self.flat(b) * block for b in range(self.dp)]
        own = width // self.experts
        turned = [
            (e % 2 ^ self.c) * (width // 2) + e // 2 * own for e in range(self.experts)
        ]
        return jnp.stack(
            [jnp.asarray(v, jnp.int32) for v in order + columns + rows + turned]
        )


def nt(a, b):
    return lax.dot_general(a, b, (((1,), (1,)), ((), ())), preferred_element_type=F32)


def nn(a, b):
    return lax.dot_general(a, b, (((1,), (0,)), ((), ())), preferred_element_type=F32)


def turn(x, cosine, sine):
    width = x.shape[1]
    lane = lax.broadcasted_iota(jnp.int32, x.shape, 1) % HEAD_DIM
    other = jnp.where(
        lane < HEAD_DIM // 2,
        pltpu.roll(x, width - HEAD_DIM // 2, 1),
        pltpu.roll(x, HEAD_DIM // 2, 1),
    )
    times = width // cosine.shape[1]
    cosine = jnp.concatenate([cosine] * times, axis=1)
    sine = jnp.concatenate([sine] * times, axis=1)
    return x * cosine + other * sine


def project_kernel(x_ref, gain_ref, w_ref, cos_ref, sin_ref, normed_ref, q_ref, kv_ref):
    step = pl.program_id(0)
    groups = q_ref.shape[0]
    rows, width = x_ref.shape
    half, three = rows // 2, 3 * HEAD_DIM

    @pl.when(step == 0)
    def _():
        x = x_ref[...].astype(F32)
        normed_ref[...] = (x * rms_scale(x) * gain_ref[...]).astype(BF16)

    part = nn(normed_ref[...], w_ref[...])

    @pl.when(step == 0)
    def _():
        q = (turn(part, cos_ref[...], sin_ref[...]) * HEAD_DIM**-0.5).astype(F32)
        for g in range(groups):
            own = q[:, g * three : (g + 1) * three].astype(BF16)
            q_ref[g, :, 0:128] = own[:half, :128]
            q_ref[g, :, 128:256] = own[half:, :128]
            q_ref[g, :, 256:320] = own[:half, 128:]
            q_ref[g, :, 320:384] = own[half:, 128:]

    @pl.when(step == 1)
    def _():
        k = turn(part, cos_ref[...], sin_ref[...])
        for g in range(groups):
            own = k[:, g * three : (g + 1) * three].astype(BF16)
            kv_ref[g, :, 0:128] = own[:, :128]
            kv_ref[g, :, 256:320] = own[:, 128:]

    @pl.when(step == 2)
    def _():
        for g in range(groups):
            own = part[:, g * three : (g + 1) * three].astype(BF16)
            kv_ref[g, :, 128:256] = own[:, :128]
            kv_ref[g, :, 320:384] = own[:, 128:]


def project(place, x, gain, weight, cosine, sine):
    rows, width = x.shape
    whole = lambda *shape: pl.BlockSpec(shape, lambda i: (0,) * len(shape))
    return pl.pallas_call(
        project_kernel,
        grid=(3,),
        out_shape=(
            jax.ShapeDtypeStruct((rows, width), BF16),
            jax.ShapeDtypeStruct((place.groups, rows // 2, 384), BF16),
            jax.ShapeDtypeStruct((place.groups, rows, 384), BF16),
        ),
        in_specs=[
            whole(rows, width),
            whole(1, width),
            pl.BlockSpec((width, width), lambda i: (0, i)),
            whole(rows, 128),
            whole(rows, 128),
        ],
        out_specs=(
            whole(rows, width),
            whole(place.groups, rows // 2, 384),
            whole(place.groups, rows, 384),
        ),
        compiler_params=pltpu.CompilerParams(vmem_limit_bytes=32 * 1024 * 1024),
        cost_estimate=pl.CostEstimate(
            flops=6 * rows * width * width, bytes_accessed=10 * width * width, transcendentals=0
        ),
    )(x, gain[None], weight, cosine, sine)


def unpack(packed, second_low):
    half = packed.shape[0]
    x = packed.astype(F32)
    lane = lax.broadcasted_iota(jnp.int32, (half, 128), 1)
    low = lane < HEAD_DIM
    first, second, third = x[:, 0:128], x[:, 128:256], x[:, 256:384]
    turned = pltpu.roll(third, HEAD_DIM, 1)
    zero = jnp.zeros_like(third)
    pair = [
        jnp.where(low, first, zero),
        jnp.where(low, second, zero),
        jnp.where(low, zero, first),
        jnp.where(low, zero, second),
    ]
    if second_low:
        single = [jnp.where(low, third, zero), jnp.where(low, turned, zero)]
    else:
        single = [jnp.where(low, zero, turned), jnp.where(low, zero, third)]
    return (
        jnp.concatenate(pair, axis=0).astype(BF16),
        jnp.concatenate(single, axis=0).astype(BF16),
    )


def visible_keys(kz, source, lanes, rows, limit):
    first = (kz * lanes + source) * rows
    place = first + lax.broadcasted_iota(jnp.int32, (rows, limit.shape[1]), 0)
    return place < limit


def attend_kernel(sources, lanes, info, limit_ref, q_ref, *refs):
    kv_refs, (out_ref, lse_ref, turned) = refs[:sources], refs[sources:]
    shards, half, _ = q_ref.shape
    rows = 2 * half
    for s in range(sources):
        for z in range(shards):
            turned[s, z] = kv_refs[s][z].astype(F32).T.astype(BF16)

    def shard(z, carry):
        pair, single = unpack(q_ref[z], True)
        limit = limit_ref[z]

        def step(kz, state):
            largest, total, acc_pair, acc_single = state
            scores = []
            for s in range(sources):
                keep = visible_keys(kz, info[shards + s], lanes, rows, limit)
                kv = kv_refs[s]
                two = nt(kv[kz, :, 0:128], pair)
                one = nt(kv[kz, :, 256:384], single)
                both = jnp.concatenate([two, one], axis=1)
                keep = jnp.concatenate([keep] * 3, axis=1)
                scores.append(jnp.where(keep, both, NEG))
            newest = largest
            for sc in scores:
                newest = jnp.maximum(newest, jnp.max(sc, axis=0, keepdims=True))
            fade = jnp.exp(largest - newest)
            total = total * fade
            acc_pair = acc_pair * fade[:, : 2 * rows]
            acc_single = acc_single * fade[:, 2 * rows :]
            for s, sc in enumerate(scores):
                power = jnp.exp(sc - newest)
                total = total + jnp.sum(power, axis=0, keepdims=True)
                power = power.astype(BF16)
                acc_pair = acc_pair + nn(turned[s, kz, 128:256, :], power[:, : 2 * rows])
                acc_single = acc_single + nn(turned[s, kz, 256:384, :], power[:, 2 * rows :])
            return newest, total, acc_pair, acc_single

        largest, total, acc_pair, acc_single = lax.fori_loop(
            0,
            info[z],
            step,
            (
                jnp.full((1, 3 * rows), NEG, F32),
                jnp.zeros((1, 3 * rows), F32),
                jnp.zeros((128, 2 * rows), F32),
                jnp.zeros((128, rows), F32),
            ),
        )
        lse_ref[z] = largest + jnp.log(total)
        share = 1.0 / total
        first = acc_pair[:HEAD_DIM, :rows] * share[:, :rows]
        second = acc_pair[HEAD_DIM:, rows:] * share[:, rows : 2 * rows]
        third = acc_single[HEAD_DIM:] * share[:, 2 * rows :]
        packed = jnp.concatenate(
            [a[:, part] for part in (slice(0, half), slice(half, rows)) for a in (first, second)]
            + [third[:, :half], third[:, half:]],
            axis=0,
        )
        out_ref[z] = packed.T.astype(BF16)
        return carry

    lax.fori_loop(0, shards, shard, 0)


def attend(place, info, limit, q, kvs):
    shards, half, lanes = q.shape
    vmem = pl.BlockSpec(memory_space=pltpu.VMEM)
    sources = len(kvs)
    work = 2 * 4 * 3 * 2 * half * sources * shards * 2 * half * 128
    return pl.pallas_call(
        functools.partial(attend_kernel, sources, place.lanes),
        out_shape=(
            jax.ShapeDtypeStruct(q.shape, BF16),
            jax.ShapeDtypeStruct((shards, 1, 6 * half), F32),
        ),
        in_specs=[pl.BlockSpec(memory_space=pltpu.SMEM)] + [vmem] * (2 + sources),
        out_specs=(vmem, vmem),
        scratch_shapes=[pltpu.VMEM((sources, shards, lanes, 2 * half), BF16)],
        compiler_params=pltpu.CompilerParams(vmem_limit_bytes=40 * 1024 * 1024),
        cost_estimate=pl.CostEstimate(flops=work, bytes_accessed=4 * 2**20, transcendentals=6 * 2**20),
    )(info, limit, q, *kvs)


def attend_back_kernel(sources, lanes, info, limit_ref, lse_ref, q_ref, out_ref, grad_ref, *refs):
    kv_refs = refs[:sources]
    dq_ref, dkv_refs, (turned, total) = refs[sources], refs[sources + 1 : -2], refs[-2:]
    shards, half, _ = q_ref.shape
    rows = 2 * half
    for s in range(sources):
        for z in range(shards):
            turned[s, z] = kv_refs[s][z].astype(F32).T.astype(BF16)
    total[...] = jnp.zeros_like(total)

    def shard(z, carry):
        pair, single = unpack(q_ref[z], True)
        grad_pair, grad_single = unpack(grad_ref[z], False)
        limit, lse = limit_ref[z], lse_ref[z]
        product = (grad_ref[z].astype(F32) * out_ref[z].astype(F32)).T
        sums = [
            jnp.sum(product[i * HEAD_DIM : (i + 1) * HEAD_DIM], axis=0, keepdims=True)
            for i in range(6)
        ]
        delta = jnp.concatenate([sums[0], sums[2], sums[1], sums[3], sums[4], sums[5]], axis=1)

        def step(kz, state):
            dq_pair, dq_single = state
            for s in range(sources):
                keep = visible_keys(kz, info[shards + s], lanes, rows, limit)
                keep = jnp.concatenate([keep] * 3, axis=1)
                kv = kv_refs[s]
                k01, v01, kv2 = kv[kz, :, 0:128], kv[kz, :, 128:256], kv[kz, :, 256:384]
                scores = jnp.concatenate([nt(k01, pair), nt(kv2, single)], axis=1)
                grads = jnp.concatenate([nt(v01, grad_pair), nt(kv2, grad_single)], axis=1)
                power = jnp.where(keep, jnp.exp(scores - lse), 0.0)
                slope = (power * (grads - delta)).astype(BF16)
                power = power.astype(BF16)
                dq_pair = dq_pair + nn(turned[s, kz, 0:128, :], slope[:, : 2 * rows])
                dq_single = dq_single + nn(turned[s, kz, 256:384, :], slope[:, 2 * rows :])
                total[s, kz, :, 0:128] += nn(slope[:, : 2 * rows], pair)
                total[s, kz, :, 128:256] += nn(power[:, : 2 * rows], grad_pair)
                total[s, kz, :, 256:384] += nn(slope[:, 2 * rows :], single) + nn(
                    power[:, 2 * rows :], grad_single
                )
            return dq_pair, dq_single

        dq_pair, dq_single = lax.fori_loop(
            0,
            info[z],
            step,
            (jnp.zeros((128, 2 * rows), F32), jnp.zeros((128, rows), F32)),
        )
        first, second = dq_pair[:HEAD_DIM, :rows], dq_pair[HEAD_DIM:, rows:]
        third = dq_single[:HEAD_DIM]
        packed = jnp.concatenate(
            [a[:, part] for part in (slice(0, half), slice(half, rows)) for a in (first, second)]
            + [third[:, :half], third[:, half:]],
            axis=0,
        )
        dq_ref[z] = packed.T.astype(BF16)
        return carry

    lax.fori_loop(0, shards, shard, 0)
    for s in range(sources):
        dkv_refs[s][...] = total[s].astype(BF16)


def attend_back(place, info, limit, lse, q, out, grad, kvs):
    shards, half, lanes = q.shape
    vmem = pl.BlockSpec(memory_space=pltpu.VMEM)
    sources = len(kvs)
    work = 2 * 8 * 3 * 2 * half * sources * shards * 2 * half * 128
    return pl.pallas_call(
        functools.partial(attend_back_kernel, sources, place.lanes),
        out_shape=(jax.ShapeDtypeStruct(q.shape, BF16),)
        + (jax.ShapeDtypeStruct(kvs[0].shape, BF16),) * sources,
        in_specs=[pl.BlockSpec(memory_space=pltpu.SMEM)] + [vmem] * (5 + sources),
        out_specs=(vmem,) * (1 + sources),
        scratch_shapes=[
            pltpu.VMEM((sources, shards, lanes, 2 * half), BF16),
            pltpu.VMEM((sources, shards, 2 * half, lanes), F32),
        ],
        compiler_params=pltpu.CompilerParams(vmem_limit_bytes=52 * 1024 * 1024),
        cost_estimate=pl.CostEstimate(flops=work, bytes_accessed=6 * 2**20, transcendentals=6 * 2**20),
    )(info, limit, lse, q, out, grad, *kvs)


def finish_kernel(
    dq_ref, dkv_ref, w_ref, cos_ref, sin_ref, x_ref, gain_ref, middle_ref,
    projected_ref, input_ref, norm_ref, gather,
):
    groups, half, _ = dq_ref.shape
    rows, width = x_ref.shape
    three = 3 * HEAD_DIM
    for g in range(groups):
        at = g * three
        dq, dkv = dq_ref[g].astype(F32), dkv_ref[g].astype(F32)
        gather[0, :half, at : at + 128] = dq[:, 0:128]
        gather[0, half:, at : at + 128] = dq[:, 128:256]
        gather[0, :half, at + 128 : at + three] = dq[:, 256:320]
        gather[0, half:, at + 128 : at + three] = dq[:, 320:384]
        gather[1, :, at : at + 128] = dkv[:, 0:128]
        gather[1, :, at + 128 : at + three] = dkv[:, 256:320]
        gather[2, :, at : at + 128] = dkv[:, 128:256]
        gather[2, :, at + 128 : at + three] = dkv[:, 320:384]
    cosine, sine = cos_ref[...], -sin_ref[...]
    parts = [
        (turn(gather[0], cosine, sine) * HEAD_DIM**-0.5).astype(BF16),
        turn(gather[1], cosine, sine).astype(BF16),
        gather[2].astype(BF16),
    ]
    grad = jnp.zeros((rows, width), F32)
    for i, part in enumerate(parts):
        projected_ref[:, i * width : (i + 1) * width] = part
        grad = grad + nt(part, w_ref[:, i * width : (i + 1) * width])
    x = x_ref[...].astype(F32)
    scale = rms_scale(x)
    norm_ref[...] = jnp.sum(grad * x * scale, axis=0, keepdims=True)
    input_ref[...] = middle_ref[...] + rms_back(x, scale, gain_ref[...], grad)


def finish(dq, dkv, weight, cosine, sine, x, gain, middle):
    rows, width = x.shape
    vmem = pl.BlockSpec(memory_space=pltpu.VMEM)
    return pl.pallas_call(
        finish_kernel,
        out_shape=(
            jax.ShapeDtypeStruct((rows, 3 * width), BF16),
            jax.ShapeDtypeStruct((rows, width), F32),
            jax.ShapeDtypeStruct((1, width), F32),
        ),
        in_specs=[vmem] * 8,
        out_specs=(vmem,) * 3,
        scratch_shapes=[pltpu.VMEM((3, rows, width), F32)],
        compiler_params=pltpu.CompilerParams(vmem_limit_bytes=40 * 1024 * 1024),
        cost_estimate=pl.CostEstimate(
            flops=6 * rows * width * width, bytes_accessed=10 * width * width, transcendentals=0
        ),
    )(dq, dkv, weight, cosine, sine, x, gain[None], middle)


def heads_to_rows(packed):
    groups, half, _ = packed.shape
    pair = jnp.concatenate([packed[:, :, 0:128], packed[:, :, 128:256]], axis=1)
    single = jnp.concatenate([packed[:, :, 256:320], packed[:, :, 320:384]], axis=1)
    joined = jnp.concatenate([pair, single], axis=2)
    return joined.transpose(1, 0, 2).reshape(2 * half, groups * 3 * HEAD_DIM)


def rows_to_heads(rows, groups):
    count = rows.shape[0]
    half = count // 2
    split = rows.reshape(count, groups, 3 * HEAD_DIM).transpose(1, 0, 2)
    return jnp.concatenate(
        [split[:, :half, :128], split[:, half:, :128], split[:, :half, 128:], split[:, half:, 128:]],
        axis=2,
    )


def trade_heads(a):
    return lax.all_to_all(a, "g", split_axis=0, concat_axis=0, tiled=True)


def ffn_kernel(shared, dp, experts, table, x_ref, dy_ref, gate_ref, up_ref, down_ref, *refs):
    if shared:
        result, back, in_keep, in_send, out_keep, out_send, stage, turned, turned_dy = refs
    else:
        both, in_keep, in_send, out_keep, out_send, stage, turned, result, back = refs
    step = pl.program_id(0)
    width = x_ref.shape[1]
    rows = x_ref.shape[0]

    @pl.when(step == 0)
    def _():
        whole = x_ref[...].astype(F32).T
        block = width // dp
        for b in range(dp):
            start = pl.multiple_of(table[2 * STEPS + b], 8)
            stage[pl.ds(start, block), :] = whole[b * block : (b + 1) * block]
        turned[...] = stage[...].astype(BF16)
        if shared:
            whole = dy_ref[...].astype(F32).T
            block = width // experts
            for e in range(experts):
                start = pl.multiple_of(table[2 * STEPS + dp + e], 8)
                stage[pl.ds(start, block), :] = whole[e * block : (e + 1) * block]
            turned_dy[...] = stage[...].astype(BF16)
        result[...] = jnp.zeros_like(result)
        back[...] = jnp.zeros_like(back)

    x, dy = x_ref[...], dy_ref[...]
    w_gate, w_up, w_down = gate_ref[0], up_ref[0], down_ref[0]
    gate, up = nn(x, w_gate), nn(x, w_up)
    grad = nt(dy, w_down)
    sig = jax.nn.sigmoid(gate)
    silu = gate * sig
    act = (silu * up).astype(BF16)
    grad_gate = (grad * up * (sig * (1.0 + gate * (1.0 - sig)))).astype(BF16)
    grad_up = (grad * silu).astype(BF16)
    result[...] += nn(act, w_down)
    back[...] += nt(grad_gate, w_gate) + nt(grad_up, w_up)
    xt = turned[...]
    half = width // 2
    for k, upper in enumerate((grad_gate, grad_up)):
        grad_in = nn(xt, upper).astype(BF16)
        if shared:

            @pl.when(step < STEPS // 2)
            def _():
                in_keep[k] = grad_in

            @pl.when(step >= STEPS // 2)
            def _():
                in_send[k] = grad_in

        else:
            in_keep[k] = grad_in[:half]
            in_send[k] = grad_in[half:]
    if shared:
        grad_out = nn(turned_dy[...], act).astype(BF16)
        out_keep[...] = grad_out[:half]
        out_send[...] = grad_out[half:]
    else:
        grad_out = lax.dot_general(
            act, dy, (((0,), (0,)), ((), ())), preferred_element_type=F32
        ).astype(BF16)

        @pl.when(step < STEPS // 2)
        def _():
            out_keep[...] = grad_out

        @pl.when(step >= STEPS // 2)
        def _():
            out_send[...] = grad_out

        @pl.when(step == STEPS - 1)
        def _():
            both[:, :width] = result[...].astype(BF16)
            both[:, width:] = back[...].astype(BF16)


def ffn(shared, place, table, x, dy, w_in, w_out, e):
    rows, width = x.shape
    hidden = w_out.shape[1]
    chunk = hidden // STEPS
    near, far = STEPS // 2 - 1, STEPS // 2
    sds = jax.ShapeDtypeStruct
    first = lambda i, t: (0, 0, jnp.minimum(i, near))
    second = lambda i, t: (0, 0, jnp.maximum(i - far, 0))
    if shared:
        out_shape = (
            sds((rows, width), F32),
            sds((rows, width), F32),
            sds((2, width, hidden // 2), BF16),
            sds((2, width, hidden // 2), BF16),
            sds((width // 2, hidden), BF16),
            sds((width // 2, hidden), BF16),
        )
        out_specs = (
            pl.BlockSpec((rows, width), lambda i, t: (0, 0)),
            pl.BlockSpec((rows, width), lambda i, t: (0, 0)),
            pl.BlockSpec((2, width, chunk), first),
            pl.BlockSpec((2, width, chunk), second),
            pl.BlockSpec((width // 2, chunk), lambda i, t: (0, t[STEPS + i])),
            pl.BlockSpec((width // 2, chunk), lambda i, t: (0, t[STEPS + i])),
        )
        extra = [pltpu.VMEM((width, rows), BF16)]
    else:
        out_shape = (
            sds((rows, 2 * width), BF16),
            sds((2, width // 2, hidden), BF16),
            sds((2, width // 2, hidden), BF16),
            sds((hidden // 2, width), BF16),
            sds((hidden // 2, width), BF16),
        )
        out_specs = (
            pl.BlockSpec((rows, 2 * width), lambda i, t: (0, 0)),
            pl.BlockSpec((2, width // 2, chunk), lambda i, t: (0, 0, t[i])),
            pl.BlockSpec((2, width // 2, chunk), lambda i, t: (0, 0, t[i])),
            pl.BlockSpec((chunk, width), lambda i, t: (jnp.minimum(i, near), 0)),
            pl.BlockSpec((chunk, width), lambda i, t: (jnp.maximum(i - far, 0), 0)),
        )
        extra = [pltpu.VMEM((rows, width), F32), pltpu.VMEM((rows, width), F32)]
    return pl.pallas_call(
        functools.partial(ffn_kernel, shared, place.dp, place.experts),
        out_shape=out_shape,
        grid_spec=pltpu.PrefetchScalarGridSpec(
            num_scalar_prefetch=1,
            grid=(STEPS,),
            in_specs=[
                pl.BlockSpec((rows, width), lambda i, t: (0, 0)),
                pl.BlockSpec((rows, width), lambda i, t: (0, 0)),
                pl.BlockSpec((1, width, chunk), lambda i, t: (e, 0, t[i])),
                pl.BlockSpec((1, width, chunk), lambda i, t: (e, 0, STEPS + t[i])),
                pl.BlockSpec((1, chunk, width), lambda i, t: (e, t[i], 0)),
            ],
            out_specs=out_specs,
            scratch_shapes=[pltpu.VMEM((width, rows), F32), pltpu.VMEM((width, rows), BF16)]
            + extra,
        ),
        compiler_params=pltpu.CompilerParams(vmem_limit_bytes=48 * 1024 * 1024),
        cost_estimate=pl.CostEstimate(
            flops=2 * 9 * rows * width * hidden,
            bytes_accessed=12 * width * hidden,
            transcendentals=rows * hidden,
        ),
    )(table, x, dy, w_in, w_in, w_out)


def swap(a, axis, bit=1):
    size = lax.axis_size(axis)
    return lax.ppermute(a, axis, [(i, i ^ bit) for i in range(size)])


def add(a, b, kind=BF16):
    return (a.astype(F32) + b.astype(F32)).astype(kind)


def half_of(a, dim, index):
    size = a.shape[dim] // 2
    return lax.dynamic_slice_in_dim(a, index * size, size, dim)


def exchange(keep, came, dim, mine):
    return [add(half_of(keep, dim, i), half_of(came, dim, i)) for i in (mine, 1 - mine)]


def scatter(a, axis, dim):
    return lax.psum_scatter(a, axis, scatter_dimension=dim, tiled=True)


def reduce_experts(place, keep, send, dim):
    if place.lanes == 2:
        came = swap(send, "r")
        keep, send = exchange(keep, came, dim, place.low)
        came = swap(send, "g", 1)
        keep, send = exchange(keep, came, dim, place.high)
        return add(keep, swap(send, "g", 2), F32)
    came = swap(send, "g", 1)
    keep, send = exchange(keep, came, dim, place.high)
    return scatter(add(keep, swap(send, "g", 2)), "r", dim).astype(F32)


def reduce_tokens(place, keep, came, dim):
    if place.lanes == 2:
        keep, send = exchange(keep, came, dim, place.r)
        came = swap(send, "r")
    keep, send = exchange(keep, came, dim, place.low)
    came = swap(send, "g", 1)
    keep, send = exchange(keep, came, dim, place.high)
    came = swap(send, "g", 2)
    if place.lanes == 2:
        return add(keep, came, F32)
    return scatter(add(keep, came), "r", dim).astype(F32)


def reduce_shared_in(place, keep, send):
    came = swap(send, "c")
    if place.rows_y == 2:
        keep, send = [
            add(lax.dynamic_index_in_dim(keep, i, 0, False), lax.dynamic_index_in_dim(came, i, 0, False))
            for i in (place.y, 1 - place.y)
        ]
        return reduce_tokens(place, keep, swap(send, "y"), 0)
    total = add(keep, came)
    two, width, columns = total.shape
    parts = place.rows_y // 2
    total = total.reshape(two, width, parts, columns // parts).transpose(0, 2, 1, 3)
    mine = scatter(total.reshape(two * parts, width, columns // parts), "y", 0)[0]
    return reduce_tokens(place, mine, jnp.zeros_like(mine), 0)


def reduce_shared_out(place, keep, send):
    came = swap(send, "c")
    if place.rows_y == 2:
        keep, send = exchange(keep, came, 0, place.y)
        return reduce_tokens(place, keep, swap(send, "y"), 1)
    mine = scatter(add(keep, came), "y", 0)
    return reduce_tokens(place, mine, jnp.zeros_like(mine), 1)


def to_flat(place, x):
    rows, width = x.shape
    x = x.reshape(rows, 2, 2, place.lanes, width // place.dp)
    order = (0, 3, 2, 1, 4) if place.lanes == 2 else (0, 2, 1, 3, 4)
    return x.transpose(order).reshape(rows, width)


def weight_grad(place, left, right):
    rows, columns = right.shape
    own = columns // place.experts
    parts = right.reshape(rows, place.rows_y, 2, own)
    keep, send = [
        lax.dot_general(
            left,
            lax.dynamic_index_in_dim(parts, i, 2, False).reshape(rows, columns // 2),
            (((0,), (0,)), ((), ())),
            preferred_element_type=F32,
        ).astype(BF16)
        for i in (place.c, 1 - place.c)
    ]
    came = swap(send, "c")
    width = left.shape[1]
    if place.rows_y == 2:
        keep, send = [
            add(
                lax.dynamic_slice_in_dim(keep, i * own, own, 1),
                lax.dynamic_slice_in_dim(came, i * own, own, 1),
            )
            for i in (place.y, 1 - place.y)
        ]
        return reduce_tokens(place, keep, swap(send, "y"), 0)
    total = add(keep, came).reshape(width, place.rows_y, own).transpose(1, 0, 2)
    mine = scatter(total, "y", 0)[0]
    return reduce_tokens(place, mine, jnp.zeros_like(mine), 0)


def local(
    tokens,
    norm_attn,
    query_key_value_weight,
    attention_output_weight,
    norm_ffn,
    router,
    expert_in,
    expert_out,
    shared_gate_up_weight,
    shared_down_weight,
    block_lengths,
    routes,
    cotangent,
):
    place = Place()
    hidden = tokens[0].astype(F32)
    row_count, model_width = hidden.shape
    shard_index = lax.axis_index(DP)
    length = row_count * place.dp
    positions = shard_index * row_count + jnp.arange(row_count, dtype=jnp.int32)
    bounds = jnp.cumsum(block_lengths[0])
    cosine, sine = rope_table(positions)
    normalized_rows, own_q, own_kv = project(
        place, tokens[0], norm_attn, query_key_value_weight, cosine, sine
    )
    kv = trade_heads(own_kv)
    q = trade_heads(own_q)
    if place.lanes == 2:
        kvs = [kv, swap(kv, "r")]
        lanes_of = [place.r, 1 - place.r]
    else:
        every_kv = lax.all_gather(kv, "r", axis=0, tiled=False)
        kvs = [every_kv[i] for i in range(place.lanes)]
        lanes_of = [jnp.int32(i) for i in range(place.lanes)]
    starts = (jnp.arange(place.groups, dtype=jnp.int32) * place.lanes + place.r) * row_count
    query_places = starts[:, None] + jnp.arange(row_count, dtype=jnp.int32)[None, :]
    limit = jnp.min(
        jnp.where(bounds[None, None, :] > query_places[:, :, None], bounds, length), axis=-1
    )
    span = row_count * place.lanes
    info = jnp.concatenate([(jnp.max(limit, axis=1) + span - 1) // span, jnp.stack(lanes_of)])
    info = info.astype(jnp.int32)
    limit = limit[:, None, :]
    expert_in = jnp.transpose(expert_in, (1, 0, 2))
    expert_out = jnp.transpose(expert_out, (1, 0, 2))
    own_out, lse = attend(place, info, limit, q, kvs)
    attended_low = heads_to_rows(trade_heads(own_out))
    residual_between = hidden + jnp.dot(
        attended_low, attention_output_weight, preferred_element_type=F32
    )
    scale_two = rms_scale(residual_between)
    combined_input = (residual_between * scale_two * norm_ffn).astype(BF16)
    experts_total = router.shape[1]
    local_experts = expert_in.shape[0]
    groups = place.experts
    capacity = row_count * TOP * 5 // (4 * experts_total)
    router_scores = jnp.dot(combined_input, router, preferred_element_type=F32)
    chosen = routes[0]
    column = jnp.arange(experts_total, dtype=jnp.int32)
    pick_hot = (chosen[:, :, None] == column[None, None, :]).astype(F32)
    picked = jnp.sum(pick_hot * router_scores[:, None, :], axis=-1)
    gate_weights = jax.nn.softmax(picked, axis=-1)
    column_expert = column % groups * local_experts + column // groups
    flat_routes = chosen.reshape(row_count * TOP)
    route_hot = (flat_routes[:, None] == column_expert[None, :]).astype(jnp.int32)
    earlier = jnp.cumsum(route_hot, axis=0) - route_hot
    slot_index = jnp.sum(earlier * route_hot, axis=1)
    target = jnp.where(
        slot_index < capacity, jnp.sum(route_hot * column[None, :], axis=1) * capacity + slot_index, -1
    ).reshape(row_count, TOP)
    seats = jnp.arange(experts_total * capacity, dtype=jnp.int32)
    hot = [(target[:, k : k + 1] == seats[None, :]).astype(BF16) for k in range(TOP)]
    upstream = cotangent[0]
    grad_upper = upstream.astype(F32)

    def dispatch(matrix, rows):
        return lax.dot_general(
            matrix, rows, (((0,), (0,)), ((), ())), preferred_element_type=F32
        )

    def trade(rows):
        return lax.all_to_all(rows, EX, split_axis=1, concat_axis=1, tiled=True)

    seat_shape = (local_experts, groups, capacity, model_width)
    every = hot[0] + hot[1]
    send_rows = dispatch(every, combined_input).astype(BF16)
    seat_gates = jnp.sum(
        sum(
            (target[:, k : k + 1] == seats[None, :]) * gate_weights[:, k : k + 1] for k in range(TOP)
        ),
        axis=0,
    )
    grad_send = (dispatch(every, upstream) * seat_gates[:, None]).astype(BF16)
    arrived = trade(send_rows.reshape(seat_shape)).reshape(
        local_experts, groups * capacity, model_width
    )
    grad_arrived = trade(grad_send.reshape(seat_shape)).reshape(
        local_experts, groups * capacity, model_width
    )
    shared_result, grad_mixed, *shared_grads = ffn(
        True,
        place,
        place.shared_table(model_width),
        combined_input,
        upstream,
        shared_gate_up_weight[None],
        shared_down_weight[None],
        0,
    )
    table = place.expert_table(model_width)
    came_back, in_grads, out_grads = [], [], []
    for e in range(local_experts):
        both, in_keep, in_send, out_keep, out_send = ffn(
            False, place, table, arrived[e], grad_arrived[e], expert_in, expert_out, e
        )
        came_back.append(
            lax.all_to_all(
                both.reshape(groups, capacity, 2 * model_width),
                EX,
                split_axis=0,
                concat_axis=0,
                tiled=True,
            ).reshape(groups * capacity, 2 * model_width)
        )
        in_grads.append(reduce_experts(place, in_keep, in_send, 1))
        out_grads.append(reduce_experts(place, out_keep, out_send, 0))
    sum_shared_in = reduce_shared_in(place, *shared_grads[:2])
    sum_shared_out = reduce_shared_out(place, *shared_grads[2:])
    returned = jnp.concatenate(came_back, axis=0)
    back_rows = [
        jnp.dot(h, returned[:, :model_width], preferred_element_type=F32) for h in hot
    ]
    routed = sum(gate_weights[:, k : k + 1] * back_rows[k] for k in range(TOP))
    output = (residual_between + routed + shared_result).astype(BF16)[None]
    grad_gates = jnp.stack([jnp.sum(b * grad_upper, axis=-1) for b in back_rows], axis=1)
    grad_picked = gate_weights * (
        grad_gates - jnp.sum(gate_weights * grad_gates, axis=-1, keepdims=True)
    )
    grad_logits = jnp.sum(pick_hot * grad_picked[:, :, None], axis=1).astype(BF16)
    grad_router = jnp.einsum("td,te->de", combined_input, grad_logits, preferred_element_type=F32)
    grad_mixed = (
        grad_mixed
        + jnp.einsum("te,de->td", grad_logits, router, preferred_element_type=F32)
        + jnp.dot(every, returned[:, model_width:], preferred_element_type=F32)
    )
    grad_norm_ffn = jnp.sum(grad_mixed * residual_between * scale_two, axis=0)
    grad_middle = grad_upper + rms_back(residual_between, scale_two, norm_ffn, grad_mixed)
    grad_attn_low = grad_middle.astype(BF16)
    grad_attended = jnp.einsum(
        "te,de->td", grad_attn_low, attention_output_weight, preferred_element_type=F32
    ).astype(BF16)
    own_grad = trade_heads(rows_to_heads(grad_attended, place.groups))
    own_dq, *own_dkv = attend_back(place, info, limit, lse, q, own_out, own_grad, kvs)
    if place.lanes == 2:
        dkv = add(own_dkv[0], swap(own_dkv[1], "r"))
    else:
        dkv = scatter(jnp.stack(own_dkv), "r", 0)[0]
    grad_projected, grad_input, grad_norm_attn = finish(
        trade_heads(own_dq),
        trade_heads(dkv),
        query_key_value_weight,
        cosine,
        sine,
        tokens[0],
        norm_attn,
        grad_middle,
    )
    grad_norm_attn = grad_norm_attn[0]
    sum_qkv = weight_grad(place, to_flat(place, normalized_rows), grad_projected)
    sum_out = weight_grad(place, to_flat(place, attended_low), grad_attn_low)
    small = jnp.concatenate([grad_norm_ffn[:, None], grad_router], axis=1)
    small = lax.psum(small, DP + EX)
    own = model_width // place.dp
    small = lax.dynamic_slice_in_dim(small, shard_index * own, own, 0)
    sum_router = lax.dynamic_slice_in_dim(
        small[:, 1:], lax.axis_index(EX) * local_experts, local_experts, 1
    )
    sum_norm_attn = lax.dynamic_slice_in_dim(
        lax.psum(grad_norm_attn, DP + EX), shard_index * own, own, 0
    )
    part_in = jnp.stack([g.transpose(1, 0, 2).reshape(own, -1) for g in in_grads], axis=1)
    part_out = jnp.stack(out_grads, axis=1)
    return (
        output,
        grad_input[None],
        sum_norm_attn,
        sum_qkv,
        sum_out,
        small[:, 0],
        sum_router,
        part_in,
        part_out,
        sum_shared_in,
        sum_shared_out.T,
    )


def solution(mesh):
    dp, experts = mesh.shape["dp"], mesh.shape["expert"]
    finer = Mesh(mesh.devices.reshape(4, dp // 4, experts // 2, 2), ("g", "r", "y", "c"))
    whole = P()
    return jax.shard_map(
        local,
        mesh=finer,
        in_specs=(
            P(EX, DP, None),
            whole,
            whole,
            whole,
            whole,
            whole,
            P(None, EX, None),
            P(None, EX, None),
            whole,
            whole,
            P(EX, None),
            P(EX, DP, None),
            P(EX, DP, None),
        ),
        out_specs=(
            P(EX, DP, None),
            P(EX, DP, None),
            P(DP),
            P(DP, EX),
            P(DP, EX),
            P(DP),
            P(DP, EX),
            P(DP, EX, None),
            P(DP, EX, None),
            P(DP, EX),
            P(DP, EX),
        ),
        check_vma=False,
    )
```

```python
import functools

import jax
import jax.numpy as jnp
from jax import lax
from jax.experimental import pallas as pl
from jax.experimental.pallas import tpu as pltpu
from jax.sharding import Mesh
from jax.sharding import PartitionSpec as P

HEADS = 12
HEAD_DIM = 64
TOP = 2
EPS = 1e-06
NEG = -1e30
F32 = jnp.float32
BF16 = jnp.bfloat16
STEPS = 8
DP = ("g", "r")
EX = ("y", "c")
LEADS = ("g", "r")
SMALL = pl.CostEstimate(flops=1024, bytes_accessed=1024, transcendentals=0)


def rope_table(positions):
    lane = jnp.arange(2 * HEAD_DIM, dtype=jnp.int32) % HEAD_DIM
    half_dim = HEAD_DIM // 2
    frequency = 10000.0 ** (-(lane % half_dim).astype(F32) * 2.0 / HEAD_DIM)
    angles = positions.astype(F32)[:, None] * frequency[None, :]
    return jnp.cos(angles), jnp.sin(angles) * jnp.where(lane < half_dim, -1.0, 1.0)


def rms_scale(hidden):
    return lax.rsqrt(jnp.mean(hidden * hidden, axis=-1, keepdims=True) + EPS)


def rms_back(hidden, scale_rows, gain_vector, upstream):
    normed_grad = upstream * gain_vector
    inner_mean = jnp.mean(normed_grad * hidden, axis=-1, keepdims=True)
    return scale_rows * normed_grad - hidden * scale_rows**3 * inner_mean


class Place:
    def __init__(self):
        self.groups, self.lanes = lax.axis_size("g"), lax.axis_size("r")
        self.rows_y = lax.axis_size("y")
        self.dp = self.groups * self.lanes
        self.experts = self.rows_y * 2
        self.g, self.r = lax.axis_index("g"), lax.axis_index("r")
        self.y, self.c = lax.axis_index("y"), lax.axis_index("c")
        self.low, self.high = self.g % 2, self.g // 2

    def own(self, b):
        g, r = b // self.lanes, b % self.lanes
        low, high = g % 2, g // 2
        if self.lanes == 2:
            return r ^ self.r, low * 2 + high
        return low ^ self.low, high * self.lanes + r

    def flat(self, b):
        g, r = b // self.lanes, b % self.lanes
        if self.lanes == 2:
            return r * 4 + (g % 2) * 2 + g // 2
        return (g % 2 * 2 + g // 2) * self.lanes + r

    def expert_table(self, width, lead):
        sub = STEPS // 4
        order = []
        for pos in range(STEPS):
            half, rest = pos // 4, pos % 4
            if self.lanes == 2 and lead == "r":
                low, high, part = rest // 2, rest % 2, half ^ self.r
            elif self.lanes == 2:
                low, high, part = half ^ self.low, rest % 2, rest // 2
            else:
                low, high, part = half ^ self.low, rest // 2, rest % 2
            order.append((high * 2 + low) * sub + part)
        block = width // self.dp
        rows = []
        for b in range(self.dp):
            half, rest = self.own(b)
            rows.append(half * (width // 2) + rest * block)
        return jnp.stack([jnp.asarray(v, jnp.int32) for v in order + [0] * STEPS + rows])

    def shared_table(self, width):
        per = 16 // self.experts
        order, columns = [], []
        sub = STEPS // 4
        for pos in range(STEPS):
            half, rest = pos // 4, pos % 4
            j = (rest // per * 2 + (half ^ self.c)) * per + rest % per
            order.append(j)
            g, part = j // sub, j % sub
            if self.lanes == 2:
                columns.append(part * 4 + g % 2 * 2 + g // 2)
            else:
                columns.append((g % 2 * 2 + g // 2) * sub + part)
        block = width // self.dp
        rows = [self.flat(b) * block for b in range(self.dp)]
        own = width // self.experts
        turned = [
            (e % 2 ^ self.c) * (width // 2) + e // 2 * own for e in range(self.experts)
        ]
        return jnp.stack(
            [jnp.asarray(v, jnp.int32) for v in order + columns + rows + turned]
        )


def nt(a, b):
    return lax.dot_general(a, b, (((1,), (1,)), ((), ())), preferred_element_type=F32)


def nn(a, b):
    return lax.dot_general(a, b, (((1,), (0,)), ((), ())), preferred_element_type=F32)


def turn(x, cosine, sine):
    width = x.shape[1]
    lane = lax.broadcasted_iota(jnp.int32, x.shape, 1) % HEAD_DIM
    other = jnp.where(
        lane < HEAD_DIM // 2,
        pltpu.roll(x, width - HEAD_DIM // 2, 1),
        pltpu.roll(x, HEAD_DIM // 2, 1),
    )
    times = width // cosine.shape[1]
    cosine = jnp.concatenate([cosine] * times, axis=1)
    sine = jnp.concatenate([sine] * times, axis=1)
    return x * cosine + other * sine


def project_kernel(here, x_ref, gain_ref, w_ref, cos_ref, sin_ref, normed_ref, *refs):
    step = pl.program_id(0)
    groups = (len(refs) - 2) // 2
    q_refs, kv_refs, (q_all, kv_all) = refs[:groups], refs[groups:-2], refs[-2:]
    half, three = x_ref.shape[0] // 2, 3 * HEAD_DIM

    @pl.when(step == 0)
    def _():
        x = x_ref[...].astype(F32)
        normed_ref[...] = (x * rms_scale(x) * gain_ref[...]).astype(BF16)

    part = nn(normed_ref[...], w_ref[...])

    @pl.when(step == 0)
    def _():
        pack_heads(turn(part, cos_ref[...], sin_ref[...]) * HEAD_DIM**-0.5, q_all)

    @pl.when(step == 1)
    def _():
        k = turn(part, cos_ref[...], sin_ref[...])
        for g in range(groups):
            own = k[:, g * three : (g + 1) * three].astype(BF16)
            kv_all[g, :, 0:128] = own[:, :128]
            kv_all[g, :, 256:320] = own[:, 128:]

    @pl.when(step == 2)
    def _():
        for g in range(groups):
            own = part[:, g * three : (g + 1) * three].astype(BF16)
            kv_all[g, :, 128:256] = own[:, :128]
            kv_all[g, :, 320:384] = own[:, 128:]
        for d in range(groups):
            q_refs[d][...] = q_all[here[0] ^ d]
            kv_refs[d][...] = kv_all[here[0] ^ d]


def pack_heads(rows, packed_ref):
    half, three = rows.shape[0] // 2, 3 * HEAD_DIM
    for g in range(packed_ref.shape[0]):
        own = rows[:, g * three : (g + 1) * three].astype(BF16)
        packed_ref[g, :, 0:128] = own[:half, :128]
        packed_ref[g, :, 128:256] = own[half:, :128]
        packed_ref[g, :, 256:320] = own[:half, 128:]
        packed_ref[g, :, 320:384] = own[half:, 128:]


def project(place, x, gain, weight, cosine, sine):
    rows, width = x.shape
    groups = place.groups
    sds = jax.ShapeDtypeStruct
    whole = lambda *shape: pl.BlockSpec(shape, lambda i, t: (0,) * len(shape))
    normed, *parts = pl.pallas_call(
        project_kernel,
        out_shape=(sds((rows, width), BF16),)
        + (sds((rows // 2, 384), BF16),) * groups
        + (sds((rows, 384), BF16),) * groups,
        grid_spec=pltpu.PrefetchScalarGridSpec(
            num_scalar_prefetch=1,
            grid=(3,),
            in_specs=[
                whole(rows, width),
                whole(1, width),
                pl.BlockSpec((width, width), lambda i, t: (0, i)),
                whole(rows, 128),
                whole(rows, 128),
            ],
            out_specs=(whole(rows, width),)
            + (whole(rows // 2, 384),) * groups
            + (whole(rows, 384),) * groups,
            scratch_shapes=[
                pltpu.VMEM((groups, rows // 2, 384), BF16),
                pltpu.VMEM((groups, rows, 384), BF16),
            ],
        ),
        compiler_params=pltpu.CompilerParams(vmem_limit_bytes=32 * 1024 * 1024),
        cost_estimate=SMALL,
    )(place.g[None], x, gain[None], weight, cosine, sine)
    return normed, parts[:groups], parts[groups:]


def unpack(packed, second_low):
    half = packed.shape[0]
    x = packed.astype(F32)
    lane = lax.broadcasted_iota(jnp.int32, (half, 128), 1)
    low = lane < HEAD_DIM
    first, second, third = x[:, 0:128], x[:, 128:256], x[:, 256:384]
    turned = pltpu.roll(third, HEAD_DIM, 1)
    zero = jnp.zeros_like(third)
    pair = [
        jnp.where(low, first, zero),
        jnp.where(low, second, zero),
        jnp.where(low, zero, first),
        jnp.where(low, zero, second),
    ]
    if second_low:
        single = [jnp.where(low, third, zero), jnp.where(low, turned, zero)]
    else:
        single = [jnp.where(low, zero, turned), jnp.where(low, zero, third)]
    return (
        jnp.concatenate(pair, axis=0).astype(BF16),
        jnp.concatenate(single, axis=0).astype(BF16),
    )


def visible_keys(kz, source, lanes, rows, limit):
    first = (kz * lanes + source) * rows
    place = first + lax.broadcasted_iota(jnp.int32, (rows, limit.shape[1]), 0)
    return place < limit


def attend_kernel(sources, shards, lanes, info, limit_ref, *refs):
    q_refs, kv_refs = refs[:shards], refs[shards : shards * (1 + sources)]
    out_refs, (lse_ref, q_ref, kv_all, turned, out_ref) = refs[shards * (1 + sources) : -5], refs[-5:]
    half = q_ref.shape[1]
    rows = 2 * half
    gather_heads(info, q_refs, q_ref)
    gather_keys(info, shards, kv_refs, kv_all, turned)

    def shard(z, carry):
        pair, single = unpack(q_ref[z], True)
        limit = limit_ref[z]

        def step(kz, state):
            largest, total, acc_pair, acc_single = state
            scores = []
            for s in range(sources):
                keep = visible_keys(kz, info[1 + shards + s], lanes, rows, limit)
                two = nt(kv_all[s, kz, :, 0:128], pair)
                one = nt(kv_all[s, kz, :, 256:384], single)
                both = jnp.concatenate([two, one], axis=1)
                keep = jnp.concatenate([keep] * 3, axis=1)
                scores.append(jnp.where(keep, both, NEG))
            newest = largest
            for sc in scores:
                newest = jnp.maximum(newest, jnp.max(sc, axis=0, keepdims=True))
            fade = jnp.exp(largest - newest)
            total = total * fade
            acc_pair = acc_pair * fade[:, : 2 * rows]
            acc_single = acc_single * fade[:, 2 * rows :]
            for s, sc in enumerate(scores):
                power = jnp.exp(sc - newest)
                total = total + jnp.sum(power, axis=0, keepdims=True)
                power = power.astype(BF16)
                acc_pair = acc_pair + nn(turned[s, kz, 128:256, :], power[:, : 2 * rows])
                acc_single = acc_single + nn(turned[s, kz, 256:384, :], power[:, 2 * rows :])
            return newest, total, acc_pair, acc_single

        largest, total, acc_pair, acc_single = lax.fori_loop(
            0,
            info[1 + z],
            step,
            (
                jnp.full((1, 3 * rows), NEG, F32),
                jnp.zeros((1, 3 * rows), F32),
                jnp.zeros((128, 2 * rows), F32),
                jnp.zeros((128, rows), F32),
            ),
        )
        lse_ref[z] = largest + jnp.log(total)
        share = 1.0 / total
        first = acc_pair[:HEAD_DIM, :rows] * share[:, :rows]
        second = acc_pair[HEAD_DIM:, rows:] * share[:, rows : 2 * rows]
        third = acc_single[HEAD_DIM:] * share[:, 2 * rows :]
        packed = jnp.concatenate(
            [a[:, part] for part in (slice(0, half), slice(half, rows)) for a in (first, second)]
            + [third[:, :half], third[:, half:]],
            axis=0,
        )
        out_ref[z] = packed.T.astype(BF16)
        return carry

    lax.fori_loop(0, shards, shard, 0)


    for d in range(shards):
        out_refs[d][...] = out_ref[info[0] ^ d]


def gather_heads(info, refs, packed_ref):
    for d, ref in enumerate(refs):
        packed_ref[info[0] ^ d] = ref[...]


def gather_keys(info, shards, refs, kv_all, turned):
    for i, ref in enumerate(refs):
        at = info[0] ^ (i % shards)
        kv_all[i // shards, at] = ref[...]
        turned[i // shards, at] = ref[...].astype(F32).T.astype(BF16)


def attend(place, info, limit, qs, kvs):
    half, lanes = qs[0].shape
    shards, sources = len(qs), len(kvs) // len(qs)
    vmem = pl.BlockSpec(memory_space=pltpu.VMEM)
    sds = jax.ShapeDtypeStruct
    *outs, lse = pl.pallas_call(
        functools.partial(attend_kernel, sources, shards, place.lanes),
        out_shape=(sds((half, lanes), BF16),) * shards + (sds((shards, 1, 6 * half), F32),),
        in_specs=[pl.BlockSpec(memory_space=pltpu.SMEM)] + [vmem] * (1 + shards * (1 + sources)),
        out_specs=(vmem,) * (shards + 1),
        scratch_shapes=[
            pltpu.VMEM((shards, half, lanes), BF16),
            pltpu.VMEM((sources, shards, 2 * half, lanes), BF16),
            pltpu.VMEM((sources, shards, lanes, 2 * half), BF16),
            pltpu.VMEM((shards, half, lanes), BF16),
        ],
        compiler_params=pltpu.CompilerParams(vmem_limit_bytes=48 * 1024 * 1024),
        cost_estimate=SMALL,
    )(info, limit, *qs, *kvs)
    return outs, lse


def attend_back_kernel(sources, shards, lanes, info, limit_ref, lse_ref, *refs):
    q_refs, o_refs, g_refs = (refs[i * shards : (i + 1) * shards] for i in range(3))
    kv_refs = refs[3 * shards : (3 + sources) * shards]
    dq_refs = refs[(3 + sources) * shards : (4 + sources) * shards]
    dkv_refs = refs[(4 + sources) * shards : (4 + 2 * sources) * shards]
    q_ref, out_ref, grad_ref, dq_ref, kv_all, turned, total = refs[-7:]
    half = q_ref.shape[1]
    rows = 2 * half
    gather_heads(info, q_refs, q_ref)
    gather_heads(info, o_refs, out_ref)
    gather_heads(info, g_refs, grad_ref)
    gather_keys(info, shards, kv_refs, kv_all, turned)
    total[...] = jnp.zeros_like(total)

    def shard(z, carry):
        pair, single = unpack(q_ref[z], True)
        grad_pair, grad_single = unpack(grad_ref[z], False)
        limit, lse = limit_ref[z], lse_ref[z]
        product = (grad_ref[z].astype(F32) * out_ref[z].astype(F32)).T
        sums = [
            jnp.sum(product[i * HEAD_DIM : (i + 1) * HEAD_DIM], axis=0, keepdims=True)
            for i in range(6)
        ]
        delta = jnp.concatenate([sums[0], sums[2], sums[1], sums[3], sums[4], sums[5]], axis=1)

        def step(kz, state):
            dq_pair, dq_single = state
            for s in range(sources):
                keep = visible_keys(kz, info[1 + shards + s], lanes, rows, limit)
                keep = jnp.concatenate([keep] * 3, axis=1)
                k01, v01 = kv_all[s, kz, :, 0:128], kv_all[s, kz, :, 128:256]
                kv2 = kv_all[s, kz, :, 256:384]
                scores = jnp.concatenate([nt(k01, pair), nt(kv2, single)], axis=1)
                grads = jnp.concatenate([nt(v01, grad_pair), nt(kv2, grad_single)], axis=1)
                power = jnp.where(keep, jnp.exp(scores - lse), 0.0)
                slope = (power * (grads - delta)).astype(BF16)
                power = power.astype(BF16)
                dq_pair = dq_pair + nn(turned[s, kz, 0:128, :], slope[:, : 2 * rows])
                dq_single = dq_single + nn(turned[s, kz, 256:384, :], slope[:, 2 * rows :])
                total[s, kz, :, 0:128] += nn(slope[:, : 2 * rows], pair)
                total[s, kz, :, 128:256] += nn(power[:, : 2 * rows], grad_pair)
                total[s, kz, :, 256:384] += nn(slope[:, 2 * rows :], single) + nn(
                    power[:, 2 * rows :], grad_single
                )
            return dq_pair, dq_single

        dq_pair, dq_single = lax.fori_loop(
            0,
            info[1 + z],
            step,
            (jnp.zeros((128, 2 * rows), F32), jnp.zeros((128, rows), F32)),
        )
        first, second = dq_pair[:HEAD_DIM, :rows], dq_pair[HEAD_DIM:, rows:]
        third = dq_single[:HEAD_DIM]
        packed = jnp.concatenate(
            [a[:, part] for part in (slice(0, half), slice(half, rows)) for a in (first, second)]
            + [third[:, :half], third[:, half:]],
            axis=0,
        )
        dq_ref[z] = packed.T.astype(BF16)
        return carry

    lax.fori_loop(0, shards, shard, 0)
    for d in range(shards):
        dq_refs[d][...] = dq_ref[info[0] ^ d]
    for i, ref in enumerate(dkv_refs):
        ref[...] = total[i // shards, info[0] ^ (i % shards)].astype(BF16)


def attend_back(place, info, limit, lse, qs, outs, grads, kvs):
    half, lanes = qs[0].shape
    shards, sources = len(qs), len(kvs) // len(qs)
    vmem = pl.BlockSpec(memory_space=pltpu.VMEM)
    sds = jax.ShapeDtypeStruct
    parts = pl.pallas_call(
        functools.partial(attend_back_kernel, sources, shards, place.lanes),
        out_shape=(sds((half, lanes), BF16),) * shards
        + (sds((2 * half, lanes), BF16),) * (shards * sources),
        in_specs=[pl.BlockSpec(memory_space=pltpu.SMEM)] + [vmem] * (2 + shards * (3 + sources)),
        out_specs=(vmem,) * (shards * (1 + sources)),
        scratch_shapes=[pltpu.VMEM((shards, half, lanes), BF16)] * 4
        + [
            pltpu.VMEM((sources, shards, 2 * half, lanes), BF16),
            pltpu.VMEM((sources, shards, lanes, 2 * half), BF16),
            pltpu.VMEM((sources, shards, 2 * half, lanes), F32),
        ],
        compiler_params=pltpu.CompilerParams(vmem_limit_bytes=56 * 1024 * 1024),
        cost_estimate=SMALL,
    )(info, limit, lse, *qs, *outs, *grads, *kvs)
    return parts[:shards], [parts[i * shards : (i + 1) * shards] for i in range(1, 1 + sources)]


def finish_kernel(
    here, w_ref, cos_ref, sin_ref, x_ref, gain_ref, middle_ref, *refs,
):
    groups = (len(refs) - 6) // 2
    dq_refs, dkv_refs = refs[:groups], refs[groups : 2 * groups]
    projected_ref, input_ref, norm_ref, dq_all, dkv_all, gather = refs[2 * groups :]
    rows, width = x_ref.shape
    half, three = rows // 2, 3 * HEAD_DIM
    for d in range(groups):
        dq_all[here[0] ^ d] = dq_refs[d][...].astype(F32)
        dkv_all[here[0] ^ d] = dkv_refs[d][...].astype(F32)
    for g in range(groups):
        at = g * three
        dq, dkv = dq_all[g], dkv_all[g]
        gather[0, :half, at : at + 128] = dq[:, 0:128]
        gather[0, half:, at : at + 128] = dq[:, 128:256]
        gather[0, :half, at + 128 : at + three] = dq[:, 256:320]
        gather[0, half:, at + 128 : at + three] = dq[:, 320:384]
        gather[1, :, at : at + 128] = dkv[:, 0:128]
        gather[1, :, at + 128 : at + three] = dkv[:, 256:320]
        gather[2, :, at : at + 128] = dkv[:, 128:256]
        gather[2, :, at + 128 : at + three] = dkv[:, 320:384]
    cosine, sine = cos_ref[...], -sin_ref[...]
    parts = [
        (turn(gather[0], cosine, sine) * HEAD_DIM**-0.5).astype(BF16),
        turn(gather[1], cosine, sine).astype(BF16),
        gather[2].astype(BF16),
    ]
    grad = jnp.zeros((rows, width), F32)
    for i, part in enumerate(parts):
        projected_ref[:, i * width : (i + 1) * width] = part
        grad = grad + nt(part, w_ref[:, i * width : (i + 1) * width])
    x = x_ref[...].astype(F32)
    scale = rms_scale(x)
    norm_ref[...] = jnp.sum(grad * x * scale, axis=0, keepdims=True)
    input_ref[...] = middle_ref[...] + rms_back(x, scale, gain_ref[...], grad)


def finish(place, dqs, dkvs, weight, cosine, sine, x, gain, middle):
    rows, width = x.shape
    groups = place.groups
    vmem = pl.BlockSpec(memory_space=pltpu.VMEM)
    return pl.pallas_call(
        finish_kernel,
        out_shape=(
            jax.ShapeDtypeStruct((rows, 3 * width), BF16),
            jax.ShapeDtypeStruct((rows, width), F32),
            jax.ShapeDtypeStruct((1, width), F32),
        ),
        in_specs=[pl.BlockSpec(memory_space=pltpu.SMEM)] + [vmem] * (6 + 2 * groups),
        out_specs=(vmem,) * 3,
        scratch_shapes=[
            pltpu.VMEM((groups, rows // 2, 384), F32),
            pltpu.VMEM((groups, rows, 384), F32),
            pltpu.VMEM((3, rows, width), F32),
        ],
        compiler_params=pltpu.CompilerParams(vmem_limit_bytes=48 * 1024 * 1024),
        cost_estimate=SMALL,
    )(place.g[None], weight, cosine, sine, x, gain[None], middle, *dqs, *dkvs)


def middle_kernel(
    here, x_ref, grad_ref, w_ref, gain_ref, router_ref, pick0, pick1, seat0, seat1, *refs,
):
    groups = 4
    o_refs = refs[:groups]
    low_ref, middle_ref, mixed_ref, gate_ref = refs[groups : groups + 4]
    sent = refs[groups + 4 : -2]
    o_all, gather = refs[-2:]
    count = len(sent) // 2
    half, three = x_ref.shape[0] // 2, 3 * HEAD_DIM
    for d in range(groups):
        o_all[here[0] ^ d] = o_refs[d][...].astype(F32)
    for g in range(groups):
        at = g * three
        gather[:half, at : at + 128] = o_all[g, :, 0:128]
        gather[half:, at : at + 128] = o_all[g, :, 128:256]
        gather[:half, at + 128 : at + three] = o_all[g, :, 256:320]
        gather[half:, at + 128 : at + three] = o_all[g, :, 320:384]
    low = gather[...].astype(BF16)
    low_ref[...] = low
    middle = x_ref[...].astype(F32) + nn(low, w_ref[...])
    middle_ref[...] = middle
    mixed = (middle * rms_scale(middle) * gain_ref[...]).astype(BF16)
    mixed_ref[...] = mixed
    scores = nn(mixed, router_ref[...])
    picked = [jnp.sum(scores * p[...], axis=1, keepdims=True) for p in (pick0, pick1)]
    largest = jnp.maximum(*picked)
    powers = [jnp.exp(p - largest) for p in picked]
    gates = [p / (powers[0] + powers[1]) for p in powers]
    gate_ref[...] = jnp.concatenate(gates, axis=1)
    seats = (seat0[...], seat1[...])
    held = jnp.zeros((seats[0].shape[0], 1), F32)
    for seat, gate in zip(seats, gates):
        high = gate.astype(BF16)
        rest = (gate - high.astype(F32)).astype(BF16)
        held = held + jnp.sum(nn(seat, jnp.concatenate([high, rest], axis=1)), axis=1, keepdims=True)
    every = seats[0] + seats[1]
    rows = nn(every, mixed).astype(BF16)
    grads = (nn(every, grad_ref[...]) * held).astype(BF16)
    capacity = sent[0].shape[1]
    for d in range(count):
        for e in range(sent[0].shape[0]):
            at = (e * count + d) * capacity
            sent[d][e] = rows[at : at + capacity]
            sent[count + d][e] = grads[at : at + capacity]


def middle_part(place, capacity, outs, x, grad, weight, gain, router, picks, seats):
    rows, width = x.shape
    groups, count = place.groups, place.experts
    local = router.shape[1] // count
    vmem = pl.BlockSpec(memory_space=pltpu.VMEM)
    sds = jax.ShapeDtypeStruct
    low, middle, mixed, gates, *sent = pl.pallas_call(
        middle_kernel,
        out_shape=(
            sds((rows, width), BF16),
            sds((rows, width), F32),
            sds((rows, width), BF16),
            sds((rows, TOP), F32),
        )
        + (sds((local, capacity, width), BF16),) * (2 * count),
        in_specs=[pl.BlockSpec(memory_space=pltpu.SMEM)] + [vmem] * (9 + groups),
        out_specs=(vmem,) * (4 + 2 * count),
        scratch_shapes=[
            pltpu.VMEM((groups, rows // 2, 384), F32),
            pltpu.VMEM((rows, width), F32),
        ],
        compiler_params=pltpu.CompilerParams(vmem_limit_bytes=48 * 1024 * 1024),
        cost_estimate=SMALL,
    )(place.g[None], x, grad, weight, gain[None], router, *picks, *seats, *outs)
    return low, middle, mixed, gates, sent[:count], sent[count:]


def trade(parts, axis):
    size = lax.axis_size(axis)
    return [parts[0]] + [
        lax.ppermute(parts[d], axis, [(i, i ^ d) for i in range(size)]) for d in range(1, size)
    ]


def ffn_kernel(shared, count, dp, experts, table, *refs):
    x_refs, dy_refs, (gate_ref, up_ref, down_ref) = refs[:count], refs[count : 2 * count], refs[2 * count : 2 * count + 3]
    refs = refs[2 * count + 3 :]
    if shared:
        result, back, in_keep, in_send, out_keep, out_send, stage, turned, turned_dy = refs
        x_ref, dy_ref = x_refs[0], dy_refs[0]
    else:
        both, refs = refs[:count], refs[count:]
        gate_keep, gate_send, up_keep, up_send, out_keep, out_send = refs[:6]
        in_keep, in_send = (gate_keep, up_keep), (gate_send, up_send)
        stage, turned, result, back, x_ref, dy_ref = refs[6:]
    step = pl.program_id(0)
    width = x_ref.shape[1]
    rows = x_ref.shape[0]

    @pl.when(step == 0)
    def _():
        if not shared:
            part = rows // count
            for d in range(count):
                x_ref[d * part : (d + 1) * part] = x_refs[d][0]
                dy_ref[d * part : (d + 1) * part] = dy_refs[d][0]
        whole = x_ref[...].astype(F32).T
        block = width // dp
        for b in range(dp):
            start = pl.multiple_of(table[2 * STEPS + b], 8)
            stage[pl.ds(start, block), :] = whole[b * block : (b + 1) * block]
        turned[...] = stage[...].astype(BF16)
        if shared:
            whole = dy_ref[...].astype(F32).T
            block = width // experts
            for e in range(experts):
                start = pl.multiple_of(table[2 * STEPS + dp + e], 8)
                stage[pl.ds(start, block), :] = whole[e * block : (e + 1) * block]
            turned_dy[...] = stage[...].astype(BF16)
        result[...] = jnp.zeros_like(result)
        back[...] = jnp.zeros_like(back)

    x, dy = x_ref[...], dy_ref[...]
    w_gate, w_up, w_down = gate_ref[0], up_ref[0], down_ref[0]
    gate, up = nn(x, w_gate), nn(x, w_up)
    grad = nt(dy, w_down)
    sig = jax.nn.sigmoid(gate)
    silu = gate * sig
    act = (silu * up).astype(BF16)
    grad_gate = (grad * up * (sig * (1.0 + gate * (1.0 - sig)))).astype(BF16)
    grad_up = (grad * silu).astype(BF16)
    result[...] += nn(act, w_down)
    back[...] += nt(grad_gate, w_gate) + nt(grad_up, w_up)
    xt = turned[...]
    half = width // 2
    for k, upper in enumerate((grad_gate, grad_up)):
        grad_in = nn(xt, upper).astype(BF16)
        if shared:

            @pl.when(step < STEPS // 2)
            def _():
                in_keep[k] = grad_in

            @pl.when(step >= STEPS // 2)
            def _():
                in_send[k] = grad_in

        else:
            in_keep[k][...] = grad_in[:half]
            in_send[k][...] = grad_in[half:]
    if shared:
        grad_out = nn(turned_dy[...], act).astype(BF16)
        out_keep[...] = grad_out[:half]
        out_send[...] = grad_out[half:]
    else:
        grad_out = lax.dot_general(
            act, dy, (((0,), (0,)), ((), ())), preferred_element_type=F32
        ).astype(BF16)

        @pl.when(step < STEPS // 2)
        def _():
            out_keep[...] = grad_out

        @pl.when(step >= STEPS // 2)
        def _():
            out_send[...] = grad_out

        @pl.when(step == STEPS - 1)
        def _():
            part = rows // count
            for d in range(count):
                both[d][:, :width] = result[d * part : (d + 1) * part].astype(BF16)
                both[d][:, width:] = back[d * part : (d + 1) * part].astype(BF16)


def ffn(shared, place, table, xs, dys, w_in, w_out, e):
    count = len(xs)
    part, width = xs[0].shape[-2:]
    rows = part * count
    if shared:
        given = pl.BlockSpec((rows, width), lambda i, t: (0, 0))
    else:
        given = pl.BlockSpec((1, part, width), lambda i, t: (e, 0, 0))
    hidden = w_out.shape[1]
    chunk = hidden // STEPS
    near, far = STEPS // 2 - 1, STEPS // 2
    sds = jax.ShapeDtypeStruct
    first = lambda i, t: (0, 0, jnp.minimum(i, near))
    second = lambda i, t: (0, 0, jnp.maximum(i - far, 0))
    if shared:
        out_shape = (
            sds((rows, width), F32),
            sds((rows, width), F32),
            sds((2, width, hidden // 2), BF16),
            sds((2, width, hidden // 2), BF16),
            sds((width // 2, hidden), BF16),
            sds((width // 2, hidden), BF16),
        )
        out_specs = (
            pl.BlockSpec((rows, width), lambda i, t: (0, 0)),
            pl.BlockSpec((rows, width), lambda i, t: (0, 0)),
            pl.BlockSpec((2, width, chunk), first),
            pl.BlockSpec((2, width, chunk), second),
            pl.BlockSpec((width // 2, chunk), lambda i, t: (0, t[STEPS + i])),
            pl.BlockSpec((width // 2, chunk), lambda i, t: (0, t[STEPS + i])),
        )
        extra = [pltpu.VMEM((width, rows), BF16)]
    else:
        out_shape = (
            *[sds((part, 2 * width), BF16)] * count,
            *[sds((width // 2, hidden), BF16)] * 4,
            sds((hidden // 2, width), BF16),
            sds((hidden // 2, width), BF16),
        )
        out_specs = (
            *[pl.BlockSpec((part, 2 * width), lambda i, t: (0, 0))] * count,
            *[pl.BlockSpec((width // 2, chunk), lambda i, t: (0, t[i]))] * 4,
            pl.BlockSpec((chunk, width), lambda i, t: (jnp.minimum(i, near), 0)),
            pl.BlockSpec((chunk, width), lambda i, t: (jnp.maximum(i - far, 0), 0)),
        )
        extra = [pltpu.VMEM((rows, width), F32)] * 2 + [pltpu.VMEM((rows, width), BF16)] * 2
    return pl.pallas_call(
        functools.partial(ffn_kernel, shared, count, place.dp, place.experts),
        out_shape=out_shape,
        grid_spec=pltpu.PrefetchScalarGridSpec(
            num_scalar_prefetch=1,
            grid=(STEPS,),
            in_specs=[
                *[given] * (2 * count),
                pl.BlockSpec((1, width, chunk), lambda i, t: (e, 0, t[i])),
                pl.BlockSpec((1, width, chunk), lambda i, t: (e, 0, STEPS + t[i])),
                pl.BlockSpec((1, chunk, width), lambda i, t: (e, t[i], 0)),
            ],
            out_specs=out_specs,
            scratch_shapes=[pltpu.VMEM((width, rows), F32), pltpu.VMEM((width, rows), BF16)]
            + extra,
        ),
        compiler_params=pltpu.CompilerParams(vmem_limit_bytes=48 * 1024 * 1024),
        cost_estimate=SMALL,
    )(table, *xs, *dys, w_in, w_in, w_out)


def swap(a, axis, bit=1):
    size = lax.axis_size(axis)
    return lax.ppermute(a, axis, [(i, i ^ bit) for i in range(size)])


def add(a, b, kind=BF16):
    return (a.astype(F32) + b.astype(F32)).astype(kind)


def half_of(a, dim, index):
    size = a.shape[dim] // 2
    return lax.dynamic_slice_in_dim(a, index * size, size, dim)


def exchange(keep, came, dim, mine):
    return [add(half_of(keep, dim, i), half_of(came, dim, i)) for i in (mine, 1 - mine)]


def scatter(a, axis, dim):
    return lax.psum_scatter(a, axis, scatter_dimension=dim, tiled=True)


def reduce_experts(place, keep, send):
    came = swap(send, "g", 1)
    keep, send = exchange(keep, came, 0, place.high)
    return scatter(add(keep, swap(send, "g", 2)), "r", 0).astype(F32)


def after(x, *values):
    return lax.optimization_barrier((x, *values))[0]


def reduce_tokens(place, keep, came, dim):
    keep, send = exchange(keep, came, dim, place.low)
    came = swap(send, "g", 1)
    keep, send = exchange(keep, came, dim, place.high)
    came = swap(send, "g", 2)
    return scatter(add(keep, came), "r", dim).astype(F32)


def reduce_shared_in(place, keep, send):
    total = add(keep, swap(send, "c"))
    two, width, columns = total.shape
    parts = place.rows_y // 2
    total = total.reshape(two, width, parts, columns // parts).transpose(0, 2, 1, 3)
    mine = scatter(total.reshape(two * parts, width, columns // parts), "y", 0)[0]
    return reduce_tokens(place, mine, jnp.zeros_like(mine), 0)


def reduce_shared_out(place, keep, send):
    mine = scatter(add(keep, swap(send, "c")), "y", 0)
    return reduce_tokens(place, mine, jnp.zeros_like(mine), 1)


def to_flat(place, x):
    rows, width = x.shape
    x = x.reshape(rows, 2, 2, place.lanes, width // place.dp)
    order = (0, 3, 2, 1, 4) if place.lanes == 2 else (0, 2, 1, 3, 4)
    return x.transpose(order).reshape(rows, width)


def weight_grad(place, left, right, extra):
    rows, columns = right.shape
    width = left.shape[1]
    own = columns // place.experts
    parts = right.reshape(rows, place.rows_y, 2, own)
    extra = extra.reshape(width, place.rows_y, 2, extra.shape[-1]).astype(BF16)
    keep, send = [
        jnp.concatenate(
            [
                lax.dot_general(
                    left,
                    lax.dynamic_index_in_dim(parts, i, 2, False).reshape(rows, columns // 2),
                    (((0,), (0,)), ((), ())),
                    preferred_element_type=F32,
                )
                .astype(BF16)
                .reshape(width, place.rows_y, own),
                lax.dynamic_index_in_dim(extra, i, 2, False),
            ],
            axis=2,
        ).transpose(1, 0, 2)
        for i in (place.c, 1 - place.c)
    ]
    return keep, send


def reduce_weight(place, keep, send):
    mine = scatter(add(keep, swap(send, "c")), "y", 0)[0]
    return reduce_tokens(place, mine, jnp.zeros_like(mine), 0)


def in_two(vector):
    high = vector.astype(BF16).astype(F32)
    return [high, vector - high]


def beside(place, columns, experts_of):
    width = columns[0].shape[0]
    every = jnp.stack(columns, axis=1)[:, None, :]
    every = jnp.broadcast_to(every, (width, place.experts, len(columns)))
    parts = [every] if experts_of is None else [every, experts_of]
    used = sum(p.shape[2] for p in parts)
    return jnp.concatenate(parts + [jnp.zeros((width, place.experts, 64 - used), F32)], axis=2)


def combine_kernel(
    here, hot0, hot1, gate_ref, pick0, pick1, grad_ref, middle_ref,
    shared_ref, back_ref, mixed_in_ref, router_ref, gain_ref, w_ref, *refs,
):
    output_ref, middle_grad_ref, low_ref, *head_refs = refs[-11:-4]
    norm_ref, router_grad_ref, returned, heads = refs[-4:]
    ret_refs = refs[:-11]
    width = grad_ref.shape[1]
    part = ret_refs[0].shape[0]
    for i, ref in enumerate(ret_refs):
        returned[i * part : (i + 1) * part] = ref[...]
    hots = (hot0[...], hot1[...])
    grad = grad_ref[...].astype(F32)
    middle = middle_ref[...]
    backs = [nn(h, returned[:, :width]) for h in hots]
    gates = [gate_ref[:, k : k + 1] for k in range(TOP)]
    routed = sum(gates[k] * backs[k] for k in range(TOP))
    output_ref[...] = (middle + routed + shared_ref[...]).astype(BF16)
    slopes = [jnp.sum(b * grad, axis=1, keepdims=True) for b in backs]
    inner = sum(gates[k] * slopes[k] for k in range(TOP))
    logits = sum(
        pick[...] * (gates[k] * (slopes[k] - inner)) for k, pick in enumerate((pick0, pick1))
    ).astype(BF16)
    router_grad_ref[...] = lax.dot_general(
        logits, mixed_in_ref[...], (((0,), (0,)), ((), ())), preferred_element_type=F32
    )
    mixed = back_ref[...] + nn(logits, router_ref[...]) + nn(hots[0] + hots[1], returned[:, width:])
    scale = rms_scale(middle)
    norm_ref[...] = jnp.sum(mixed * middle * scale, axis=0, keepdims=True)
    middle_grad = grad + rms_back(middle, scale, gain_ref[...], mixed)
    middle_grad_ref[...] = middle_grad
    low = middle_grad.astype(BF16)
    low_ref[...] = low
    pack_heads(nt(low, w_ref[...]), heads)
    for d, ref in enumerate(head_refs):
        ref[...] = heads[here[0] ^ d]


def combine(place, hots, rets, gates, picks, grad, middle, shared, back, mixed_in, router, gain, weight):
    rows, width = grad.shape
    vmem = pl.BlockSpec(memory_space=pltpu.VMEM)
    sds = jax.ShapeDtypeStruct
    output, middle_grad, low, *heads, norm, router_grad = pl.pallas_call(
        combine_kernel,
        out_shape=(
            sds((rows, width), BF16),
            sds((rows, width), F32),
            sds((rows, width), BF16),
        )
        + (sds((rows // 2, 384), BF16),) * place.groups
        + (
            sds((1, width), F32),
            sds((router.shape[1], width), F32),
        ),
        in_specs=[pl.BlockSpec(memory_space=pltpu.SMEM)] + [vmem] * (13 + len(rets)),
        out_specs=(vmem,) * (5 + place.groups),
        scratch_shapes=[
            pltpu.VMEM((hots[0].shape[1], 2 * width), BF16),
            pltpu.VMEM((place.groups, rows // 2, 384), BF16),
        ],
        compiler_params=pltpu.CompilerParams(vmem_limit_bytes=48 * 1024 * 1024),
        cost_estimate=SMALL,
    )(
        place.g[None], *hots, gates, *picks, grad, middle, shared, back, mixed_in,
        router.T, gain[None], weight, *rets,
    )
    return output, middle_grad, low, heads, norm, router_grad


class Sum:
    def __init__(self, keep, send, stages):
        self.keep, self.send, self.stages = keep, send, list(stages)

    def step(self, *behind):
        axis, bit, dim, mine = self.stages.pop(0)
        send = after(self.send, *behind) if behind else self.send
        came = swap(send, axis, bit)
        if dim is None:
            self.keep = add(self.keep, came, F32)
        else:
            self.keep, self.send = exchange(self.keep, came, dim, mine)
        return self.keep

    def finish(self):
        while self.stages:
            self.step()
        return self.keep


def expert_sum(place, keep, send, lead):
    if lead == "r":
        near = [("r", 1, 0, place.low), ("g", 1, 0, place.high)]
    else:
        near = [("g", 1, 0, place.r), ("r", 1, 0, place.high)]
    return Sum(keep, send, near + [("g", 2, None, None)])


def every_sum(place, keep, send, dim):
    return Sum(
        keep,
        send,
        [
            ("c", 1, 0, place.y),
            ("y", 1, dim, place.r),
            ("r", 1, dim, place.low),
            ("g", 1, dim, place.high),
            ("g", 2, None, None),
        ],
    )


def local(
    tokens,
    norm_attn,
    query_key_value_weight,
    attention_output_weight,
    norm_ffn,
    router,
    expert_in,
    expert_out,
    shared_gate_up_weight,
    shared_down_weight,
    block_lengths,
    routes,
    cotangent,
):
    place = Place()
    fast = place.lanes == 2 and place.rows_y == 2
    _, row_count, model_width = tokens.shape
    shard_index = lax.axis_index(DP)
    length = row_count * place.dp
    positions = shard_index * row_count + jnp.arange(row_count, dtype=jnp.int32)
    bounds = jnp.cumsum(block_lengths[0])
    cosine, sine = rope_table(positions)
    experts_total = router.shape[1]
    local_experts = expert_in.shape[1]
    groups = place.experts
    capacity = row_count * TOP * 5 // (4 * experts_total)
    chosen = routes[0]
    column = jnp.arange(experts_total, dtype=jnp.int32)
    picks = [(chosen[:, k : k + 1] == column[None, :]).astype(F32) for k in range(TOP)]
    flat_routes = chosen.reshape(row_count * TOP)
    route_hot = (flat_routes[:, None] == column[None, :]).astype(jnp.int32)
    earlier = jnp.cumsum(route_hot, axis=0) - route_hot
    slot_index = jnp.sum(earlier * route_hot, axis=1)
    partner = (flat_routes // local_experts) ^ lax.axis_index(EX)
    target = jnp.where(
        slot_index < capacity,
        (flat_routes % local_experts * groups + partner) * capacity + slot_index,
        -1,
    ).reshape(row_count, TOP)
    seats = jnp.arange(experts_total * capacity, dtype=jnp.int32)
    hots = [(target[:, k : k + 1] == seats[None, :]).astype(BF16) for k in range(TOP)]
    seated = [(target[:, k][None, :] == seats[:, None]).astype(BF16) for k in range(TOP)]
    upstream = cotangent[0]

    normalized_rows, own_q, own_kv = project(
        place, tokens[0], norm_attn, query_key_value_weight, cosine, sine
    )
    kv = trade(own_kv, "g")
    q = trade(own_q, "g")
    if fast:
        kvs = kv + [swap(a, "r") for a in kv]
        lanes_of = [place.r, 1 - place.r]
    else:
        every_kv = [lax.all_gather(a, "r", axis=0, tiled=False) for a in kv]
        kvs = [a[i] for i in range(place.lanes) for a in every_kv]
        lanes_of = [jnp.int32(i) for i in range(place.lanes)]
    starts = (jnp.arange(place.groups, dtype=jnp.int32) * place.lanes + place.r) * row_count
    query_places = starts[:, None] + jnp.arange(row_count, dtype=jnp.int32)[None, :]
    limit = jnp.min(
        jnp.where(bounds[None, None, :] > query_places[:, :, None], bounds, length), axis=-1
    )
    span = row_count * place.lanes
    info = jnp.concatenate(
        [place.g[None], (jnp.max(limit, axis=1) + span - 1) // span, jnp.stack(lanes_of)]
    ).astype(jnp.int32)
    limit = limit[:, None, :]
    expert_in = jnp.transpose(expert_in, (1, 0, 2))
    expert_out = jnp.transpose(expert_out, (1, 0, 2))
    q[0] = after(q[0], expert_in, expert_out)
    own_out, lse = attend(place, info, limit, q, kvs)
    attended_low, middle, mixed_in, gates, send_rows, send_grads = middle_part(
        place,
        capacity,
        trade(own_out, "g"),
        tokens[0],
        upstream,
        attention_output_weight,
        norm_ffn,
        router,
        picks,
        seated,
    )
    arrived = trade(send_rows, EX)
    grad_arrived = trade(send_grads, EX)
    shared_result, shared_back, *shared_grads = ffn(
        True,
        place,
        place.shared_table(model_width),
        [mixed_in],
        [upstream],
        shared_gate_up_weight[None],
        shared_down_weight[None],
        0,
    )
    came_back, parts = [], []
    behind = shared_result
    for e in range(local_experts):
        own = [after(arrived[0], behind)] + arrived[1:]
        results = ffn(
            False,
            place,
            place.expert_table(model_width, LEADS[e]),
            own,
            grad_arrived,
            expert_in,
            expert_out,
            e,
        )
        behind = results[0]
        came_back.append(trade(results[:groups], EX))
        parts.append(results[groups:])
    rets = [a for back in came_back for a in back]
    if fast:
        sums = [
            [expert_sum(place, *parts[e][k : k + 2], "r") for k in (0, 2)]
            + [expert_sum(place, *parts[e][4:], LEADS[e])]
            for e in range(local_experts)
        ]
        shared_in = every_sum(place, *shared_grads[:2], 1)
        shared_out = every_sum(place, *shared_grads[2:], 1)
        shared_in.step()
        shared_out.step()
        (first, second, third), (fourth, fifth, sixth) = sums
        first.step()
        third.step()
        rets[-1] = after(rets[-1], first.keep, third.keep)
    output, grad_middle, grad_attn_low, own_grad, grad_norm_ffn, grad_router = combine(
        place,
        hots,
        rets,
        gates,
        picks,
        upstream,
        middle,
        shared_result,
        shared_back,
        mixed_in,
        router,
        norm_ffn,
        attention_output_weight,
    )
    flat = lambda x: to_flat(place, x)
    extra = beside(
        place,
        in_two(flat(grad_norm_ffn)[0]),
        flat(grad_router).T.reshape(model_width, groups, local_experts),
    )
    own_grad = trade(own_grad, "g")
    sides_out = weight_grad(place, flat(attended_low), grad_attn_low, extra)
    if fast:
        second.step(first.keep)
        first.step()
        third.step()
        shared_in.step(rets[-1])
        shared_out.step(rets[-1])
        sum_out = every_sum(place, *sides_out, 1)
        sum_out.step()
        own_grad[0] = after(own_grad[0], first.keep)
    own_dq, own_dkv = attend_back(place, info, limit, lse, q, own_out, own_grad, kvs)
    dq = trade(own_dq, "g")
    if fast:
        first.step()
        came = [swap(a, "r") for a in own_dkv[1]]
        came[0] = after(came[0], second.keep, third.keep)
        dkv = [add(a, b) for a, b in zip(own_dkv[0], came)]
        fourth.step(came[0])
        second.step()
    else:
        dkv = [
            scatter(jnp.stack([a[d] for a in own_dkv]), "r", 0)[0] for d in range(place.groups)
        ]
    dkv = trade(dkv, "g")
    if fast:
        dkv[0] = after(dkv[0], second.keep, fourth.keep, shared_in.keep)
    grad_projected, grad_input, grad_norm_attn = finish(
        place,
        dq,
        dkv,
        query_key_value_weight,
        cosine,
        sine,
        tokens[0],
        norm_attn,
        grad_middle,
    )
    extra = beside(place, in_two(flat(grad_norm_attn)[0]), None)
    sides_qkv = weight_grad(place, flat(normalized_rows), grad_projected, extra)
    if fast:
        fifth.step(fourth.keep)
        sum_qkv = every_sum(place, *sides_qkv, 1)
        sum_qkv.step()
        fourth.step()
        sixth.step(fifth.keep)
        in_grads = [[s.finish() for s in row[:2]] for row in sums]
        out_grads = [row[2].finish() for row in sums]
        sum_shared_in, sum_shared_out = shared_in.finish()[0], shared_out.finish()
        sum_out, sum_qkv = sum_out.finish()[0], sum_qkv.finish()[0]
    else:
        in_grads = [
            [reduce_experts(place, *part[k : k + 2]) for k in (0, 2)] for part in parts
        ]
        out_grads = [reduce_experts(place, *part[4:]) for part in parts]
        sum_shared_in = reduce_shared_in(place, *shared_grads[:2])
        sum_shared_out = reduce_shared_out(place, *shared_grads[2:])
        sum_out, sum_qkv = reduce_weight(place, *sides_out), reduce_weight(place, *sides_qkv)
    own = model_width // place.experts
    sum_out, small = sum_out[:, :own], sum_out[:, own:]
    sum_norm_ffn, sum_router = small[:, 0] + small[:, 1], small[:, 2 : 2 + local_experts]
    sum_qkv, small = sum_qkv[:, : 3 * own], sum_qkv[:, 3 * own :]
    sum_norm_attn = small[:, 0] + small[:, 1]
    part_in = jnp.stack([jnp.concatenate(g, axis=1) for g in in_grads], axis=1)
    part_out = jnp.stack(out_grads, axis=1)
    return (
        output[None],
        grad_input[None],
        sum_norm_attn,
        sum_qkv,
        sum_out,
        sum_norm_ffn,
        sum_router,
        part_in,
        part_out,
        sum_shared_in,
        sum_shared_out.T,
    )


def solution(mesh):
    dp, experts = mesh.shape["dp"], mesh.shape["expert"]
    finer = Mesh(mesh.devices.reshape(4, dp // 4, experts // 2, 2), ("g", "r", "y", "c"))
    whole = P()
    return jax.shard_map(
        local,
        mesh=finer,
        in_specs=(
            P(EX, DP, None),
            whole,
            whole,
            whole,
            whole,
            whole,
            P(None, EX, None),
            P(None, EX, None),
            whole,
            whole,
            P(EX, None),
            P(EX, DP, None),
            P(EX, DP, None),
        ),
        out_specs=(
            P(EX, DP, None),
            P(EX, DP, None),
            P(DP),
            P(DP, EX),
            P(DP, EX),
            P(DP),
            P(DP, EX),
            P(DP, EX, None),
            P(DP, EX, None),
            P(DP, EX),
            P(DP, EX),
        ),
        check_vma=False,
    )
```

```python
import functools

import jax
import jax.numpy as jnp
from jax import lax
from jax.experimental import pallas as pl
from jax.experimental.pallas import tpu as pltpu
from jax.sharding import Mesh
from jax.sharding import PartitionSpec as P

HEADS = 12
HEAD_DIM = 64
TOP = 2
EPS = 1e-06
NEG = -1e30
F32 = jnp.float32
BF16 = jnp.bfloat16
STEPS = 8
DP = ("g", "r")
EX = ("y", "c")
LEADS = ("g", "g")
VMEM = 56 * 1024 * 1024


def takes(microseconds):
    return pl.CostEstimate(
        flops=int(microseconds * 1.15e9), bytes_accessed=1024, transcendentals=0
    )


def rope_table(positions):
    lane = jnp.arange(2 * HEAD_DIM, dtype=jnp.int32) % HEAD_DIM
    half_dim = HEAD_DIM // 2
    frequency = 10000.0 ** (-(lane % half_dim).astype(F32) * 2.0 / HEAD_DIM)
    angles = positions.astype(F32)[:, None] * frequency[None, :]
    return jnp.cos(angles), jnp.sin(angles) * jnp.where(lane < half_dim, -1.0, 1.0)


def rms_scale(hidden):
    return lax.rsqrt(jnp.mean(hidden * hidden, axis=-1, keepdims=True) + EPS)


def rms_back(hidden, scale_rows, gain_vector, upstream):
    normed_grad = upstream * gain_vector
    inner_mean = jnp.mean(normed_grad * hidden, axis=-1, keepdims=True)
    return scale_rows * normed_grad - hidden * scale_rows**3 * inner_mean


class Place:
    def __init__(self):
        self.groups, self.lanes = lax.axis_size("g"), lax.axis_size("r")
        self.rows_y = lax.axis_size("y")
        self.dp = self.groups * self.lanes
        self.experts = self.rows_y * 2
        self.g, self.r = lax.axis_index("g"), lax.axis_index("r")
        self.y, self.c = lax.axis_index("y"), lax.axis_index("c")
        self.low, self.high = self.g % 2, self.g // 2

    def own(self, b):
        g, r = b // self.lanes, b % self.lanes
        low, high = g % 2, g // 2
        if self.lanes == 2:
            return r ^ self.r, low * 2 + high
        return low ^ self.low, high * self.lanes + r

    def flat(self, b):
        g, r = b // self.lanes, b % self.lanes
        if self.lanes == 2:
            return r * 4 + (g % 2) * 2 + g // 2
        return (g % 2 * 2 + g // 2) * self.lanes + r

    def expert_table(self, width, lead):
        sub = STEPS // 4
        order = []
        for pos in range(STEPS):
            half, rest = pos // 4, pos % 4
            if self.lanes == 2 and lead == "r":
                low, high, part = rest // 2, rest % 2, half ^ self.r
            elif self.lanes == 2:
                low, high, part = half ^ self.low, rest % 2, rest // 2
            else:
                low, high, part = half ^ self.low, rest // 2, rest % 2
            order.append((high * 2 + low) * sub + part)
        block = width // self.dp
        rows = []
        for b in range(self.dp):
            half, rest = self.own(b)
            rows.append(half * (width // 2) + rest * block)
        return jnp.stack([jnp.asarray(v, jnp.int32) for v in order + [0] * STEPS + rows])

    def shared_table(self, width):
        per = 16 // self.experts
        order, columns = [], []
        sub = STEPS // 4
        for pos in range(STEPS):
            half, rest = pos // 4, pos % 4
            j = (rest // per * 2 + (half ^ self.c)) * per + rest % per
            order.append(j)
            g, part = j // sub, j % sub
            if self.lanes == 2:
                columns.append(part * 4 + g % 2 * 2 + g // 2)
            else:
                columns.append((g % 2 * 2 + g // 2) * sub + part)
        block = width // self.dp
        rows = [self.flat(b) * block for b in range(self.dp)]
        own = width // self.experts
        turned = [
            (e % 2 ^ self.c) * (width // 2) + e // 2 * own for e in range(self.experts)
        ]
        return jnp.stack(
            [jnp.asarray(v, jnp.int32) for v in order + columns + rows + turned]
        )


def nt(a, b):
    return lax.dot_general(a, b, (((1,), (1,)), ((), ())), preferred_element_type=F32)


def nn(a, b):
    return lax.dot_general(a, b, (((1,), (0,)), ((), ())), preferred_element_type=F32)


def turn(x, cosine, sine):
    width = x.shape[1]
    lane = lax.broadcasted_iota(jnp.int32, x.shape, 1) % HEAD_DIM
    other = jnp.where(
        lane < HEAD_DIM // 2,
        pltpu.roll(x, width - HEAD_DIM // 2, 1),
        pltpu.roll(x, HEAD_DIM // 2, 1),
    )
    times = width // cosine.shape[1]
    cosine = jnp.concatenate([cosine] * times, axis=1)
    sine = jnp.concatenate([sine] * times, axis=1)
    return x * cosine + other * sine


def project_kernel(here, x_ref, gain_ref, w_ref, cos_ref, sin_ref, normed_ref, *refs):
    step = pl.program_id(0)
    groups = (len(refs) - 2) // 2
    q_refs, kv_refs, (q_all, kv_all) = refs[:groups], refs[groups:-2], refs[-2:]
    half, three = x_ref.shape[0] // 2, 3 * HEAD_DIM

    @pl.when(step == 0)
    def _():
        x = x_ref[...].astype(F32)
        normed_ref[...] = (x * rms_scale(x) * gain_ref[...]).astype(BF16)

    part = nn(normed_ref[...], w_ref[...])

    @pl.when(step == 0)
    def _():
        pack_heads(turn(part, cos_ref[...], sin_ref[...]) * HEAD_DIM**-0.5, q_all)

    @pl.when(step == 1)
    def _():
        k = turn(part, cos_ref[...], sin_ref[...])
        for g in range(groups):
            own = k[:, g * three : (g + 1) * three].astype(BF16)
            kv_all[g, :, 0:128] = own[:, :128]
            kv_all[g, :, 256:320] = own[:, 128:]

    @pl.when(step == 2)
    def _():
        for g in range(groups):
            own = part[:, g * three : (g + 1) * three].astype(BF16)
            kv_all[g, :, 128:256] = own[:, :128]
            kv_all[g, :, 320:384] = own[:, 128:]
        for d in range(groups):
            q_refs[d][...] = q_all[here[0] ^ d]
            kv_refs[d][...] = kv_all[here[0] ^ d]


def pack_heads(rows, packed_ref):
    half, three = rows.shape[0] // 2, 3 * HEAD_DIM
    for g in range(packed_ref.shape[0]):
        own = rows[:, g * three : (g + 1) * three].astype(BF16)
        packed_ref[g, :, 0:128] = own[:half, :128]
        packed_ref[g, :, 128:256] = own[half:, :128]
        packed_ref[g, :, 256:320] = own[:half, 128:]
        packed_ref[g, :, 320:384] = own[half:, 128:]


def project(place, x, gain, weight, cosine, sine):
    rows, width = x.shape
    groups = place.groups
    sds = jax.ShapeDtypeStruct
    whole = lambda *shape: pl.BlockSpec(shape, lambda i, t: (0,) * len(shape))
    normed, *parts = pl.pallas_call(
        project_kernel,
        out_shape=(sds((rows, width), BF16),)
        + (sds((rows // 2, 384), BF16),) * groups
        + (sds((rows, 384), BF16),) * groups,
        grid_spec=pltpu.PrefetchScalarGridSpec(
            num_scalar_prefetch=1,
            grid=(3,),
            in_specs=[
                whole(rows, width),
                whole(1, width),
                pl.BlockSpec((width, width), lambda i, t: (0, i)),
                whole(rows, 128),
                whole(rows, 128),
            ],
            out_specs=(whole(rows, width),)
            + (whole(rows // 2, 384),) * groups
            + (whole(rows, 384),) * groups,
            scratch_shapes=[
                pltpu.VMEM((groups, rows // 2, 384), BF16),
                pltpu.VMEM((groups, rows, 384), BF16),
            ],
        ),
        compiler_params=pltpu.CompilerParams(vmem_limit_bytes=VMEM),
        cost_estimate=takes(4),
    )(place.g[None], x, gain[None], weight, cosine, sine)
    return normed, parts[:groups], parts[groups:]


def unpack(packed, second_low):
    half = packed.shape[0]
    x = packed.astype(F32)
    lane = lax.broadcasted_iota(jnp.int32, (half, 128), 1)
    low = lane < HEAD_DIM
    first, second, third = x[:, 0:128], x[:, 128:256], x[:, 256:384]
    turned = pltpu.roll(third, HEAD_DIM, 1)
    zero = jnp.zeros_like(third)
    pair = [
        jnp.where(low, first, zero),
        jnp.where(low, second, zero),
        jnp.where(low, zero, first),
        jnp.where(low, zero, second),
    ]
    if second_low:
        single = [jnp.where(low, third, zero), jnp.where(low, turned, zero)]
    else:
        single = [jnp.where(low, zero, turned), jnp.where(low, zero, third)]
    return (
        jnp.concatenate(pair, axis=0).astype(BF16),
        jnp.concatenate(single, axis=0).astype(BF16),
    )


def visible_keys(kz, source, lanes, rows, limit):
    first = (kz * lanes + source) * rows
    place = first + lax.broadcasted_iota(jnp.int32, (rows, limit.shape[1]), 0)
    return place < limit


def attend_kernel(sources, shards, lanes, info, limit_ref, *refs):
    q_refs, kv_refs = refs[:shards], refs[shards : shards * (1 + sources)]
    out_refs, (lse_ref, q_ref, kv_all, turned, out_ref) = refs[shards * (1 + sources) : -5], refs[-5:]
    half = q_ref.shape[1]
    rows = 2 * half
    gather_heads(info, q_refs, q_ref)
    gather_keys(info, shards, kv_refs, kv_all, turned)

    def shard(z, carry):
        pair, single = unpack(q_ref[z], True)
        limit = limit_ref[z]

        def step(kz, state):
            largest, total, acc_pair, acc_single = state
            scores = []
            for s in range(sources):
                keep = visible_keys(kz, info[1 + shards + s], lanes, rows, limit)
                two = nt(kv_all[s, kz, :, 0:128], pair)
                one = nt(kv_all[s, kz, :, 256:384], single)
                both = jnp.concatenate([two, one], axis=1)
                keep = jnp.concatenate([keep] * 3, axis=1)
                scores.append(jnp.where(keep, both, NEG))
            newest = largest
            for sc in scores:
                newest = jnp.maximum(newest, jnp.max(sc, axis=0, keepdims=True))
            fade = jnp.exp(largest - newest)
            total = total * fade
            acc_pair = acc_pair * fade[:, : 2 * rows]
            acc_single = acc_single * fade[:, 2 * rows :]
            for s, sc in enumerate(scores):
                power = jnp.exp(sc - newest)
                total = total + jnp.sum(power, axis=0, keepdims=True)
                power = power.astype(BF16)
                acc_pair = acc_pair + nn(turned[s, kz, 128:256, :], power[:, : 2 * rows])
                acc_single = acc_single + nn(turned[s, kz, 256:384, :], power[:, 2 * rows :])
            return newest, total, acc_pair, acc_single

        largest, total, acc_pair, acc_single = lax.fori_loop(
            0,
            info[1 + z],
            step,
            (
                jnp.full((1, 3 * rows), NEG, F32),
                jnp.zeros((1, 3 * rows), F32),
                jnp.zeros((128, 2 * rows), F32),
                jnp.zeros((128, rows), F32),
            ),
        )
        lse_ref[z] = largest + jnp.log(total)
        share = 1.0 / total
        first = acc_pair[:HEAD_DIM, :rows] * share[:, :rows]
        second = acc_pair[HEAD_DIM:, rows:] * share[:, rows : 2 * rows]
        third = acc_single[HEAD_DIM:] * share[:, 2 * rows :]
        packed = jnp.concatenate(
            [a[:, part] for part in (slice(0, half), slice(half, rows)) for a in (first, second)]
            + [third[:, :half], third[:, half:]],
            axis=0,
        )
        out_ref[z] = packed.T.astype(BF16)
        return carry

    lax.fori_loop(0, shards, shard, 0)


    for d in range(shards):
        out_refs[d][...] = out_ref[info[0] ^ d]


def gather_heads(info, refs, packed_ref):
    for d, ref in enumerate(refs):
        packed_ref[info[0] ^ d] = ref[...]


def gather_keys(info, shards, refs, kv_all, turned):
    for i, ref in enumerate(refs):
        at = info[0] ^ (i % shards)
        kv_all[i // shards, at] = ref[...]
        turned[i // shards, at] = ref[...].astype(F32).T.astype(BF16)


def attend(place, info, limit, qs, kvs):
    half, lanes = qs[0].shape
    shards, sources = len(qs), len(kvs) // len(qs)
    vmem = pl.BlockSpec(memory_space=pltpu.VMEM)
    sds = jax.ShapeDtypeStruct
    *outs, lse = pl.pallas_call(
        functools.partial(attend_kernel, sources, shards, place.lanes),
        out_shape=(sds((half, lanes), BF16),) * shards + (sds((shards, 1, 6 * half), F32),),
        in_specs=[pl.BlockSpec(memory_space=pltpu.SMEM)] + [vmem] * (1 + shards * (1 + sources)),
        out_specs=(vmem,) * (shards + 1),
        scratch_shapes=[
            pltpu.VMEM((shards, half, lanes), BF16),
            pltpu.VMEM((sources, shards, 2 * half, lanes), BF16),
            pltpu.VMEM((sources, shards, lanes, 2 * half), BF16),
            pltpu.VMEM((shards, half, lanes), BF16),
        ],
        compiler_params=pltpu.CompilerParams(vmem_limit_bytes=VMEM),
        cost_estimate=takes(12),
    )(info, limit, *qs, *kvs)
    return outs, lse


def attend_back_kernel(sources, shards, lanes, info, limit_ref, lse_ref, *refs):
    q_refs, o_refs, g_refs = (refs[i * shards : (i + 1) * shards] for i in range(3))
    kv_refs = refs[3 * shards : (3 + sources) * shards]
    dq_refs = refs[(3 + sources) * shards : (4 + sources) * shards]
    dkv_refs = refs[(4 + sources) * shards : (4 + sources) * shards + sources]
    q_ref, out_ref, grad_ref, dq_ref, kv_all, turned, total = refs[-7:]
    half = q_ref.shape[1]
    rows = 2 * half
    gather_heads(info, q_refs, q_ref)
    gather_heads(info, o_refs, out_ref)
    gather_heads(info, g_refs, grad_ref)
    gather_keys(info, shards, kv_refs, kv_all, turned)
    total[...] = jnp.zeros_like(total)

    def shard(z, carry):
        pair, single = unpack(q_ref[z], True)
        grad_pair, grad_single = unpack(grad_ref[z], False)
        limit, lse = limit_ref[z], lse_ref[z]
        product = (grad_ref[z].astype(F32) * out_ref[z].astype(F32)).T
        sums = [
            jnp.sum(product[i * HEAD_DIM : (i + 1) * HEAD_DIM], axis=0, keepdims=True)
            for i in range(6)
        ]
        delta = jnp.concatenate([sums[0], sums[2], sums[1], sums[3], sums[4], sums[5]], axis=1)

        def step(kz, state):
            dq_pair, dq_single = state
            for s in range(sources):
                keep = visible_keys(kz, info[1 + shards + s], lanes, rows, limit)
                keep = jnp.concatenate([keep] * 3, axis=1)
                k01, v01 = kv_all[s, kz, :, 0:128], kv_all[s, kz, :, 128:256]
                kv2 = kv_all[s, kz, :, 256:384]
                scores = jnp.concatenate([nt(k01, pair), nt(kv2, single)], axis=1)
                grads = jnp.concatenate([nt(v01, grad_pair), nt(kv2, grad_single)], axis=1)
                power = jnp.where(keep, jnp.exp(scores - lse), 0.0)
                slope = (power * (grads - delta)).astype(BF16)
                power = power.astype(BF16)
                dq_pair = dq_pair + nn(turned[s, kz, 0:128, :], slope[:, : 2 * rows])
                dq_single = dq_single + nn(turned[s, kz, 256:384, :], slope[:, 2 * rows :])
                total[s, kz, :, 0:128] += nn(slope[:, : 2 * rows], pair)
                total[s, kz, :, 128:256] += nn(power[:, : 2 * rows], grad_pair)
                total[s, kz, :, 256:384] += nn(slope[:, 2 * rows :], single) + nn(
                    power[:, 2 * rows :], grad_single
                )
            return dq_pair, dq_single

        dq_pair, dq_single = lax.fori_loop(
            0,
            info[1 + z],
            step,
            (jnp.zeros((128, 2 * rows), F32), jnp.zeros((128, rows), F32)),
        )
        first, second = dq_pair[:HEAD_DIM, :rows], dq_pair[HEAD_DIM:, rows:]
        third = dq_single[:HEAD_DIM]
        packed = jnp.concatenate(
            [a[:, part] for part in (slice(0, half), slice(half, rows)) for a in (first, second)]
            + [third[:, :half], third[:, half:]],
            axis=0,
        )
        dq_ref[z] = packed.T.astype(BF16)
        return carry

    lax.fori_loop(0, shards, shard, 0)
    for d in range(shards):
        dq_refs[d][...] = dq_ref[info[0] ^ d]
    for s, ref in enumerate(dkv_refs):
        for d in range(shards):
            ref[d] = total[s, info[0] ^ d].astype(BF16)


def attend_back(place, info, limit, lse, qs, outs, grads, kvs):
    half, lanes = qs[0].shape
    shards, sources = len(qs), len(kvs) // len(qs)
    vmem = pl.BlockSpec(memory_space=pltpu.VMEM)
    sds = jax.ShapeDtypeStruct
    parts = pl.pallas_call(
        functools.partial(attend_back_kernel, sources, shards, place.lanes),
        out_shape=(sds((half, lanes), BF16),) * shards
        + (sds((shards, 2 * half, lanes), BF16),) * sources,
        in_specs=[pl.BlockSpec(memory_space=pltpu.SMEM)] + [vmem] * (2 + shards * (3 + sources)),
        out_specs=(vmem,) * (shards + sources),
        scratch_shapes=[pltpu.VMEM((shards, half, lanes), BF16)] * 4
        + [
            pltpu.VMEM((sources, shards, 2 * half, lanes), BF16),
            pltpu.VMEM((sources, shards, lanes, 2 * half), BF16),
            pltpu.VMEM((sources, shards, 2 * half, lanes), F32),
        ],
        compiler_params=pltpu.CompilerParams(vmem_limit_bytes=VMEM),
        cost_estimate=takes(19),
    )(info, limit, lse, *qs, *outs, *grads, *kvs)
    return list(parts[:shards]), parts[shards:]


def finish_kernel(
    here, w_ref, cos_ref, sin_ref, x_ref, gain_ref, middle_ref, *refs,
):
    groups = (len(refs) - 6) // 2
    dq_refs, dkv_refs = refs[:groups], refs[groups : 2 * groups]
    projected_ref, input_ref, norm_ref, dq_all, dkv_all, gather = refs[2 * groups :]
    rows, width = x_ref.shape
    half, three = rows // 2, 3 * HEAD_DIM
    for d in range(groups):
        dq_all[here[0] ^ d] = dq_refs[d][...].astype(F32)
        dkv_all[here[0] ^ d] = dkv_refs[d][...].astype(F32)
    for g in range(groups):
        at = g * three
        dq, dkv = dq_all[g], dkv_all[g]
        gather[0, :half, at : at + 128] = dq[:, 0:128]
        gather[0, half:, at : at + 128] = dq[:, 128:256]
        gather[0, :half, at + 128 : at + three] = dq[:, 256:320]
        gather[0, half:, at + 128 : at + three] = dq[:, 320:384]
        gather[1, :, at : at + 128] = dkv[:, 0:128]
        gather[1, :, at + 128 : at + three] = dkv[:, 256:320]
        gather[2, :, at : at + 128] = dkv[:, 128:256]
        gather[2, :, at + 128 : at + three] = dkv[:, 320:384]
    cosine, sine = cos_ref[...], -sin_ref[...]
    parts = [
        (turn(gather[0], cosine, sine) * HEAD_DIM**-0.5).astype(BF16),
        turn(gather[1], cosine, sine).astype(BF16),
        gather[2].astype(BF16),
    ]
    grad = jnp.zeros((rows, width), F32)
    for i, part in enumerate(parts):
        projected_ref[:, i * width : (i + 1) * width] = part
        grad = grad + nt(part, w_ref[:, i * width : (i + 1) * width])
    x = x_ref[...].astype(F32)
    scale = rms_scale(x)
    norm_ref[...] = jnp.sum(grad * x * scale, axis=0, keepdims=True)
    input_ref[...] = middle_ref[...] + rms_back(x, scale, gain_ref[...], grad)


def finish(place, dqs, dkvs, weight, cosine, sine, x, gain, middle):
    rows, width = x.shape
    groups = place.groups
    vmem = pl.BlockSpec(memory_space=pltpu.VMEM)
    return pl.pallas_call(
        finish_kernel,
        out_shape=(
            jax.ShapeDtypeStruct((rows, 3 * width), BF16),
            jax.ShapeDtypeStruct((rows, width), F32),
            jax.ShapeDtypeStruct((1, width), F32),
        ),
        in_specs=[pl.BlockSpec(memory_space=pltpu.SMEM)] + [vmem] * (6 + 2 * groups),
        out_specs=(vmem,) * 3,
        scratch_shapes=[
            pltpu.VMEM((groups, rows // 2, 384), F32),
            pltpu.VMEM((groups, rows, 384), F32),
            pltpu.VMEM((3, rows, width), F32),
        ],
        compiler_params=pltpu.CompilerParams(vmem_limit_bytes=VMEM),
        cost_estimate=takes(5),
    )(place.g[None], weight, cosine, sine, x, gain[None], middle, *dqs, *dkvs)


def middle_kernel(
    here, x_ref, grad_ref, w_ref, gain_ref, router_ref, pick0, pick1, seat0, seat1, *refs,
):
    groups = 4
    o_refs = refs[:groups]
    low_ref, middle_ref, mixed_ref, gate_ref = refs[groups : groups + 4]
    sent = refs[groups + 4 : -2]
    o_all, gather = refs[-2:]
    count = len(sent) // 2
    half, three = x_ref.shape[0] // 2, 3 * HEAD_DIM
    for d in range(groups):
        o_all[here[0] ^ d] = o_refs[d][...].astype(F32)
    for g in range(groups):
        at = g * three
        gather[:half, at : at + 128] = o_all[g, :, 0:128]
        gather[half:, at : at + 128] = o_all[g, :, 128:256]
        gather[:half, at + 128 : at + three] = o_all[g, :, 256:320]
        gather[half:, at + 128 : at + three] = o_all[g, :, 320:384]
    low = gather[...].astype(BF16)
    low_ref[...] = low
    middle = x_ref[...].astype(F32) + nn(low, w_ref[...])
    middle_ref[...] = middle
    mixed = (middle * rms_scale(middle) * gain_ref[...]).astype(BF16)
    mixed_ref[...] = mixed
    scores = nn(mixed, router_ref[...])
    picked = [jnp.sum(scores * p[...], axis=1, keepdims=True) for p in (pick0, pick1)]
    largest = jnp.maximum(*picked)
    powers = [jnp.exp(p - largest) for p in picked]
    gates = [p / (powers[0] + powers[1]) for p in powers]
    gate_ref[...] = jnp.concatenate(gates, axis=1)
    seats = (seat0[...], seat1[...])
    held = jnp.zeros((seats[0].shape[0], 1), F32)
    for seat, gate in zip(seats, gates):
        high = gate.astype(BF16)
        rest = (gate - high.astype(F32)).astype(BF16)
        held = held + jnp.sum(nn(seat, jnp.concatenate([high, rest], axis=1)), axis=1, keepdims=True)
    every = seats[0] + seats[1]
    rows = nn(every, mixed).astype(BF16)
    grads = (nn(every, grad_ref[...]) * held).astype(BF16)
    capacity = sent[0].shape[1]
    for d in range(count):
        for e in range(sent[0].shape[0]):
            at = (e * count + d) * capacity
            sent[d][e] = rows[at : at + capacity]
            sent[count + d][e] = grads[at : at + capacity]


def middle_part(place, capacity, outs, x, grad, weight, gain, router, picks, seats):
    rows, width = x.shape
    groups, count = place.groups, place.experts
    local = router.shape[1] // count
    vmem = pl.BlockSpec(memory_space=pltpu.VMEM)
    sds = jax.ShapeDtypeStruct
    low, middle, mixed, gates, *sent = pl.pallas_call(
        middle_kernel,
        out_shape=(
            sds((rows, width), BF16),
            sds((rows, width), F32),
            sds((rows, width), BF16),
            sds((rows, TOP), F32),
        )
        + (sds((local, capacity, width), BF16),) * (2 * count),
        in_specs=[pl.BlockSpec(memory_space=pltpu.SMEM)] + [vmem] * (9 + groups),
        out_specs=(vmem,) * (4 + 2 * count),
        scratch_shapes=[
            pltpu.VMEM((groups, rows // 2, 384), F32),
            pltpu.VMEM((rows, width), F32),
        ],
        compiler_params=pltpu.CompilerParams(vmem_limit_bytes=VMEM),
        cost_estimate=takes(4),
    )(place.g[None], x, grad, weight, gain[None], router, *picks, *seats, *outs)
    return low, middle, mixed, gates, sent[:count], sent[count:]


def trade(parts, axis):
    size = lax.axis_size(axis)
    return [parts[0]] + [
        lax.ppermute(parts[d], axis, [(i, i ^ d) for i in range(size)]) for d in range(1, size)
    ]


def ffn_kernel(shared, count, dp, experts, table, *refs):
    x_refs, dy_refs, (gate_ref, up_ref, down_ref) = refs[:count], refs[count : 2 * count], refs[2 * count : 2 * count + 3]
    refs = refs[2 * count + 3 :]
    if shared:
        result, back, in_keep, in_send, out_keep, out_send, stage, turned, turned_dy = refs
        x_ref, dy_ref = x_refs[0], dy_refs[0]
    else:
        both, refs = refs[:count], refs[count:]
        gate_keep, gate_send, up_keep, up_send, out_keep, out_send = refs[:6]
        in_keep, in_send = (gate_keep, up_keep), (gate_send, up_send)
        stage, turned, result, back, x_ref, dy_ref = refs[6:]
    step = pl.program_id(0)
    width = x_ref.shape[1]
    rows = x_ref.shape[0]

    @pl.when(step == 0)
    def _():
        if not shared:
            part = rows // count
            for d in range(count):
                x_ref[d * part : (d + 1) * part] = x_refs[d][0]
                dy_ref[d * part : (d + 1) * part] = dy_refs[d][0]
        whole = x_ref[...].astype(F32).T
        block = width // dp
        for b in range(dp):
            start = pl.multiple_of(table[2 * STEPS + b], 8)
            stage[pl.ds(start, block), :] = whole[b * block : (b + 1) * block]
        turned[...] = stage[...].astype(BF16)
        if shared:
            whole = dy_ref[...].astype(F32).T
            block = width // experts
            for e in range(experts):
                start = pl.multiple_of(table[2 * STEPS + dp + e], 8)
                stage[pl.ds(start, block), :] = whole[e * block : (e + 1) * block]
            turned_dy[...] = stage[...].astype(BF16)
        result[...] = jnp.zeros_like(result)
        back[...] = jnp.zeros_like(back)

    x, dy = x_ref[...], dy_ref[...]
    w_gate, w_up, w_down = gate_ref[0], up_ref[0], down_ref[0]
    gate, up = nn(x, w_gate), nn(x, w_up)
    grad = nt(dy, w_down)
    sig = jax.nn.sigmoid(gate)
    silu = gate * sig
    act = (silu * up).astype(BF16)
    grad_gate = (grad * up * (sig * (1.0 + gate * (1.0 - sig)))).astype(BF16)
    grad_up = (grad * silu).astype(BF16)
    result[...] += nn(act, w_down)
    back[...] += nt(grad_gate, w_gate) + nt(grad_up, w_up)
    xt = turned[...]
    half = width // 2
    for k, upper in enumerate((grad_gate, grad_up)):
        grad_in = nn(xt, upper).astype(BF16)
        if shared:

            @pl.when(step < STEPS // 2)
            def _():
                in_keep[k] = grad_in

            @pl.when(step >= STEPS // 2)
            def _():
                in_send[k] = grad_in

        else:
            in_keep[k][...] = grad_in[:half]
            in_send[k][...] = grad_in[half:]
    if shared:
        grad_out = nn(turned_dy[...], act).astype(BF16)
        out_keep[...] = grad_out[:half]
        out_send[...] = grad_out[half:]
    else:
        grad_out = lax.dot_general(
            act, dy, (((0,), (0,)), ((), ())), preferred_element_type=F32
        ).astype(BF16)

        @pl.when(step < STEPS // 2)
        def _():
            out_keep[...] = grad_out

        @pl.when(step >= STEPS // 2)
        def _():
            out_send[...] = grad_out

        @pl.when(step == STEPS - 1)
        def _():
            part = rows // count
            for d in range(count):
                both[d][:, :width] = result[d * part : (d + 1) * part].astype(BF16)
                both[d][:, width:] = back[d * part : (d + 1) * part].astype(BF16)


def ffn(shared, place, table, xs, dys, w_in, w_out, e):
    count = len(xs)
    part, width = xs[0].shape[-2:]
    rows = part * count
    if shared:
        given = pl.BlockSpec((rows, width), lambda i, t: (0, 0))
    else:
        given = pl.BlockSpec((1, part, width), lambda i, t: (e, 0, 0))
    hidden = w_out.shape[1]
    chunk = hidden // STEPS
    near, far = STEPS // 2 - 1, STEPS // 2
    sds = jax.ShapeDtypeStruct
    first = lambda i, t: (0, 0, jnp.minimum(i, near))
    second = lambda i, t: (0, 0, jnp.maximum(i - far, 0))
    if shared:
        out_shape = (
            sds((rows, width), F32),
            sds((rows, width), F32),
            sds((2, width, hidden // 2), BF16),
            sds((2, width, hidden // 2), BF16),
            sds((width // 2, hidden), BF16),
            sds((width // 2, hidden), BF16),
        )
        out_specs = (
            pl.BlockSpec((rows, width), lambda i, t: (0, 0)),
            pl.BlockSpec((rows, width), lambda i, t: (0, 0)),
            pl.BlockSpec((2, width, chunk), first),
            pl.BlockSpec((2, width, chunk), second),
            pl.BlockSpec((width // 2, chunk), lambda i, t: (0, t[STEPS + i])),
            pl.BlockSpec((width // 2, chunk), lambda i, t: (0, t[STEPS + i])),
        )
        extra = [pltpu.VMEM((width, rows), BF16)]
    else:
        out_shape = (
            *[sds((part, 2 * width), BF16)] * count,
            *[sds((width // 2, hidden), BF16)] * 4,
            sds((hidden // 2, width), BF16),
            sds((hidden // 2, width), BF16),
        )
        out_specs = (
            *[pl.BlockSpec((part, 2 * width), lambda i, t: (0, 0))] * count,
            *[pl.BlockSpec((width // 2, chunk), lambda i, t: (0, t[i]))] * 4,
            pl.BlockSpec((chunk, width), lambda i, t: (jnp.minimum(i, near), 0)),
            pl.BlockSpec((chunk, width), lambda i, t: (jnp.maximum(i - far, 0), 0)),
        )
        extra = [pltpu.VMEM((rows, width), F32)] * 2 + [pltpu.VMEM((rows, width), BF16)] * 2
    return pl.pallas_call(
        functools.partial(ffn_kernel, shared, count, place.dp, place.experts),
        out_shape=out_shape,
        grid_spec=pltpu.PrefetchScalarGridSpec(
            num_scalar_prefetch=1,
            grid=(STEPS,),
            in_specs=[
                *[given] * (2 * count),
                pl.BlockSpec((1, width, chunk), lambda i, t: (e, 0, t[i])),
                pl.BlockSpec((1, width, chunk), lambda i, t: (e, 0, STEPS + t[i])),
                pl.BlockSpec((1, chunk, width), lambda i, t: (e, t[i], 0)),
            ],
            out_specs=out_specs,
            scratch_shapes=[pltpu.VMEM((width, rows), F32), pltpu.VMEM((width, rows), BF16)]
            + extra,
        ),
        compiler_params=pltpu.CompilerParams(vmem_limit_bytes=VMEM),
        cost_estimate=takes(18),
    )(table, *xs, *dys, w_in, w_in, w_out)


def swap(a, axis, bit=1):
    size = lax.axis_size(axis)
    return lax.ppermute(a, axis, [(i, i ^ bit) for i in range(size)])


def add(a, b, kind=BF16):
    return (a.astype(F32) + b.astype(F32)).astype(kind)


def half_of(a, dim, index):
    size = a.shape[dim] // 2
    return lax.dynamic_slice_in_dim(a, index * size, size, dim)


def exchange(keep, came, dim, mine):
    return [add(half_of(keep, dim, i), half_of(came, dim, i)) for i in (mine, 1 - mine)]


def scatter(a, axis, dim):
    return lax.psum_scatter(a, axis, scatter_dimension=dim, tiled=True)


def reduce_experts(place, keep, send):
    came = swap(send, "g", 1)
    keep, send = exchange(keep, came, 0, place.high)
    return scatter(add(keep, swap(send, "g", 2)), "r", 0).astype(F32)


def after(x, *values):
    return lax.optimization_barrier((x, *values))[0]


def reduce_tokens(place, keep, came, dim):
    keep, send = exchange(keep, came, dim, place.low)
    came = swap(send, "g", 1)
    keep, send = exchange(keep, came, dim, place.high)
    came = swap(send, "g", 2)
    return scatter(add(keep, came), "r", dim).astype(F32)


def reduce_shared_in(place, keep, send):
    total = add(keep, swap(send, "c"))
    two, width, columns = total.shape
    parts = place.rows_y // 2
    total = total.reshape(two, width, parts, columns // parts).transpose(0, 2, 1, 3)
    mine = scatter(total.reshape(two * parts, width, columns // parts), "y", 0)[0]
    return reduce_tokens(place, mine, jnp.zeros_like(mine), 0)


def reduce_shared_out(place, keep, send):
    mine = scatter(add(keep, swap(send, "c")), "y", 0)
    return reduce_tokens(place, mine, jnp.zeros_like(mine), 1)


def to_flat(place, x):
    rows, width = x.shape
    x = x.reshape(rows, 2, 2, place.lanes, width // place.dp)
    order = (0, 3, 2, 1, 4) if place.lanes == 2 else (0, 2, 1, 3, 4)
    return x.transpose(order).reshape(rows, width)


def weight_grad(place, left, right, extra):
    rows, columns = right.shape
    width = left.shape[1]
    own = columns // place.experts
    parts = right.reshape(rows, place.rows_y, 2, own)
    extra = extra.reshape(width, place.rows_y, 2, extra.shape[-1]).astype(BF16)
    keep, send = [
        jnp.concatenate(
            [
                lax.dot_general(
                    left,
                    lax.dynamic_index_in_dim(parts, i, 2, False).reshape(rows, columns // 2),
                    (((0,), (0,)), ((), ())),
                    preferred_element_type=F32,
                )
                .astype(BF16)
                .reshape(width, place.rows_y, own),
                lax.dynamic_index_in_dim(extra, i, 2, False),
            ],
            axis=2,
        ).transpose(1, 0, 2)
        for i in (place.c, 1 - place.c)
    ]
    return keep, send


def reduce_weight(place, keep, send):
    mine = scatter(add(keep, swap(send, "c")), "y", 0)[0]
    return reduce_tokens(place, mine, jnp.zeros_like(mine), 0)


def in_two(vector):
    high = vector.astype(BF16).astype(F32)
    return [high, vector - high]


def beside(place, columns, experts_of):
    width = columns[0].shape[0]
    every = jnp.stack(columns, axis=1)[:, None, :]
    every = jnp.broadcast_to(every, (width, place.experts, len(columns)))
    parts = [every] if experts_of is None else [every, experts_of]
    used = sum(p.shape[2] for p in parts)
    return jnp.concatenate(parts + [jnp.zeros((width, place.experts, 64 - used), F32)], axis=2)


def combine_kernel(
    here, hot0, hot1, gate_ref, pick0, pick1, grad_ref, middle_ref,
    shared_ref, back_ref, mixed_in_ref, router_ref, gain_ref, w_ref, *refs,
):
    output_ref, middle_grad_ref, low_ref, *head_refs = refs[-11:-4]
    norm_ref, router_grad_ref, returned, heads = refs[-4:]
    ret_refs = refs[:-11]
    width = grad_ref.shape[1]
    part = ret_refs[0].shape[0]
    for i, ref in enumerate(ret_refs):
        returned[i * part : (i + 1) * part] = ref[...]
    hots = (hot0[...], hot1[...])
    grad = grad_ref[...].astype(F32)
    middle = middle_ref[...]
    backs = [nn(h, returned[:, :width]) for h in hots]
    gates = [gate_ref[:, k : k + 1] for k in range(TOP)]
    routed = sum(gates[k] * backs[k] for k in range(TOP))
    output_ref[...] = (middle + routed + shared_ref[...]).astype(BF16)
    slopes = [jnp.sum(b * grad, axis=1, keepdims=True) for b in backs]
    inner = sum(gates[k] * slopes[k] for k in range(TOP))
    logits = sum(
        pick[...] * (gates[k] * (slopes[k] - inner)) for k, pick in enumerate((pick0, pick1))
    ).astype(BF16)
    router_grad_ref[...] = lax.dot_general(
        logits, mixed_in_ref[...], (((0,), (0,)), ((), ())), preferred_element_type=F32
    )
    mixed = back_ref[...] + nn(logits, router_ref[...]) + nn(hots[0] + hots[1], returned[:, width:])
    scale = rms_scale(middle)
    norm_ref[...] = jnp.sum(mixed * middle * scale, axis=0, keepdims=True)
    middle_grad = grad + rms_back(middle, scale, gain_ref[...], mixed)
    middle_grad_ref[...] = middle_grad
    low = middle_grad.astype(BF16)
    low_ref[...] = low
    pack_heads(nt(low, w_ref[...]), heads)
    for d, ref in enumerate(head_refs):
        ref[...] = heads[here[0] ^ d]


def combine(place, hots, rets, gates, picks, grad, middle, shared, back, mixed_in, router, gain, weight):
    rows, width = grad.shape
    vmem = pl.BlockSpec(memory_space=pltpu.VMEM)
    sds = jax.ShapeDtypeStruct
    output, middle_grad, low, *heads, norm, router_grad = pl.pallas_call(
        combine_kernel,
        out_shape=(
            sds((rows, width), BF16),
            sds((rows, width), F32),
            sds((rows, width), BF16),
        )
        + (sds((rows // 2, 384), BF16),) * place.groups
        + (
            sds((1, width), F32),
            sds((router.shape[1], width), F32),
        ),
        in_specs=[pl.BlockSpec(memory_space=pltpu.SMEM)] + [vmem] * (13 + len(rets)),
        out_specs=(vmem,) * (5 + place.groups),
        scratch_shapes=[
            pltpu.VMEM((hots[0].shape[1], 2 * width), BF16),
            pltpu.VMEM((place.groups, rows // 2, 384), BF16),
        ],
        compiler_params=pltpu.CompilerParams(vmem_limit_bytes=VMEM),
        cost_estimate=takes(5),
    )(
        place.g[None], *hots, gates, *picks, grad, middle, shared, back, mixed_in,
        router.T, gain[None], weight, *rets,
    )
    return output, middle_grad, low, heads, norm, router_grad


class Sum:
    def __init__(self, keep, send, stages):
        self.keep, self.send, self.stages, self.came = keep, send, list(stages), None

    def begin(self, *behind):
        axis, bit, *self.split = self.stages.pop(0)
        send = after(self.send, *behind) if behind else self.send
        self.came = self.came_last = swap(send, axis, bit)
        return self

    def end(self, *until):
        dim, mine = self.split
        came = after(self.came, *until) if until else self.came
        if dim is None:
            self.keep = add(self.keep, came, F32)
        else:
            self.keep, self.send = exchange(self.keep, came, dim, mine)
        self.came = None
        return self

    def finish(self):
        if self.came is not None:
            self.end()
        while self.stages:
            self.begin().end()
        return self.keep


def expert_sum(place, keep, send, lead):
    if lead == "r":
        near = [("r", 1, 0, place.low), ("g", 1, 0, place.high)]
    else:
        near = [("g", 1, 0, place.r), ("r", 1, 0, place.high)]
    return Sum(keep, send, near + [("g", 2, None, None)])


def every_sum(place, keep, send, dim):
    return Sum(
        keep,
        send,
        [
            ("c", 1, 0, place.y),
            ("y", 1, dim, place.r),
            ("r", 1, dim, place.low),
            ("g", 1, dim, place.high),
            ("g", 2, None, None),
        ],
    )


def local(
    tokens,
    norm_attn,
    query_key_value_weight,
    attention_output_weight,
    norm_ffn,
    router,
    expert_in,
    expert_out,
    shared_gate_up_weight,
    shared_down_weight,
    block_lengths,
    routes,
    cotangent,
):
    place = Place()
    fast = place.lanes == 2 and place.rows_y == 2
    _, row_count, model_width = tokens.shape
    shard_index = lax.axis_index(DP)
    length = row_count * place.dp
    positions = shard_index * row_count + jnp.arange(row_count, dtype=jnp.int32)
    bounds = jnp.cumsum(block_lengths[0])
    cosine, sine = rope_table(positions)
    experts_total = router.shape[1]
    local_experts = expert_in.shape[1]
    groups = place.experts
    capacity = row_count * TOP * 5 // (4 * experts_total)
    chosen = routes[0]
    column = jnp.arange(experts_total, dtype=jnp.int32)
    picks = [(chosen[:, k : k + 1] == column[None, :]).astype(F32) for k in range(TOP)]
    flat_routes = chosen.reshape(row_count * TOP)
    route_hot = (flat_routes[:, None] == column[None, :]).astype(jnp.int32)
    earlier = jnp.cumsum(route_hot, axis=0) - route_hot
    slot_index = jnp.sum(earlier * route_hot, axis=1)
    partner = (flat_routes // local_experts) ^ lax.axis_index(EX)
    target = jnp.where(
        slot_index < capacity,
        (flat_routes % local_experts * groups + partner) * capacity + slot_index,
        -1,
    ).reshape(row_count, TOP)
    seats = jnp.arange(experts_total * capacity, dtype=jnp.int32)
    hots = [(target[:, k : k + 1] == seats[None, :]).astype(BF16) for k in range(TOP)]
    seated = [(target[:, k][None, :] == seats[:, None]).astype(BF16) for k in range(TOP)]
    upstream = cotangent[0]

    normalized_rows, own_q, own_kv = project(
        place, tokens[0], norm_attn, query_key_value_weight, cosine, sine
    )
    kv = trade(own_kv, "g")
    q = trade(own_q, "g")
    if fast:
        kvs = kv + [swap(a, "r") for a in kv]
        lanes_of = [place.r, 1 - place.r]
    else:
        every_kv = [lax.all_gather(a, "r", axis=0, tiled=False) for a in kv]
        kvs = [a[i] for i in range(place.lanes) for a in every_kv]
        lanes_of = [jnp.int32(i) for i in range(place.lanes)]
    starts = (jnp.arange(place.groups, dtype=jnp.int32) * place.lanes + place.r) * row_count
    query_places = starts[:, None] + jnp.arange(row_count, dtype=jnp.int32)[None, :]
    limit = jnp.min(
        jnp.where(bounds[None, None, :] > query_places[:, :, None], bounds, length), axis=-1
    )
    span = row_count * place.lanes
    info = jnp.concatenate(
        [place.g[None], (jnp.max(limit, axis=1) + span - 1) // span, jnp.stack(lanes_of)]
    ).astype(jnp.int32)
    limit = limit[:, None, :]
    expert_in, expert_out, *_ = lax.optimization_barrier((expert_in, expert_out, *kv[1:]))
    expert_in = jnp.transpose(expert_in, (1, 0, 2))
    expert_out = jnp.transpose(expert_out, (1, 0, 2))
    tables = [place.expert_table(model_width, lead) for lead in LEADS]
    shared_order = place.shared_table(model_width)
    q[0], *tables = lax.optimization_barrier((q[0], *tables, shared_order, expert_in, expert_out))
    *tables, shared_order, expert_in, expert_out = tables
    own_out, lse = attend(place, info, limit, q, kvs)
    attended_low, middle, mixed_in, gates, send_rows, send_grads = middle_part(
        place,
        capacity,
        trade(own_out, "g"),
        tokens[0],
        upstream,
        attention_output_weight,
        norm_ffn,
        router,
        picks,
        seated,
    )
    arrived = trade(send_rows, EX)
    grad_arrived = trade(send_grads, EX)
    shared_result, shared_back, *shared_grads = ffn(
        True,
        place,
        shared_order,
        [mixed_in],
        [upstream],
        shared_gate_up_weight[None],
        shared_down_weight[None],
        0,
    )
    came_back, parts = [], []
    behind = [shared_result]
    if fast:
        shared_in = every_sum(place, *shared_grads[:2], 1)
        shared_out = every_sum(place, *shared_grads[2:], 1)
    for e in range(local_experts):
        own = [after(arrived[0], *behind)] + arrived[1:]
        results = ffn(
            False,
            place,
            tables[e],
            own,
            grad_arrived,
            expert_in,
            expert_out,
            e,
        )
        behind = [results[0]]
        came_back.append(trade(results[:groups], EX))
        parts.append(results[groups:])
    rets = [a for back in came_back for a in back]
    if fast:
        sums = [
            [expert_sum(place, *parts[e][k : k + 2], "r") for k in (0, 2)]
            + [expert_sum(place, *parts[e][4:], LEADS[e])]
            for e in range(local_experts)
        ]
        (first, second, third), (fourth, fifth, sixth) = sums
        both_done = parts[-1][0]
        first.begin()
        third.begin()
        second.begin(both_done)
        sixth.begin(both_done)
        shared_out.begin().end(both_done)
        shared_in.begin().end(both_done)
        first.end(both_done)
        third.end(both_done)
        shared_out.begin(rets[-1])
        shared_in.begin(rets[-1])
        rets[-1] = after(rets[-1], first.keep, third.keep, shared_in.keep, shared_out.keep)
    output, grad_middle, grad_attn_low, own_grad, grad_norm_ffn, grad_router = combine(
        place,
        hots,
        rets,
        gates,
        picks,
        upstream,
        middle,
        shared_result,
        shared_back,
        mixed_in,
        router,
        norm_ffn,
        attention_output_weight,
    )
    flat = lambda x: to_flat(place, x)
    own_grad = trade(own_grad, "g")
    if fast:
        third.begin()
        first.begin(own_grad[1])
        sixth.end(grad_middle).begin()
        own_grad[0] = after(own_grad[0], second.came, sixth.keep, shared_out.came)
    own_dq, own_dkv = attend_back(place, info, limit, lse, q, own_out, own_grad, kvs)
    dq = trade(own_dq, "g")
    grad_attn_low, own_dq[0] = lax.optimization_barrier((grad_attn_low, own_dq[0]))
    extra = beside(
        place,
        in_two(flat(grad_norm_ffn)[0]),
        flat(grad_router).T.reshape(model_width, groups, local_experts),
    )
    sides_out = weight_grad(place, flat(attended_low), grad_attn_low, extra)
    if fast:
        went_back = own_dkv[0]
        came = swap(after(own_dkv[1], first.came), "r")
        first.end(went_back).begin(dq[2], dq[3])
        third.end(went_back)
        second.end(went_back)
        sixth.end(went_back)
        came = after(came, second.send, sixth.send, third.send, first.came, *dq[1:])
        fourth.begin(came)
        fifth.begin(came)
        dkv = [add(own_dkv[0][d], came[d]) for d in range(place.groups)]
    else:
        dkv = [
            scatter(jnp.stack([a[d] for a in own_dkv]), "r", 0)[0] for d in range(place.groups)
        ]
    dkv = trade(dkv, "g")
    if fast:
        sum_out = every_sum(place, *sides_out, 1).begin()
        second.begin(dkv[1])
        sixth.begin(dkv[1])
        third.begin(dkv[1])
        dkv[0] = after(dkv[0], fourth.came, shared_in.came, sum_out.came)
    grad_projected, grad_input, grad_norm_attn = finish(
        place,
        dq,
        dkv,
        query_key_value_weight,
        cosine,
        sine,
        tokens[0],
        norm_attn,
        grad_middle,
    )
    extra = beside(place, in_two(flat(grad_norm_attn)[0]), None)
    right = grad_projected
    if fast:
        fourth.end(grad_projected).begin()
        shared_in.end(grad_projected)
        shared_out.end(grad_projected)
        sum_out.end(grad_projected).begin()
        right = after(
            grad_projected, fifth.came, fourth.send, shared_in.send, shared_out.send, sum_out.came,
            second.came, sixth.came,
        )
    sides_qkv = weight_grad(place, flat(normalized_rows), right, extra)
    if fast:
        sum_qkv = every_sum(place, *sides_qkv, 1).begin()
        shared_in.begin()
        shared_out.begin(shared_in.send)
        sum_out.end(right).begin()
        fifth.end(right).begin()
        second.end(right).begin()
        sum_qkv.end(right, fourth.came).begin()
        fourth.end(sum_qkv.send).begin()
        for chunk in (first, third, sixth):
            chunk.end(sum_qkv.send)
        sum_out.end(sum_qkv.send).begin()
        sum_qkv.end(shared_in.came).begin(shared_out.came, sum_out.came)
        for chunk in (fifth, shared_in, shared_out, sum_out):
            chunk.end(sum_qkv.send).begin()
        for chunk in (second, fourth):
            chunk.end(sum_qkv.send)
        sum_qkv.end().begin()
        for chunk in (shared_in, shared_out):
            chunk.end(sum_qkv.send).begin()
        for chunk in (fifth, sum_out):
            chunk.end(sum_qkv.send)
        sum_qkv.end().begin()
        in_grads = [[s.finish() for s in row[:2]] for row in sums]
        out_grads = [row[2].finish() for row in sums]
        sum_shared_in, sum_shared_out = shared_in.finish()[0], shared_out.finish()
        sum_out, sum_qkv = sum_out.finish()[0], sum_qkv.finish()[0]
    else:
        in_grads = [
            [reduce_experts(place, *part[k : k + 2]) for k in (0, 2)] for part in parts
        ]
        out_grads = [reduce_experts(place, *part[4:]) for part in parts]
        sum_shared_in = reduce_shared_in(place, *shared_grads[:2])
        sum_shared_out = reduce_shared_out(place, *shared_grads[2:])
        sum_out, sum_qkv = reduce_weight(place, *sides_out), reduce_weight(place, *sides_qkv)
    own = model_width // place.experts
    sum_out, small = sum_out[:, :own], sum_out[:, own:]
    sum_norm_ffn, sum_router = small[:, 0] + small[:, 1], small[:, 2 : 2 + local_experts]
    sum_qkv, small = sum_qkv[:, : 3 * own], sum_qkv[:, 3 * own :]
    sum_norm_attn = small[:, 0] + small[:, 1]
    part_in = jnp.stack([jnp.concatenate(g, axis=1) for g in in_grads], axis=1)
    part_out = jnp.stack(out_grads, axis=1)
    return (
        output[None],
        grad_input[None],
        sum_norm_attn,
        sum_qkv,
        sum_out,
        sum_norm_ffn,
        sum_router,
        part_in,
        part_out,
        sum_shared_in,
        sum_shared_out.T,
    )


def solution(mesh):
    dp, experts = mesh.shape["dp"], mesh.shape["expert"]
    finer = Mesh(mesh.devices.reshape(4, dp // 4, experts // 2, 2), ("g", "r", "y", "c"))
    whole = P()
    return jax.shard_map(
        local,
        mesh=finer,
        in_specs=(
            P(EX, DP, None),
            whole,
            whole,
            whole,
            whole,
            whole,
            P(None, EX, None),
            P(None, EX, None),
            whole,
            whole,
            P(EX, None),
            P(EX, DP, None),
            P(EX, DP, None),
        ),
        out_specs=(
            P(EX, DP, None),
            P(EX, DP, None),
            P(DP),
            P(DP, EX),
            P(DP, EX),
            P(DP),
            P(DP, EX),
            P(DP, EX, None),
            P(DP, EX, None),
            P(DP, EX),
            P(DP, EX),
        ),
        check_vma=False,
    )
```

```python
import functools

import jax
import jax.numpy as jnp
from jax import lax
from jax.experimental import pallas as pl
from jax.experimental.pallas import tpu as pltpu
from jax.sharding import Mesh
from jax.sharding import PartitionSpec as P

HEADS = 12
HEAD_DIM = 64
TOP = 2
EPS = 1e-06
NEG = -1e30
F32 = jnp.float32
BF16 = jnp.bfloat16
STEPS = 8
DP = ("g", "r")
EX = ("y", "c")
LEADS = ("g", "g")
VMEM = 56 * 1024 * 1024


def takes(microseconds):
    return pl.CostEstimate(
        flops=int(microseconds * 1.15e9), bytes_accessed=1024, transcendentals=0
    )


def rope_table(positions):
    lane = jnp.arange(2 * HEAD_DIM, dtype=jnp.int32) % HEAD_DIM
    half_dim = HEAD_DIM // 2
    frequency = 10000.0 ** (-(lane % half_dim).astype(F32) * 2.0 / HEAD_DIM)
    angles = positions.astype(F32)[:, None] * frequency[None, :]
    return jnp.cos(angles), jnp.sin(angles) * jnp.where(lane < half_dim, -1.0, 1.0)


def rms_scale(hidden):
    return lax.rsqrt(jnp.mean(hidden * hidden, axis=-1, keepdims=True) + EPS)


def rms_back(hidden, scale_rows, gain_vector, upstream):
    normed_grad = upstream * gain_vector
    inner_mean = jnp.mean(normed_grad * hidden, axis=-1, keepdims=True)
    return scale_rows * normed_grad - hidden * scale_rows**3 * inner_mean


class Place:
    def __init__(self):
        self.groups, self.lanes = lax.axis_size("g"), lax.axis_size("r")
        self.rows_y = lax.axis_size("y")
        self.dp = self.groups * self.lanes
        self.experts = self.rows_y * 2
        self.g, self.r = lax.axis_index("g"), lax.axis_index("r")
        self.y, self.c = lax.axis_index("y"), lax.axis_index("c")
        self.low, self.high = self.g % 2, self.g // 2

    def own(self, b):
        g, r = b // self.lanes, b % self.lanes
        low, high = g % 2, g // 2
        if self.lanes == 2:
            return r ^ self.r, low * 2 + high
        return low ^ self.low, high * self.lanes + r

    def flat(self, b):
        g, r = b // self.lanes, b % self.lanes
        if self.lanes == 2:
            return r * 4 + (g % 2) * 2 + g // 2
        return (g % 2 * 2 + g // 2) * self.lanes + r

    def expert_table(self, width, lead):
        sub = STEPS // 4
        order = []
        for pos in range(STEPS):
            half, rest = pos // 4, pos % 4
            if self.lanes == 2 and lead == "r":
                low, high, part = rest // 2, rest % 2, half ^ self.r
            elif self.lanes == 2:
                low, high, part = half ^ self.low, rest % 2, rest // 2
            else:
                low, high, part = half ^ self.low, rest // 2, rest % 2
            order.append((high * 2 + low) * sub + part)
        block = width // self.dp
        rows = []
        for b in range(self.dp):
            half, rest = self.own(b)
            rows.append(half * (width // 2) + rest * block)
        return jnp.stack([jnp.asarray(v, jnp.int32) for v in order + [0] * STEPS + rows])

    def shared_table(self, width):
        per = 16 // self.experts
        order, columns = [], []
        sub = STEPS // 4
        for pos in range(STEPS):
            half, rest = pos // 4, pos % 4
            j = (rest // per * 2 + (half ^ self.c)) * per + rest % per
            order.append(j)
            g, part = j // sub, j % sub
            if self.lanes == 2:
                columns.append(part * 4 + g % 2 * 2 + g // 2)
            else:
                columns.append((g % 2 * 2 + g // 2) * sub + part)
        block = width // self.dp
        rows = [self.flat(b) * block for b in range(self.dp)]
        own = width // self.experts
        turned = [
            (e % 2 ^ self.c) * (width // 2) + e // 2 * own for e in range(self.experts)
        ]
        return jnp.stack(
            [jnp.asarray(v, jnp.int32) for v in order + columns + rows + turned]
        )


def nt(a, b):
    return lax.dot_general(a, b, (((1,), (1,)), ((), ())), preferred_element_type=F32)


def nn(a, b):
    return lax.dot_general(a, b, (((1,), (0,)), ((), ())), preferred_element_type=F32)


def turn(x, cosine, sine):
    width = x.shape[1]
    lane = lax.broadcasted_iota(jnp.int32, x.shape, 1) % HEAD_DIM
    other = jnp.where(
        lane < HEAD_DIM // 2,
        pltpu.roll(x, width - HEAD_DIM // 2, 1),
        pltpu.roll(x, HEAD_DIM // 2, 1),
    )
    times = width // cosine.shape[1]
    cosine = jnp.concatenate([cosine] * times, axis=1)
    sine = jnp.concatenate([sine] * times, axis=1)
    return x * cosine + other * sine


def project_kernel(here, x_ref, gain_ref, w_ref, cos_ref, sin_ref, normed_ref, *refs):
    step = pl.program_id(0)
    groups = (len(refs) - 2) // 2
    q_refs, kv_refs, (q_all, kv_all) = refs[:groups], refs[groups:-2], refs[-2:]
    half, three = x_ref.shape[0] // 2, 3 * HEAD_DIM

    @pl.when(step == 0)
    def _():
        x = x_ref[...].astype(F32)
        normed_ref[...] = (x * rms_scale(x) * gain_ref[...]).astype(BF16)

    part = nn(normed_ref[...], w_ref[...])

    @pl.when(step == 0)
    def _():
        pack_heads(turn(part, cos_ref[...], sin_ref[...]) * HEAD_DIM**-0.5, q_all)

    @pl.when(step == 1)
    def _():
        k = turn(part, cos_ref[...], sin_ref[...])
        for g in range(groups):
            own = k[:, g * three : (g + 1) * three].astype(BF16)
            kv_all[g, :, 0:128] = own[:, :128]
            kv_all[g, :, 256:320] = own[:, 128:]

    @pl.when(step == 2)
    def _():
        for g in range(groups):
            own = part[:, g * three : (g + 1) * three].astype(BF16)
            kv_all[g, :, 128:256] = own[:, :128]
            kv_all[g, :, 320:384] = own[:, 128:]
        for d in range(groups):
            q_refs[d][...] = q_all[here[0] ^ d]
            kv_refs[d][...] = kv_all[here[0] ^ d]


def pack_heads(rows, packed_ref):
    half, three = rows.shape[0] // 2, 3 * HEAD_DIM
    for g in range(packed_ref.shape[0]):
        own = rows[:, g * three : (g + 1) * three].astype(BF16)
        packed_ref[g, :, 0:128] = own[:half, :128]
        packed_ref[g, :, 128:256] = own[half:, :128]
        packed_ref[g, :, 256:320] = own[:half, 128:]
        packed_ref[g, :, 320:384] = own[half:, 128:]


def project(place, x, gain, weight, cosine, sine):
    rows, width = x.shape
    groups = place.groups
    sds = jax.ShapeDtypeStruct
    whole = lambda *shape: pl.BlockSpec(shape, lambda i, t: (0,) * len(shape))
    normed, *parts = pl.pallas_call(
        project_kernel,
        out_shape=(sds((rows, width), BF16),)
        + (sds((rows // 2, 384), BF16),) * groups
        + (sds((rows, 384), BF16),) * groups,
        grid_spec=pltpu.PrefetchScalarGridSpec(
            num_scalar_prefetch=1,
            grid=(3,),
            in_specs=[
                whole(rows, width),
                whole(1, width),
                pl.BlockSpec((width, width), lambda i, t: (0, i)),
                whole(rows, 128),
                whole(rows, 128),
            ],
            out_specs=(whole(rows, width),)
            + (whole(rows // 2, 384),) * groups
            + (whole(rows, 384),) * groups,
            scratch_shapes=[
                pltpu.VMEM((groups, rows // 2, 384), BF16),
                pltpu.VMEM((groups, rows, 384), BF16),
            ],
        ),
        compiler_params=pltpu.CompilerParams(vmem_limit_bytes=VMEM),
        cost_estimate=takes(4),
    )(place.g[None], x, gain[None], weight, cosine, sine)
    return normed, parts[:groups], parts[groups:]


def unpack(packed, second_low):
    half = packed.shape[0]
    x = packed.astype(F32)
    lane = lax.broadcasted_iota(jnp.int32, (half, 128), 1)
    low = lane < HEAD_DIM
    first, second, third = x[:, 0:128], x[:, 128:256], x[:, 256:384]
    turned = pltpu.roll(third, HEAD_DIM, 1)
    zero = jnp.zeros_like(third)
    pair = [
        jnp.where(low, first, zero),
        jnp.where(low, second, zero),
        jnp.where(low, zero, first),
        jnp.where(low, zero, second),
    ]
    if second_low:
        single = [jnp.where(low, third, zero), jnp.where(low, turned, zero)]
    else:
        single = [jnp.where(low, zero, turned), jnp.where(low, zero, third)]
    return (
        jnp.concatenate(pair, axis=0).astype(BF16),
        jnp.concatenate(single, axis=0).astype(BF16),
    )


def visible_keys(kz, source, lanes, rows, limit):
    first = (kz * lanes + source) * rows
    place = first + lax.broadcasted_iota(jnp.int32, (rows, limit.shape[1]), 0)
    return place < limit


def attend_kernel(sources, shards, lanes, info, limit_ref, *refs):
    q_refs, kv_refs = refs[:shards], refs[shards : shards * (1 + sources)]
    out_refs, (lse_ref, q_ref, kv_all, turned, out_ref) = refs[shards * (1 + sources) : -5], refs[-5:]
    half = q_ref.shape[1]
    rows = 2 * half
    gather_heads(info, q_refs, q_ref)
    gather_keys(info, shards, kv_refs, kv_all, turned)

    def shard(z, carry):
        pair, single = unpack(q_ref[z], True)
        limit = limit_ref[z]

        def step(kz, state):
            largest, total, acc_pair, acc_single = state
            scores = []
            for s in range(sources):
                keep = visible_keys(kz, info[1 + shards + s], lanes, rows, limit)
                two = nt(kv_all[s, kz, :, 0:128], pair)
                one = nt(kv_all[s, kz, :, 256:384], single)
                both = jnp.concatenate([two, one], axis=1)
                keep = jnp.concatenate([keep] * 3, axis=1)
                scores.append(jnp.where(keep, both, NEG))
            newest = largest
            for sc in scores:
                newest = jnp.maximum(newest, jnp.max(sc, axis=0, keepdims=True))
            fade = jnp.exp(largest - newest)
            total = total * fade
            acc_pair = acc_pair * fade[:, : 2 * rows]
            acc_single = acc_single * fade[:, 2 * rows :]
            for s, sc in enumerate(scores):
                power = jnp.exp(sc - newest)
                total = total + jnp.sum(power, axis=0, keepdims=True)
                power = power.astype(BF16)
                acc_pair = acc_pair + nn(turned[s, kz, 128:256, :], power[:, : 2 * rows])
                acc_single = acc_single + nn(turned[s, kz, 256:384, :], power[:, 2 * rows :])
            return newest, total, acc_pair, acc_single

        largest, total, acc_pair, acc_single = lax.fori_loop(
            0,
            info[1 + z],
            step,
            (
                jnp.full((1, 3 * rows), NEG, F32),
                jnp.zeros((1, 3 * rows), F32),
                jnp.zeros((128, 2 * rows), F32),
                jnp.zeros((128, rows), F32),
            ),
        )
        lse_ref[z] = largest + jnp.log(total)
        share = 1.0 / total
        first = acc_pair[:HEAD_DIM, :rows] * share[:, :rows]
        second = acc_pair[HEAD_DIM:, rows:] * share[:, rows : 2 * rows]
        third = acc_single[HEAD_DIM:] * share[:, 2 * rows :]
        packed = jnp.concatenate(
            [a[:, part] for part in (slice(0, half), slice(half, rows)) for a in (first, second)]
            + [third[:, :half], third[:, half:]],
            axis=0,
        )
        out_ref[z] = packed.T.astype(BF16)
        return carry

    lax.fori_loop(0, shards, shard, 0)


    for d in range(shards):
        out_refs[d][...] = out_ref[info[0] ^ d]


def gather_heads(info, refs, packed_ref):
    for d, ref in enumerate(refs):
        packed_ref[info[0] ^ d] = ref[...]


def gather_keys(info, shards, refs, kv_all, turned):
    for i, ref in enumerate(refs):
        at = info[0] ^ (i % shards)
        kv_all[i // shards, at] = ref[...]
        turned[i // shards, at] = ref[...].astype(F32).T.astype(BF16)


def attend(place, info, limit, qs, kvs):
    half, lanes = qs[0].shape
    shards, sources = len(qs), len(kvs) // len(qs)
    vmem = pl.BlockSpec(memory_space=pltpu.VMEM)
    sds = jax.ShapeDtypeStruct
    *outs, lse = pl.pallas_call(
        functools.partial(attend_kernel, sources, shards, place.lanes),
        out_shape=(sds((half, lanes), BF16),) * shards + (sds((shards, 1, 6 * half), F32),),
        in_specs=[pl.BlockSpec(memory_space=pltpu.SMEM)] + [vmem] * (1 + shards * (1 + sources)),
        out_specs=(vmem,) * (shards + 1),
        scratch_shapes=[
            pltpu.VMEM((shards, half, lanes), BF16),
            pltpu.VMEM((sources, shards, 2 * half, lanes), BF16),
            pltpu.VMEM((sources, shards, lanes, 2 * half), BF16),
            pltpu.VMEM((shards, half, lanes), BF16),
        ],
        compiler_params=pltpu.CompilerParams(vmem_limit_bytes=VMEM),
        cost_estimate=takes(12),
    )(info, limit, *qs, *kvs)
    return outs, lse


def attend_back_kernel(sources, shards, lanes, info, limit_ref, lse_ref, *refs):
    q_refs, o_refs, g_refs = (refs[i * shards : (i + 1) * shards] for i in range(3))
    kv_refs = refs[3 * shards : (3 + sources) * shards]
    dq_refs = refs[(3 + sources) * shards : (4 + sources) * shards]
    dkv_refs = refs[(4 + sources) * shards : (4 + sources) * shards + sources]
    q_ref, out_ref, grad_ref, dq_ref, kv_all, turned, total = refs[-7:]
    half = q_ref.shape[1]
    rows = 2 * half
    gather_heads(info, q_refs, q_ref)
    gather_heads(info, o_refs, out_ref)
    gather_heads(info, g_refs, grad_ref)
    gather_keys(info, shards, kv_refs, kv_all, turned)
    total[...] = jnp.zeros_like(total)

    def shard(z, carry):
        pair, single = unpack(q_ref[z], True)
        grad_pair, grad_single = unpack(grad_ref[z], False)
        limit, lse = limit_ref[z], lse_ref[z]
        product = (grad_ref[z].astype(F32) * out_ref[z].astype(F32)).T
        sums = [
            jnp.sum(product[i * HEAD_DIM : (i + 1) * HEAD_DIM], axis=0, keepdims=True)
            for i in range(6)
        ]
        delta = jnp.concatenate([sums[0], sums[2], sums[1], sums[3], sums[4], sums[5]], axis=1)

        def step(kz, state):
            dq_pair, dq_single = state
            for s in range(sources):
                keep = visible_keys(kz, info[1 + shards + s], lanes, rows, limit)
                keep = jnp.concatenate([keep] * 3, axis=1)
                k01, v01 = kv_all[s, kz, :, 0:128], kv_all[s, kz, :, 128:256]
                kv2 = kv_all[s, kz, :, 256:384]
                scores = jnp.concatenate([nt(k01, pair), nt(kv2, single)], axis=1)
                grads = jnp.concatenate([nt(v01, grad_pair), nt(kv2, grad_single)], axis=1)
                power = jnp.where(keep, jnp.exp(scores - lse), 0.0)
                slope = (power * (grads - delta)).astype(BF16)
                power = power.astype(BF16)
                dq_pair = dq_pair + nn(turned[s, kz, 0:128, :], slope[:, : 2 * rows])
                dq_single = dq_single + nn(turned[s, kz, 256:384, :], slope[:, 2 * rows :])
                total[s, kz, :, 0:128] += nn(slope[:, : 2 * rows], pair)
                total[s, kz, :, 128:256] += nn(power[:, : 2 * rows], grad_pair)
                total[s, kz, :, 256:384] += nn(slope[:, 2 * rows :], single) + nn(
                    power[:, 2 * rows :], grad_single
                )
            return dq_pair, dq_single

        dq_pair, dq_single = lax.fori_loop(
            0,
            info[1 + z],
            step,
            (jnp.zeros((128, 2 * rows), F32), jnp.zeros((128, rows), F32)),
        )
        first, second = dq_pair[:HEAD_DIM, :rows], dq_pair[HEAD_DIM:, rows:]
        third = dq_single[:HEAD_DIM]
        packed = jnp.concatenate(
            [a[:, part] for part in (slice(0, half), slice(half, rows)) for a in (first, second)]
            + [third[:, :half], third[:, half:]],
            axis=0,
        )
        dq_ref[z] = packed.T.astype(BF16)
        return carry

    lax.fori_loop(0, shards, shard, 0)
    for d in range(shards):
        dq_refs[d][...] = dq_ref[info[0] ^ d]
    for s, ref in enumerate(dkv_refs):
        for d in range(shards):
            ref[d] = total[s, info[0] ^ d].astype(BF16)


def attend_back(place, info, limit, lse, qs, outs, grads, kvs):
    half, lanes = qs[0].shape
    shards, sources = len(qs), len(kvs) // len(qs)
    vmem = pl.BlockSpec(memory_space=pltpu.VMEM)
    sds = jax.ShapeDtypeStruct
    parts = pl.pallas_call(
        functools.partial(attend_back_kernel, sources, shards, place.lanes),
        out_shape=(sds((half, lanes), BF16),) * shards
        + (sds((shards, 2 * half, lanes), BF16),) * sources,
        in_specs=[pl.BlockSpec(memory_space=pltpu.SMEM)] + [vmem] * (2 + shards * (3 + sources)),
        out_specs=(vmem,) * (shards + sources),
        scratch_shapes=[pltpu.VMEM((shards, half, lanes), BF16)] * 4
        + [
            pltpu.VMEM((sources, shards, 2 * half, lanes), BF16),
            pltpu.VMEM((sources, shards, lanes, 2 * half), BF16),
            pltpu.VMEM((sources, shards, 2 * half, lanes), F32),
        ],
        compiler_params=pltpu.CompilerParams(vmem_limit_bytes=VMEM),
        cost_estimate=takes(19),
    )(info, limit, lse, *qs, *outs, *grads, *kvs)
    return list(parts[:shards]), parts[shards:]


def finish_kernel(
    here, w_ref, cos_ref, sin_ref, x_ref, gain_ref, middle_ref, *refs,
):
    groups = (len(refs) - 6) // 2
    dq_refs, dkv_refs = refs[:groups], refs[groups : 2 * groups]
    projected_ref, input_ref, norm_ref, dq_all, dkv_all, gather = refs[2 * groups :]
    rows, width = x_ref.shape
    half, three = rows // 2, 3 * HEAD_DIM
    for d in range(groups):
        dq_all[here[0] ^ d] = dq_refs[d][...].astype(F32)
        dkv_all[here[0] ^ d] = dkv_refs[d][...].astype(F32)
    for g in range(groups):
        at = g * three
        dq, dkv = dq_all[g], dkv_all[g]
        gather[0, :half, at : at + 128] = dq[:, 0:128]
        gather[0, half:, at : at + 128] = dq[:, 128:256]
        gather[0, :half, at + 128 : at + three] = dq[:, 256:320]
        gather[0, half:, at + 128 : at + three] = dq[:, 320:384]
        gather[1, :, at : at + 128] = dkv[:, 0:128]
        gather[1, :, at + 128 : at + three] = dkv[:, 256:320]
        gather[2, :, at : at + 128] = dkv[:, 128:256]
        gather[2, :, at + 128 : at + three] = dkv[:, 320:384]
    cosine, sine = cos_ref[...], -sin_ref[...]
    parts = [
        (turn(gather[0], cosine, sine) * HEAD_DIM**-0.5).astype(BF16),
        turn(gather[1], cosine, sine).astype(BF16),
        gather[2].astype(BF16),
    ]
    grad = jnp.zeros((rows, width), F32)
    for i, part in enumerate(parts):
        projected_ref[:, i * width : (i + 1) * width] = part
        grad = grad + nt(part, w_ref[:, i * width : (i + 1) * width])
    x = x_ref[...].astype(F32)
    scale = rms_scale(x)
    norm_ref[...] = jnp.sum(grad * x * scale, axis=0, keepdims=True)
    input_ref[...] = middle_ref[...] + rms_back(x, scale, gain_ref[...], grad)


def finish(place, dqs, dkvs, weight, cosine, sine, x, gain, middle):
    rows, width = x.shape
    groups = place.groups
    vmem = pl.BlockSpec(memory_space=pltpu.VMEM)
    return pl.pallas_call(
        finish_kernel,
        out_shape=(
            jax.ShapeDtypeStruct((rows, 3 * width), BF16),
            jax.ShapeDtypeStruct((rows, width), F32),
            jax.ShapeDtypeStruct((1, width), F32),
        ),
        in_specs=[pl.BlockSpec(memory_space=pltpu.SMEM)] + [vmem] * (6 + 2 * groups),
        out_specs=(vmem,) * 3,
        scratch_shapes=[
            pltpu.VMEM((groups, rows // 2, 384), F32),
            pltpu.VMEM((groups, rows, 384), F32),
            pltpu.VMEM((3, rows, width), F32),
        ],
        compiler_params=pltpu.CompilerParams(vmem_limit_bytes=VMEM),
        cost_estimate=takes(5),
    )(place.g[None], weight, cosine, sine, x, gain[None], middle, *dqs, *dkvs)


def middle_kernel(
    here, x_ref, grad_ref, w_ref, gain_ref, router_ref, pick0, pick1, seat0, seat1, *refs,
):
    groups = 4
    o_refs = refs[:groups]
    low_ref, middle_ref, mixed_ref, gate_ref = refs[groups : groups + 4]
    sent = refs[groups + 4 : -2]
    o_all, gather = refs[-2:]
    count = len(sent) // 2
    half, three = x_ref.shape[0] // 2, 3 * HEAD_DIM
    for d in range(groups):
        o_all[here[0] ^ d] = o_refs[d][...].astype(F32)
    for g in range(groups):
        at = g * three
        gather[:half, at : at + 128] = o_all[g, :, 0:128]
        gather[half:, at : at + 128] = o_all[g, :, 128:256]
        gather[:half, at + 128 : at + three] = o_all[g, :, 256:320]
        gather[half:, at + 128 : at + three] = o_all[g, :, 320:384]
    low = gather[...].astype(BF16)
    low_ref[...] = low
    middle = x_ref[...].astype(F32) + nn(low, w_ref[...])
    middle_ref[...] = middle
    mixed = (middle * rms_scale(middle) * gain_ref[...]).astype(BF16)
    mixed_ref[...] = mixed
    scores = nn(mixed, router_ref[...])
    picked = [jnp.sum(scores * p[...], axis=1, keepdims=True) for p in (pick0, pick1)]
    largest = jnp.maximum(*picked)
    powers = [jnp.exp(p - largest) for p in picked]
    gates = [p / (powers[0] + powers[1]) for p in powers]
    gate_ref[...] = jnp.concatenate(gates, axis=1)
    seats = (seat0[...], seat1[...])
    held = jnp.zeros((seats[0].shape[0], 1), F32)
    for seat, gate in zip(seats, gates):
        high = gate.astype(BF16)
        rest = (gate - high.astype(F32)).astype(BF16)
        held = held + jnp.sum(nn(seat, jnp.concatenate([high, rest], axis=1)), axis=1, keepdims=True)
    every = seats[0] + seats[1]
    rows = nn(every, mixed).astype(BF16)
    grads = (nn(every, grad_ref[...]) * held).astype(BF16)
    capacity = sent[0].shape[1]
    for d in range(count):
        for e in range(sent[0].shape[0]):
            at = (e * count + d) * capacity
            sent[d][e] = rows[at : at + capacity]
            sent[count + d][e] = grads[at : at + capacity]


def middle_part(place, capacity, outs, x, grad, weight, gain, router, picks, seats):
    rows, width = x.shape
    groups, count = place.groups, place.experts
    local = router.shape[1] // count
    vmem = pl.BlockSpec(memory_space=pltpu.VMEM)
    sds = jax.ShapeDtypeStruct
    low, middle, mixed, gates, *sent = pl.pallas_call(
        middle_kernel,
        out_shape=(
            sds((rows, width), BF16),
            sds((rows, width), F32),
            sds((rows, width), BF16),
            sds((rows, TOP), F32),
        )
        + (sds((local, capacity, width), BF16),) * (2 * count),
        in_specs=[pl.BlockSpec(memory_space=pltpu.SMEM)] + [vmem] * (9 + groups),
        out_specs=(vmem,) * (4 + 2 * count),
        scratch_shapes=[
            pltpu.VMEM((groups, rows // 2, 384), F32),
            pltpu.VMEM((rows, width), F32),
        ],
        compiler_params=pltpu.CompilerParams(vmem_limit_bytes=VMEM),
        cost_estimate=takes(4),
    )(place.g[None], x, grad, weight, gain[None], router, *picks, *seats, *outs)
    return low, middle, mixed, gates, sent[:count], sent[count:]


def trade(parts, axis):
    size = lax.axis_size(axis)
    return [parts[0]] + [
        lax.ppermute(parts[d], axis, [(i, i ^ d) for i in range(size)]) for d in range(1, size)
    ]


def ffn_kernel(shared, count, dp, experts, table, *refs):
    x_refs, dy_refs, (gate_ref, up_ref, down_ref) = refs[:count], refs[count : 2 * count], refs[2 * count : 2 * count + 3]
    refs = refs[2 * count + 3 :]
    if shared:
        result, back, in_keep, in_send, out_keep, out_send, stage, turned, turned_dy = refs
        x_ref, dy_ref = x_refs[0], dy_refs[0]
    else:
        both, refs = refs[:count], refs[count:]
        gate_keep, gate_send, up_keep, up_send, out_keep, out_send = refs[:6]
        in_keep, in_send = (gate_keep, up_keep), (gate_send, up_send)
        stage, turned, result, back, x_ref, dy_ref = refs[6:]
    step = pl.program_id(0)
    width = x_ref.shape[1]
    rows = x_ref.shape[0]

    @pl.when(step == 0)
    def _():
        if not shared:
            part = rows // count
            for d in range(count):
                x_ref[d * part : (d + 1) * part] = x_refs[d][0]
                dy_ref[d * part : (d + 1) * part] = dy_refs[d][0]
        whole = x_ref[...].astype(F32).T
        block = width // dp
        for b in range(dp):
            start = pl.multiple_of(table[2 * STEPS + b], 8)
            stage[pl.ds(start, block), :] = whole[b * block : (b + 1) * block]
        turned[...] = stage[...].astype(BF16)
        if shared:
            whole = dy_ref[...].astype(F32).T
            block = width // experts
            for e in range(experts):
                start = pl.multiple_of(table[2 * STEPS + dp + e], 8)
                stage[pl.ds(start, block), :] = whole[e * block : (e + 1) * block]
            turned_dy[...] = stage[...].astype(BF16)
        result[...] = jnp.zeros_like(result)
        back[...] = jnp.zeros_like(back)

    x, dy = x_ref[...], dy_ref[...]
    w_gate, w_up, w_down = gate_ref[0], up_ref[0], down_ref[0]
    gate, up = nn(x, w_gate), nn(x, w_up)
    grad = nt(dy, w_down)
    sig = jax.nn.sigmoid(gate)
    silu = gate * sig
    act = (silu * up).astype(BF16)
    grad_gate = (grad * up * (sig * (1.0 + gate * (1.0 - sig)))).astype(BF16)
    grad_up = (grad * silu).astype(BF16)
    result[...] += nn(act, w_down)
    back[...] += nt(grad_gate, w_gate) + nt(grad_up, w_up)
    xt = turned[...]
    half = width // 2
    for k, upper in enumerate((grad_gate, grad_up)):
        grad_in = nn(xt, upper).astype(BF16)
        if shared:

            @pl.when(step < STEPS // 2)
            def _():
                in_keep[k] = grad_in

            @pl.when(step >= STEPS // 2)
            def _():
                in_send[k] = grad_in

        else:
            in_keep[k][...] = grad_in[:half]
            in_send[k][...] = grad_in[half:]
    if shared:
        grad_out = nn(turned_dy[...], act).astype(BF16)
        out_keep[...] = grad_out[:half]
        out_send[...] = grad_out[half:]
    else:
        grad_out = lax.dot_general(
            act, dy, (((0,), (0,)), ((), ())), preferred_element_type=F32
        ).astype(BF16)

        @pl.when(step < STEPS // 2)
        def _():
            out_keep[...] = grad_out

        @pl.when(step >= STEPS // 2)
        def _():
            out_send[...] = grad_out

        @pl.when(step == STEPS - 1)
        def _():
            part = rows // count
            for d in range(count):
                both[d][:, :width] = result[d * part : (d + 1) * part].astype(BF16)
                both[d][:, width:] = back[d * part : (d + 1) * part].astype(BF16)


def ffn(shared, place, table, xs, dys, w_in, w_out, e):
    count = len(xs)
    part, width = xs[0].shape[-2:]
    rows = part * count
    if shared:
        given = pl.BlockSpec((rows, width), lambda i, t: (0, 0))
    else:
        given = pl.BlockSpec((1, part, width), lambda i, t: (e, 0, 0))
    hidden = w_out.shape[1]
    chunk = hidden // STEPS
    near, far = STEPS // 2 - 1, STEPS // 2
    sds = jax.ShapeDtypeStruct
    first = lambda i, t: (0, 0, jnp.minimum(i, near))
    second = lambda i, t: (0, 0, jnp.maximum(i - far, 0))
    if shared:
        out_shape = (
            sds((rows, width), F32),
            sds((rows, width), F32),
            sds((2, width, hidden // 2), BF16),
            sds((2, width, hidden // 2), BF16),
            sds((width // 2, hidden), BF16),
            sds((width // 2, hidden), BF16),
        )
        out_specs = (
            pl.BlockSpec((rows, width), lambda i, t: (0, 0)),
            pl.BlockSpec((rows, width), lambda i, t: (0, 0)),
            pl.BlockSpec((2, width, chunk), first),
            pl.BlockSpec((2, width, chunk), second),
            pl.BlockSpec((width // 2, chunk), lambda i, t: (0, t[STEPS + i])),
            pl.BlockSpec((width // 2, chunk), lambda i, t: (0, t[STEPS + i])),
        )
        extra = [pltpu.VMEM((width, rows), BF16)]
    else:
        out_shape = (
            *[sds((part, 2 * width), BF16)] * count,
            *[sds((width // 2, hidden), BF16)] * 4,
            sds((hidden // 2, width), BF16),
            sds((hidden // 2, width), BF16),
        )
        out_specs = (
            *[pl.BlockSpec((part, 2 * width), lambda i, t: (0, 0))] * count,
            *[pl.BlockSpec((width // 2, chunk), lambda i, t: (0, t[i]))] * 4,
            pl.BlockSpec((chunk, width), lambda i, t: (jnp.minimum(i, near), 0)),
            pl.BlockSpec((chunk, width), lambda i, t: (jnp.maximum(i - far, 0), 0)),
        )
        extra = [pltpu.VMEM((rows, width), F32)] * 2 + [pltpu.VMEM((rows, width), BF16)] * 2
    return pl.pallas_call(
        functools.partial(ffn_kernel, shared, count, place.dp, place.experts),
        out_shape=out_shape,
        grid_spec=pltpu.PrefetchScalarGridSpec(
            num_scalar_prefetch=1,
            grid=(STEPS,),
            in_specs=[
                *[given] * (2 * count),
                pl.BlockSpec((1, width, chunk), lambda i, t: (e, 0, t[i])),
                pl.BlockSpec((1, width, chunk), lambda i, t: (e, 0, STEPS + t[i])),
                pl.BlockSpec((1, chunk, width), lambda i, t: (e, t[i], 0)),
            ],
            out_specs=out_specs,
            scratch_shapes=[pltpu.VMEM((width, rows), F32), pltpu.VMEM((width, rows), BF16)]
            + extra,
        ),
        compiler_params=pltpu.CompilerParams(vmem_limit_bytes=VMEM),
        cost_estimate=takes(18),
    )(table, *xs, *dys, w_in, w_in, w_out)


def swap(a, axis, bit=1):
    size = lax.axis_size(axis)
    return lax.ppermute(a, axis, [(i, i ^ bit) for i in range(size)])


def add(a, b, kind=BF16):
    return (a.astype(F32) + b.astype(F32)).astype(kind)


def half_of(a, dim, index):
    size = a.shape[dim] // 2
    return lax.dynamic_slice_in_dim(a, index * size, size, dim)


def exchange(keep, came, dim, mine):
    return [add(half_of(keep, dim, i), half_of(came, dim, i)) for i in (mine, 1 - mine)]


def scatter(a, axis, dim):
    return lax.psum_scatter(a, axis, scatter_dimension=dim, tiled=True)


def reduce_experts(place, keep, send):
    came = swap(send, "g", 1)
    keep, send = exchange(keep, came, 0, place.high)
    return scatter(add(keep, swap(send, "g", 2)), "r", 0).astype(F32)


def after(x, *values):
    return lax.optimization_barrier((x, *values))[0]


def reduce_tokens(place, keep, came, dim):
    keep, send = exchange(keep, came, dim, place.low)
    came = swap(send, "g", 1)
    keep, send = exchange(keep, came, dim, place.high)
    came = swap(send, "g", 2)
    return scatter(add(keep, came), "r", dim).astype(F32)


def reduce_shared_in(place, keep, send):
    total = add(keep, swap(send, "c"))
    two, width, columns = total.shape
    parts = place.rows_y // 2
    total = total.reshape(two, width, parts, columns // parts).transpose(0, 2, 1, 3)
    mine = scatter(total.reshape(two * parts, width, columns // parts), "y", 0)[0]
    return reduce_tokens(place, mine, jnp.zeros_like(mine), 0)


def reduce_shared_out(place, keep, send):
    mine = scatter(add(keep, swap(send, "c")), "y", 0)
    return reduce_tokens(place, mine, jnp.zeros_like(mine), 1)


def to_flat(place, x):
    rows, width = x.shape
    x = x.reshape(rows, 2, 2, place.lanes, width // place.dp)
    order = (0, 3, 2, 1, 4) if place.lanes == 2 else (0, 2, 1, 3, 4)
    return x.transpose(order).reshape(rows, width)


def weight_grad(place, left, right, extra):
    rows, columns = right.shape
    width = left.shape[1]
    own = columns // place.experts
    parts = right.reshape(rows, place.rows_y, 2, own)
    extra = extra.reshape(width, place.rows_y, 2, extra.shape[-1]).astype(BF16)
    keep, send = [
        jnp.concatenate(
            [
                lax.dot_general(
                    left,
                    lax.dynamic_index_in_dim(parts, i, 2, False).reshape(rows, columns // 2),
                    (((0,), (0,)), ((), ())),
                    preferred_element_type=F32,
                )
                .astype(BF16)
                .reshape(width, place.rows_y, own),
                lax.dynamic_index_in_dim(extra, i, 2, False),
            ],
            axis=2,
        ).transpose(1, 0, 2)
        for i in (place.c, 1 - place.c)
    ]
    return keep, send


def reduce_weight(place, keep, send):
    mine = scatter(add(keep, swap(send, "c")), "y", 0)[0]
    return reduce_tokens(place, mine, jnp.zeros_like(mine), 0)


def in_two(vector):
    high = vector.astype(BF16).astype(F32)
    return [high, vector - high]


def beside(place, columns, experts_of):
    width = columns[0].shape[0]
    every = jnp.stack(columns, axis=1)[:, None, :]
    every = jnp.broadcast_to(every, (width, place.experts, len(columns)))
    parts = [every] if experts_of is None else [every, experts_of]
    used = sum(p.shape[2] for p in parts)
    return jnp.concatenate(parts + [jnp.zeros((width, place.experts, 64 - used), F32)], axis=2)


def combine_kernel(
    here, hot0, hot1, gate_ref, pick0, pick1, grad_ref, middle_ref,
    shared_ref, back_ref, mixed_in_ref, router_ref, gain_ref, w_ref, *refs,
):
    output_ref, middle_grad_ref, low_ref, *head_refs = refs[-11:-4]
    norm_ref, router_grad_ref, returned, heads = refs[-4:]
    ret_refs = refs[:-11]
    width = grad_ref.shape[1]
    part = ret_refs[0].shape[0]
    for i, ref in enumerate(ret_refs):
        returned[i * part : (i + 1) * part] = ref[...]
    hots = (hot0[...], hot1[...])
    grad = grad_ref[...].astype(F32)
    middle = middle_ref[...]
    backs = [nn(h, returned[:, :width]) for h in hots]
    gates = [gate_ref[:, k : k + 1] for k in range(TOP)]
    routed = sum(gates[k] * backs[k] for k in range(TOP))
    output_ref[...] = (middle + routed + shared_ref[...]).astype(BF16)
    slopes = [jnp.sum(b * grad, axis=1, keepdims=True) for b in backs]
    inner = sum(gates[k] * slopes[k] for k in range(TOP))
    logits = sum(
        pick[...] * (gates[k] * (slopes[k] - inner)) for k, pick in enumerate((pick0, pick1))
    ).astype(BF16)
    router_grad_ref[...] = lax.dot_general(
        logits, mixed_in_ref[...], (((0,), (0,)), ((), ())), preferred_element_type=F32
    )
    mixed = back_ref[...] + nn(logits, router_ref[...]) + nn(hots[0] + hots[1], returned[:, width:])
    scale = rms_scale(middle)
    norm_ref[...] = jnp.sum(mixed * middle * scale, axis=0, keepdims=True)
    middle_grad = grad + rms_back(middle, scale, gain_ref[...], mixed)
    middle_grad_ref[...] = middle_grad
    low = middle_grad.astype(BF16)
    low_ref[...] = low
    pack_heads(nt(low, w_ref[...]), heads)
    for d, ref in enumerate(head_refs):
        ref[...] = heads[here[0] ^ d]


def combine(place, hots, rets, gates, picks, grad, middle, shared, back, mixed_in, router, gain, weight):
    rows, width = grad.shape
    vmem = pl.BlockSpec(memory_space=pltpu.VMEM)
    sds = jax.ShapeDtypeStruct
    output, middle_grad, low, *heads, norm, router_grad = pl.pallas_call(
        combine_kernel,
        out_shape=(
            sds((rows, width), BF16),
            sds((rows, width), F32),
            sds((rows, width), BF16),
        )
        + (sds((rows // 2, 384), BF16),) * place.groups
        + (
            sds((1, width), F32),
            sds((router.shape[1], width), F32),
        ),
        in_specs=[pl.BlockSpec(memory_space=pltpu.SMEM)] + [vmem] * (13 + len(rets)),
        out_specs=(vmem,) * (5 + place.groups),
        scratch_shapes=[
            pltpu.VMEM((hots[0].shape[1], 2 * width), BF16),
            pltpu.VMEM((place.groups, rows // 2, 384), BF16),
        ],
        compiler_params=pltpu.CompilerParams(vmem_limit_bytes=VMEM),
        cost_estimate=takes(5),
    )(
        place.g[None], *hots, gates, *picks, grad, middle, shared, back, mixed_in,
        router.T, gain[None], weight, *rets,
    )
    return output, middle_grad, low, heads, norm, router_grad


class Sum:
    def __init__(self, keep, send, stages, direct=None):
        self.keep, self.send, self.stages, self.came = keep, send, list(stages), None
        self.direct = direct

    def begin(self, *behind):
        send = after(self.send, *behind) if behind else self.send
        if self.stages:
            axis, bit, *self.split = self.stages.pop(0)
            self.came = swap(send, axis, bit)
        else:
            self.came = trade([self.keep] + send, "g")[1:]
        return self

    def end(self, *until):
        came = after(self.came, *until) if until else self.came
        self.came = None
        if isinstance(came, list):
            self.keep, self.direct = sum(a.astype(F32) for a in [self.keep, *came]), None
        elif self.split[0] is not None:
            self.keep, self.send = exchange(self.keep, came, *self.split)
        elif self.direct is None:
            self.keep = add(self.keep, came, F32)
        else:
            size = self.keep.shape[1] // 4
            self.keep, *self.send = [
                add(*(lax.dynamic_slice_in_dim(a, at * size, size, 1) for a in (self.keep, came)))
                for at in self.direct
            ]
        return self

    def finish(self):
        if self.came is not None:
            self.end()
        while self.stages or self.direct is not None:
            self.begin().end()
        return self.keep


def expert_sum(place, keep, send, lead):
    if lead == "r":
        near = [("r", 1, 0, place.low), ("g", 1, 0, place.high)]
    else:
        near = [("g", 1, 0, place.r), ("r", 1, 0, place.high)]
    return Sum(keep, send, near + [("g", 2, None, None)])


def direct_sum(place, keep, send):
    owners = [place.g ^ d for d in range(4)]
    return Sum(
        keep,
        send,
        [("c", 1, 0, place.y), ("y", 1, 1, place.r), ("r", 1, None, None)],
        [g % 2 * 2 + g // 2 for g in owners],
    )


def every_sum(place, keep, send, dim):
    return Sum(
        keep,
        send,
        [
            ("c", 1, 0, place.y),
            ("y", 1, dim, place.r),
            ("r", 1, dim, place.low),
            ("g", 1, dim, place.high),
            ("g", 2, None, None),
        ],
    )


def local(
    tokens,
    norm_attn,
    query_key_value_weight,
    attention_output_weight,
    norm_ffn,
    router,
    expert_in,
    expert_out,
    shared_gate_up_weight,
    shared_down_weight,
    block_lengths,
    routes,
    cotangent,
):
    place = Place()
    fast = place.lanes == 2 and place.rows_y == 2
    _, row_count, model_width = tokens.shape
    shard_index = lax.axis_index(DP)
    length = row_count * place.dp
    positions = shard_index * row_count + jnp.arange(row_count, dtype=jnp.int32)
    bounds = jnp.cumsum(block_lengths[0])
    cosine, sine = rope_table(positions)
    experts_total = router.shape[1]
    local_experts = expert_in.shape[1]
    groups = place.experts
    capacity = row_count * TOP * 5 // (4 * experts_total)
    chosen = routes[0]
    column = jnp.arange(experts_total, dtype=jnp.int32)
    picks = [(chosen[:, k : k + 1] == column[None, :]).astype(F32) for k in range(TOP)]
    flat_routes = chosen.reshape(row_count * TOP)
    route_hot = (flat_routes[:, None] == column[None, :]).astype(jnp.int32)
    earlier = jnp.cumsum(route_hot, axis=0) - route_hot
    slot_index = jnp.sum(earlier * route_hot, axis=1)
    partner = (flat_routes // local_experts) ^ lax.axis_index(EX)
    target = jnp.where(
        slot_index < capacity,
        (flat_routes % local_experts * groups + partner) * capacity + slot_index,
        -1,
    ).reshape(row_count, TOP)
    seats = jnp.arange(experts_total * capacity, dtype=jnp.int32)
    hots = [(target[:, k : k + 1] == seats[None, :]).astype(BF16) for k in range(TOP)]
    seated = [(target[:, k][None, :] == seats[:, None]).astype(BF16) for k in range(TOP)]
    upstream = cotangent[0]

    normalized_rows, own_q, own_kv = project(
        place, tokens[0], norm_attn, query_key_value_weight, cosine, sine
    )
    kv = trade(own_kv, "g")
    q = trade(own_q, "g")
    expert_in = jnp.transpose(expert_in, (1, 0, 2))
    expert_out = jnp.transpose(expert_out, (1, 0, 2))
    kv[1], expert_in, expert_out = lax.optimization_barrier((kv[1], expert_in, expert_out))
    if fast:
        kvs = kv + [swap(a, "r") for a in kv]
        lanes_of = [place.r, 1 - place.r]
    else:
        every_kv = [lax.all_gather(a, "r", axis=0, tiled=False) for a in kv]
        kvs = [a[i] for i in range(place.lanes) for a in every_kv]
        lanes_of = [jnp.int32(i) for i in range(place.lanes)]
    starts = (jnp.arange(place.groups, dtype=jnp.int32) * place.lanes + place.r) * row_count
    query_places = starts[:, None] + jnp.arange(row_count, dtype=jnp.int32)[None, :]
    limit = jnp.min(
        jnp.where(bounds[None, None, :] > query_places[:, :, None], bounds, length), axis=-1
    )
    span = row_count * place.lanes
    info = jnp.concatenate(
        [place.g[None], (jnp.max(limit, axis=1) + span - 1) // span, jnp.stack(lanes_of)]
    ).astype(jnp.int32)
    limit = limit[:, None, :]
    tables = [place.expert_table(model_width, lead) for lead in LEADS]
    shared_order = place.shared_table(model_width)
    q[0], *tables = lax.optimization_barrier((q[0], *tables, shared_order))
    *tables, shared_order = tables
    own_out, lse = attend(place, info, limit, q, kvs)
    traded_out = trade(own_out, "g")
    attended_low, middle, mixed_in, gates, send_rows, send_grads = middle_part(
        place,
        capacity,
        traded_out,
        tokens[0],
        upstream,
        attention_output_weight,
        norm_ffn,
        router,
        picks,
        seated,
    )
    arrived = trade(send_rows, EX)
    grad_arrived = trade(send_grads, EX)
    shared_result, shared_back, *shared_grads = ffn(
        True,
        place,
        shared_order,
        [mixed_in],
        [upstream],
        shared_gate_up_weight[None],
        shared_down_weight[None],
        0,
    )
    came_back, parts = [], []
    behind = [shared_result]
    if fast:
        shared_in = every_sum(place, *shared_grads[:2], 1)
        shared_out = every_sum(place, *shared_grads[2:], 1)
    for e in range(local_experts):
        own = [after(arrived[0], *behind)] + arrived[1:]
        results = ffn(
            False,
            place,
            tables[e],
            own,
            grad_arrived,
            expert_in,
            expert_out,
            e,
        )
        behind = [results[0]]
        came_back.append(trade(results[:groups], EX))
        parts.append(results[groups:])
    rets = [a for back in came_back for a in back]
    if fast:
        sums = [
            [expert_sum(place, *parts[e][k : k + 2], "r") for k in (0, 2)]
            + [expert_sum(place, *parts[e][4:], LEADS[e])]
            for e in range(local_experts)
        ]
        (first, second, third), (fourth, fifth, sixth) = sums
        both_done = parts[-1][0]
        first.begin()
        third.begin()
        second.begin(both_done)
        sixth.begin(both_done)
        shared_out.begin().end(both_done)
        shared_in.begin().end(both_done)
        first.end(both_done)
        third.end(both_done)
        shared_out.begin(rets[-1])
        shared_in.begin(rets[-1])
        rets[-1] = after(rets[-1], first.keep, third.keep, shared_in.keep, shared_out.keep)
    output, grad_middle, grad_attn_low, own_grad, grad_norm_ffn, grad_router = combine(
        place,
        hots,
        rets,
        gates,
        picks,
        upstream,
        middle,
        shared_result,
        shared_back,
        mixed_in,
        router,
        norm_ffn,
        attention_output_weight,
    )
    flat = lambda x: to_flat(place, x)
    own_grad = trade(own_grad, "g")
    if fast:
        third.begin()
        first.begin(own_grad[1])
        sixth.end(grad_middle).begin()
        second.end(grad_middle).begin(own_grad[1])
        own_grad[0] = after(own_grad[0], second.send, sixth.keep, shared_out.came)
    own_dq, own_dkv = attend_back(place, info, limit, lse, q, own_out, own_grad, kvs)
    dq = trade(own_dq, "g")
    grad_attn_low, own_dq[0] = lax.optimization_barrier((grad_attn_low, own_dq[0]))
    extra = beside(
        place,
        in_two(flat(grad_norm_ffn)[0]),
        flat(grad_router).T.reshape(model_width, groups, local_experts),
    )
    sides_out = weight_grad(place, flat(attended_low), grad_attn_low, extra)
    if fast:
        went_back = own_dkv[0]
        came = swap(after(own_dkv[1], first.came), "r")
        first.end(went_back).begin(dq[2], dq[3])
        third.end(went_back)
        sixth.end(went_back)
        came = after(came, second.came, sixth.send, third.send, first.came, *dq[1:])
        fourth.begin(came)
        fifth.begin(came)
        dkv = [add(own_dkv[0][d], came[d]) for d in range(place.groups)]
    else:
        dkv = [
            scatter(jnp.stack([a[d] for a in own_dkv]), "r", 0)[0] for d in range(place.groups)
        ]
    dkv = trade(dkv, "g")
    if fast:
        sum_out = direct_sum(place, *sides_out).begin()
        sixth.begin(dkv[1])
        third.begin(dkv[1])
        second.end(dkv[1]).begin()
        dkv[0] = after(dkv[0], fourth.came, shared_in.came, sum_out.came)
    grad_projected, grad_input, grad_norm_attn = finish(
        place,
        dq,
        dkv,
        query_key_value_weight,
        cosine,
        sine,
        tokens[0],
        norm_attn,
        grad_middle,
    )
    extra = beside(place, in_two(flat(grad_norm_attn)[0]), None)
    right = grad_projected
    if fast:
        fourth.end(grad_projected).begin()
        shared_in.end(grad_projected)
        shared_out.end(grad_projected)
        sum_out.end(grad_projected).begin()
        right = after(
            grad_projected, fifth.came, fourth.send, shared_in.send, shared_out.send, sum_out.came,
            sixth.came, second.came,
        )
    sides_qkv = weight_grad(place, flat(normalized_rows), right, extra)
    if fast:
        sum_qkv = direct_sum(place, *sides_qkv).begin()
        shared_in.begin()
        shared_out.begin(shared_in.send)
        sum_out.end(right).begin()
        fifth.end(right).begin()
        sum_qkv.end(right).begin()
        fourth.end(sum_qkv.send).begin()
        for chunk in (first, second, third, sixth):
            chunk.end(sum_qkv.send)
        sum_out.end(sum_qkv.send).begin()
        sum_qkv.end(shared_in.came).begin(shared_out.came, fourth.came)
        for chunk in (fifth, shared_in, shared_out):
            chunk.end(sum_qkv.send).begin()
        sum_qkv.end().begin(fifth.came, shared_in.came, shared_out.came)
        for chunk in (shared_in, shared_out):
            chunk.end(sum_qkv.send[0]).begin()
        for chunk in (fourth, fifth, sum_out):
            chunk.end(*sum_qkv.came)
        in_grads = [[s.finish() for s in row[:2]] for row in sums]
        out_grads = [row[2].finish() for row in sums]
        sum_shared_in, sum_shared_out = shared_in.finish()[0], shared_out.finish()
        sum_out, sum_qkv = sum_out.finish()[0], sum_qkv.finish()[0]
    else:
        in_grads = [
            [reduce_experts(place, *part[k : k + 2]) for k in (0, 2)] for part in parts
        ]
        out_grads = [reduce_experts(place, *part[4:]) for part in parts]
        sum_shared_in = reduce_shared_in(place, *shared_grads[:2])
        sum_shared_out = reduce_shared_out(place, *shared_grads[2:])
        sum_out, sum_qkv = reduce_weight(place, *sides_out), reduce_weight(place, *sides_qkv)
    own = model_width // place.experts
    sum_out, small = sum_out[:, :own], sum_out[:, own:]
    sum_norm_ffn, sum_router = small[:, 0] + small[:, 1], small[:, 2 : 2 + local_experts]
    sum_qkv, small = sum_qkv[:, : 3 * own], sum_qkv[:, 3 * own :]
    sum_norm_attn = small[:, 0] + small[:, 1]
    part_in = jnp.stack([jnp.concatenate(g, axis=1) for g in in_grads], axis=1)
    part_out = jnp.stack(out_grads, axis=1)
    return (
        output[None],
        grad_input[None],
        sum_norm_attn,
        sum_qkv,
        sum_out,
        sum_norm_ffn,
        sum_router,
        part_in,
        part_out,
        sum_shared_in,
        sum_shared_out.T,
    )


def solution(mesh):
    dp, experts = mesh.shape["dp"], mesh.shape["expert"]
    finer = Mesh(mesh.devices.reshape(4, dp // 4, experts // 2, 2), ("g", "r", "y", "c"))
    whole = P()
    return jax.shard_map(
        local,
        mesh=finer,
        in_specs=(
            P(EX, DP, None),
            whole,
            whole,
            whole,
            whole,
            whole,
            P(None, EX, None),
            P(None, EX, None),
            whole,
            whole,
            P(EX, None),
            P(EX, DP, None),
            P(EX, DP, None),
        ),
        out_specs=(
            P(EX, DP, None),
            P(EX, DP, None),
            P(DP),
            P(DP, EX),
            P(DP, EX),
            P(DP),
            P(DP, EX),
            P(DP, EX, None),
            P(DP, EX, None),
            P(DP, EX),
            P(DP, EX),
        ),
        check_vma=False,
    )
```

```python
import functools

import jax
import jax.numpy as jnp
from jax import lax
from jax.experimental import pallas as pl
from jax.experimental.pallas import tpu as pltpu
from jax.sharding import Mesh
from jax.sharding import PartitionSpec as P

HEADS = 12
HEAD_DIM = 64
TOP = 2
EPS = 1e-06
NEG = -1e30
F32 = jnp.float32
BF16 = jnp.bfloat16
STEPS = 8
DP = ("g", "r")
EX = ("y", "c")
LEADS = ("g", "g")
VMEM = 56 * 1024 * 1024


def takes(microseconds):
    return pl.CostEstimate(
        flops=int(microseconds * 1.15e9), bytes_accessed=1024, transcendentals=0
    )


def rope_table(positions):
    lane = jnp.arange(2 * HEAD_DIM, dtype=jnp.int32) % HEAD_DIM
    half_dim = HEAD_DIM // 2
    frequency = 10000.0 ** (-(lane % half_dim).astype(F32) * 2.0 / HEAD_DIM)
    angles = positions.astype(F32)[:, None] * frequency[None, :]
    return jnp.cos(angles), jnp.sin(angles) * jnp.where(lane < half_dim, -1.0, 1.0)


def rms_scale(hidden):
    return lax.rsqrt(jnp.mean(hidden * hidden, axis=-1, keepdims=True) + EPS)


def rms_back(hidden, scale_rows, gain_vector, upstream):
    normed_grad = upstream * gain_vector
    inner_mean = jnp.mean(normed_grad * hidden, axis=-1, keepdims=True)
    return scale_rows * normed_grad - hidden * scale_rows**3 * inner_mean


class Place:
    def __init__(self):
        self.groups, self.lanes = lax.axis_size("g"), lax.axis_size("r")
        self.rows_y = lax.axis_size("y")
        self.dp = self.groups * self.lanes
        self.experts = self.rows_y * 2
        self.g, self.r = lax.axis_index("g"), lax.axis_index("r")
        self.y, self.c = lax.axis_index("y"), lax.axis_index("c")
        self.low, self.high = self.g % 2, self.g // 2

    def own(self, b):
        g, r = b // self.lanes, b % self.lanes
        low, high = g % 2, g // 2
        if self.lanes == 2:
            return r ^ self.r, low * 2 + high
        return low ^ self.low, high * self.lanes + r

    def flat(self, b):
        g, r = b // self.lanes, b % self.lanes
        if self.lanes == 2:
            return r * 4 + (g % 2) * 2 + g // 2
        return (g % 2 * 2 + g // 2) * self.lanes + r

    def expert_table(self, width, lead):
        sub = STEPS // 4
        order = []
        for pos in range(STEPS):
            half, rest = pos // 4, pos % 4
            if self.lanes == 2 and lead == "r":
                low, high, part = rest // 2, rest % 2, half ^ self.r
            elif self.lanes == 2:
                low, high, part = half ^ self.low, rest % 2, rest // 2
            else:
                low, high, part = half ^ self.low, rest // 2, rest % 2
            order.append((high * 2 + low) * sub + part)
        block = width // self.dp
        rows = []
        for b in range(self.dp):
            half, rest = self.own(b)
            rows.append(half * (width // 2) + rest * block)
        return jnp.stack([jnp.asarray(v, jnp.int32) for v in order + [0] * STEPS + rows])

    def shared_table(self, width):
        per = 16 // self.experts
        order, columns = [], []
        sub = STEPS // 4
        for pos in range(STEPS):
            half, rest = pos // 4, pos % 4
            j = (rest // per * 2 + (half ^ self.c)) * per + rest % per
            order.append(j)
            g, part = j // sub, j % sub
            if self.lanes == 2:
                columns.append(part * 4 + g % 2 * 2 + g // 2)
            else:
                columns.append((g % 2 * 2 + g // 2) * sub + part)
        block = width // self.dp
        rows = [self.flat(b) * block for b in range(self.dp)]
        own = width // self.experts
        turned = [
            (e % 2 ^ self.c) * (width // 2) + e // 2 * own for e in range(self.experts)
        ]
        return jnp.stack(
            [jnp.asarray(v, jnp.int32) for v in order + columns + rows + turned]
        )


def nt(a, b):
    return lax.dot_general(a, b, (((1,), (1,)), ((), ())), preferred_element_type=F32)


def nn(a, b):
    return lax.dot_general(a, b, (((1,), (0,)), ((), ())), preferred_element_type=F32)


def turn(x, cosine, sine):
    width = x.shape[1]
    lane = lax.broadcasted_iota(jnp.int32, x.shape, 1) % HEAD_DIM
    other = jnp.where(
        lane < HEAD_DIM // 2,
        pltpu.roll(x, width - HEAD_DIM // 2, 1),
        pltpu.roll(x, HEAD_DIM // 2, 1),
    )
    times = width // cosine.shape[1]
    cosine = jnp.concatenate([cosine] * times, axis=1)
    sine = jnp.concatenate([sine] * times, axis=1)
    return x * cosine + other * sine


def project_kernel(here, x_ref, gain_ref, w_ref, cos_ref, sin_ref, normed_ref, *refs):
    step = pl.program_id(0)
    groups = (len(refs) - 2) // 2
    q_refs, kv_refs, (q_all, kv_all) = refs[:groups], refs[groups:-2], refs[-2:]
    half, three = x_ref.shape[0] // 2, 3 * HEAD_DIM

    @pl.when(step == 0)
    def _():
        x = x_ref[...].astype(F32)
        normed_ref[...] = (x * rms_scale(x) * gain_ref[...]).astype(BF16)

    part = nn(normed_ref[...], w_ref[...])

    @pl.when(step == 0)
    def _():
        pack_heads(turn(part, cos_ref[...], sin_ref[...]) * HEAD_DIM**-0.5, q_all)

    @pl.when(step == 1)
    def _():
        k = turn(part, cos_ref[...], sin_ref[...])
        for g in range(groups):
            own = k[:, g * three : (g + 1) * three].astype(BF16)
            kv_all[g, :, 0:128] = own[:, :128]
            kv_all[g, :, 256:320] = own[:, 128:]

    @pl.when(step == 2)
    def _():
        for g in range(groups):
            own = part[:, g * three : (g + 1) * three].astype(BF16)
            kv_all[g, :, 128:256] = own[:, :128]
            kv_all[g, :, 320:384] = own[:, 128:]
        for d in range(groups):
            q_refs[d][...] = q_all[here[0] ^ d]
            kv_refs[d][...] = kv_all[here[0] ^ d]


def pack_heads(rows, packed_ref):
    half, three = rows.shape[0] // 2, 3 * HEAD_DIM
    for g in range(packed_ref.shape[0]):
        own = rows[:, g * three : (g + 1) * three].astype(BF16)
        packed_ref[g, :, 0:128] = own[:half, :128]
        packed_ref[g, :, 128:256] = own[half:, :128]
        packed_ref[g, :, 256:320] = own[:half, 128:]
        packed_ref[g, :, 320:384] = own[half:, 128:]


def project(place, x, gain, weight, cosine, sine):
    rows, width = x.shape
    groups = place.groups
    sds = jax.ShapeDtypeStruct
    whole = lambda *shape: pl.BlockSpec(shape, lambda i, t: (0,) * len(shape))
    normed, *parts = pl.pallas_call(
        project_kernel,
        out_shape=(sds((rows, width), BF16),)
        + (sds((rows // 2, 384), BF16),) * groups
        + (sds((rows, 384), BF16),) * groups,
        grid_spec=pltpu.PrefetchScalarGridSpec(
            num_scalar_prefetch=1,
            grid=(3,),
            in_specs=[
                whole(rows, width),
                whole(1, width),
                pl.BlockSpec((width, width), lambda i, t: (0, i)),
                whole(rows, 128),
                whole(rows, 128),
            ],
            out_specs=(whole(rows, width),)
            + (whole(rows // 2, 384),) * groups
            + (whole(rows, 384),) * groups,
            scratch_shapes=[
                pltpu.VMEM((groups, rows // 2, 384), BF16),
                pltpu.VMEM((groups, rows, 384), BF16),
            ],
        ),
        compiler_params=pltpu.CompilerParams(vmem_limit_bytes=VMEM),
        cost_estimate=takes(4),
    )(place.g[None], x, gain[None], weight, cosine, sine)
    return normed, parts[:groups], parts[groups:]


def unpack(packed, second_low):
    half = packed.shape[0]
    x = packed.astype(F32)
    lane = lax.broadcasted_iota(jnp.int32, (half, 128), 1)
    low = lane < HEAD_DIM
    first, second, third = x[:, 0:128], x[:, 128:256], x[:, 256:384]
    turned = pltpu.roll(third, HEAD_DIM, 1)
    zero = jnp.zeros_like(third)
    pair = [
        jnp.where(low, first, zero),
        jnp.where(low, second, zero),
        jnp.where(low, zero, first),
        jnp.where(low, zero, second),
    ]
    if second_low:
        single = [jnp.where(low, third, zero), jnp.where(low, turned, zero)]
    else:
        single = [jnp.where(low, zero, turned), jnp.where(low, zero, third)]
    return (
        jnp.concatenate(pair, axis=0).astype(BF16),
        jnp.concatenate(single, axis=0).astype(BF16),
    )


def visible_keys(kz, source, lanes, rows, limit):
    first = (kz * lanes + source) * rows
    place = first + lax.broadcasted_iota(jnp.int32, (rows, limit.shape[1]), 0)
    return place < limit


def attend_kernel(sources, shards, lanes, info, limit_ref, *refs):
    q_refs, kv_refs = refs[:shards], refs[shards : shards * (1 + sources)]
    out_refs, (lse_ref, q_ref, kv_all, turned, out_ref) = refs[shards * (1 + sources) : -5], refs[-5:]
    half = q_ref.shape[1]
    rows = 2 * half
    gather_heads(info, q_refs, q_ref)
    gather_keys(info, shards, kv_refs, kv_all, turned)

    def shard(z, carry):
        pair, single = unpack(q_ref[z], True)
        limit = limit_ref[z]

        def step(kz, state):
            largest, total, acc_pair, acc_single = state
            scores = []
            for s in range(sources):
                keep = visible_keys(kz, info[1 + shards + s], lanes, rows, limit)
                two = nt(kv_all[s, kz, :, 0:128], pair)
                one = nt(kv_all[s, kz, :, 256:384], single)
                both = jnp.concatenate([two, one], axis=1)
                keep = jnp.concatenate([keep] * 3, axis=1)
                scores.append(jnp.where(keep, both, NEG))
            newest = largest
            for sc in scores:
                newest = jnp.maximum(newest, jnp.max(sc, axis=0, keepdims=True))
            fade = jnp.exp(largest - newest)
            total = total * fade
            acc_pair = acc_pair * fade[:, : 2 * rows]
            acc_single = acc_single * fade[:, 2 * rows :]
            for s, sc in enumerate(scores):
                power = jnp.exp(sc - newest)
                total = total + jnp.sum(power, axis=0, keepdims=True)
                power = power.astype(BF16)
                acc_pair = acc_pair + nn(turned[s, kz, 128:256, :], power[:, : 2 * rows])
                acc_single = acc_single + nn(turned[s, kz, 256:384, :], power[:, 2 * rows :])
            return newest, total, acc_pair, acc_single

        largest, total, acc_pair, acc_single = lax.fori_loop(
            0,
            info[1 + z],
            step,
            (
                jnp.full((1, 3 * rows), NEG, F32),
                jnp.zeros((1, 3 * rows), F32),
                jnp.zeros((128, 2 * rows), F32),
                jnp.zeros((128, rows), F32),
            ),
        )
        lse_ref[z] = largest + jnp.log(total)
        share = 1.0 / total
        first = acc_pair[:HEAD_DIM, :rows] * share[:, :rows]
        second = acc_pair[HEAD_DIM:, rows:] * share[:, rows : 2 * rows]
        third = acc_single[HEAD_DIM:] * share[:, 2 * rows :]
        packed = jnp.concatenate(
            [a[:, part] for part in (slice(0, half), slice(half, rows)) for a in (first, second)]
            + [third[:, :half], third[:, half:]],
            axis=0,
        )
        out_ref[z] = packed.T.astype(BF16)
        return carry

    lax.fori_loop(0, shards, shard, 0)


    for d in range(shards):
        out_refs[d][...] = out_ref[info[0] ^ d]


def gather_heads(info, refs, packed_ref):
    for d, ref in enumerate(refs):
        packed_ref[info[0] ^ d] = ref[...]


def gather_keys(info, shards, refs, kv_all, turned):
    for i, ref in enumerate(refs):
        at = info[0] ^ (i % shards)
        kv_all[i // shards, at] = ref[...]
        turned[i // shards, at] = ref[...].astype(F32).T.astype(BF16)


def attend(place, info, limit, qs, kvs):
    half, lanes = qs[0].shape
    shards, sources = len(qs), len(kvs) // len(qs)
    vmem = pl.BlockSpec(memory_space=pltpu.VMEM)
    sds = jax.ShapeDtypeStruct
    *outs, lse = pl.pallas_call(
        functools.partial(attend_kernel, sources, shards, place.lanes),
        out_shape=(sds((half, lanes), BF16),) * shards + (sds((shards, 1, 6 * half), F32),),
        in_specs=[pl.BlockSpec(memory_space=pltpu.SMEM)] + [vmem] * (1 + shards * (1 + sources)),
        out_specs=(vmem,) * (shards + 1),
        scratch_shapes=[
            pltpu.VMEM((shards, half, lanes), BF16),
            pltpu.VMEM((sources, shards, 2 * half, lanes), BF16),
            pltpu.VMEM((sources, shards, lanes, 2 * half), BF16),
            pltpu.VMEM((shards, half, lanes), BF16),
        ],
        compiler_params=pltpu.CompilerParams(vmem_limit_bytes=VMEM),
        cost_estimate=takes(12),
    )(info, limit, *qs, *kvs)
    return outs, lse


def attend_back_kernel(sources, shards, lanes, info, limit_ref, lse_ref, *refs):
    q_refs, o_refs, g_refs = (refs[i * shards : (i + 1) * shards] for i in range(3))
    kv_refs = refs[3 * shards : (3 + sources) * shards]
    dq_refs = refs[(3 + sources) * shards : (4 + sources) * shards]
    dkv_refs = refs[(4 + sources) * shards : (4 + sources) * shards + sources]
    q_ref, out_ref, grad_ref, dq_ref, kv_all, turned, total = refs[-7:]
    half = q_ref.shape[1]
    rows = 2 * half
    gather_heads(info, q_refs, q_ref)
    gather_heads(info, o_refs, out_ref)
    gather_heads(info, g_refs, grad_ref)
    gather_keys(info, shards, kv_refs, kv_all, turned)
    total[...] = jnp.zeros_like(total)

    def shard(z, carry):
        pair, single = unpack(q_ref[z], True)
        grad_pair, grad_single = unpack(grad_ref[z], False)
        limit, lse = limit_ref[z], lse_ref[z]
        product = (grad_ref[z].astype(F32) * out_ref[z].astype(F32)).T
        sums = [
            jnp.sum(product[i * HEAD_DIM : (i + 1) * HEAD_DIM], axis=0, keepdims=True)
            for i in range(6)
        ]
        delta = jnp.concatenate([sums[0], sums[2], sums[1], sums[3], sums[4], sums[5]], axis=1)

        def step(kz, state):
            dq_pair, dq_single = state
            for s in range(sources):
                keep = visible_keys(kz, info[1 + shards + s], lanes, rows, limit)
                keep = jnp.concatenate([keep] * 3, axis=1)
                k01, v01 = kv_all[s, kz, :, 0:128], kv_all[s, kz, :, 128:256]
                kv2 = kv_all[s, kz, :, 256:384]
                scores = jnp.concatenate([nt(k01, pair), nt(kv2, single)], axis=1)
                grads = jnp.concatenate([nt(v01, grad_pair), nt(kv2, grad_single)], axis=1)
                power = jnp.where(keep, jnp.exp(scores - lse), 0.0)
                slope = (power * (grads - delta)).astype(BF16)
                power = power.astype(BF16)
                dq_pair = dq_pair + nn(turned[s, kz, 0:128, :], slope[:, : 2 * rows])
                dq_single = dq_single + nn(turned[s, kz, 256:384, :], slope[:, 2 * rows :])
                total[s, kz, :, 0:128] += nn(slope[:, : 2 * rows], pair)
                total[s, kz, :, 128:256] += nn(power[:, : 2 * rows], grad_pair)
                total[s, kz, :, 256:384] += nn(slope[:, 2 * rows :], single) + nn(
                    power[:, 2 * rows :], grad_single
                )
            return dq_pair, dq_single

        dq_pair, dq_single = lax.fori_loop(
            0,
            info[1 + z],
            step,
            (jnp.zeros((128, 2 * rows), F32), jnp.zeros((128, rows), F32)),
        )
        first, second = dq_pair[:HEAD_DIM, :rows], dq_pair[HEAD_DIM:, rows:]
        third = dq_single[:HEAD_DIM]
        packed = jnp.concatenate(
            [a[:, part] for part in (slice(0, half), slice(half, rows)) for a in (first, second)]
            + [third[:, :half], third[:, half:]],
            axis=0,
        )
        dq_ref[z] = packed.T.astype(BF16)
        return carry

    lax.fori_loop(0, shards, shard, 0)
    for d in range(shards):
        dq_refs[d][...] = dq_ref[info[0] ^ d]
    for s, ref in enumerate(dkv_refs):
        for d in range(shards):
            ref[d] = total[s, info[0] ^ d].astype(BF16)


def attend_back(place, info, limit, lse, qs, outs, grads, kvs):
    half, lanes = qs[0].shape
    shards, sources = len(qs), len(kvs) // len(qs)
    vmem = pl.BlockSpec(memory_space=pltpu.VMEM)
    sds = jax.ShapeDtypeStruct
    parts = pl.pallas_call(
        functools.partial(attend_back_kernel, sources, shards, place.lanes),
        out_shape=(sds((half, lanes), BF16),) * shards
        + (sds((shards, 2 * half, lanes), BF16),) * sources,
        in_specs=[pl.BlockSpec(memory_space=pltpu.SMEM)] + [vmem] * (2 + shards * (3 + sources)),
        out_specs=(vmem,) * (shards + sources),
        scratch_shapes=[pltpu.VMEM((shards, half, lanes), BF16)] * 4
        + [
            pltpu.VMEM((sources, shards, 2 * half, lanes), BF16),
            pltpu.VMEM((sources, shards, lanes, 2 * half), BF16),
            pltpu.VMEM((sources, shards, 2 * half, lanes), F32),
        ],
        compiler_params=pltpu.CompilerParams(vmem_limit_bytes=VMEM),
        cost_estimate=takes(19),
    )(info, limit, lse, *qs, *outs, *grads, *kvs)
    return list(parts[:shards]), parts[shards:]


def finish_kernel(
    here, w_ref, cos_ref, sin_ref, x_ref, gain_ref, middle_ref, *refs,
):
    groups = (len(refs) - 6) // 2
    dq_refs, dkv_refs = refs[:groups], refs[groups : 2 * groups]
    projected_ref, input_ref, norm_ref, dq_all, dkv_all, gather = refs[2 * groups :]
    rows, width = x_ref.shape
    half, three = rows // 2, 3 * HEAD_DIM
    for d in range(groups):
        dq_all[here[0] ^ d] = dq_refs[d][...].astype(F32)
        dkv_all[here[0] ^ d] = dkv_refs[d][...].astype(F32)
    for g in range(groups):
        at = g * three
        dq, dkv = dq_all[g], dkv_all[g]
        gather[0, :half, at : at + 128] = dq[:, 0:128]
        gather[0, half:, at : at + 128] = dq[:, 128:256]
        gather[0, :half, at + 128 : at + three] = dq[:, 256:320]
        gather[0, half:, at + 128 : at + three] = dq[:, 320:384]
        gather[1, :, at : at + 128] = dkv[:, 0:128]
        gather[1, :, at + 128 : at + three] = dkv[:, 256:320]
        gather[2, :, at : at + 128] = dkv[:, 128:256]
        gather[2, :, at + 128 : at + three] = dkv[:, 320:384]
    cosine, sine = cos_ref[...], -sin_ref[...]
    parts = [
        (turn(gather[0], cosine, sine) * HEAD_DIM**-0.5).astype(BF16),
        turn(gather[1], cosine, sine).astype(BF16),
        gather[2].astype(BF16),
    ]
    grad = jnp.zeros((rows, width), F32)
    for i, part in enumerate(parts):
        projected_ref[:, i * width : (i + 1) * width] = part
        grad = grad + nt(part, w_ref[:, i * width : (i + 1) * width])
    x = x_ref[...].astype(F32)
    scale = rms_scale(x)
    norm_ref[...] = jnp.sum(grad * x * scale, axis=0, keepdims=True)
    input_ref[...] = middle_ref[...] + rms_back(x, scale, gain_ref[...], grad)


def finish(place, dqs, dkvs, weight, cosine, sine, x, gain, middle):
    rows, width = x.shape
    groups = place.groups
    vmem = pl.BlockSpec(memory_space=pltpu.VMEM)
    return pl.pallas_call(
        finish_kernel,
        out_shape=(
            jax.ShapeDtypeStruct((rows, 3 * width), BF16),
            jax.ShapeDtypeStruct((rows, width), F32),
            jax.ShapeDtypeStruct((1, width), F32),
        ),
        in_specs=[pl.BlockSpec(memory_space=pltpu.SMEM)] + [vmem] * (6 + 2 * groups),
        out_specs=(vmem,) * 3,
        scratch_shapes=[
            pltpu.VMEM((groups, rows // 2, 384), F32),
            pltpu.VMEM((groups, rows, 384), F32),
            pltpu.VMEM((3, rows, width), F32),
        ],
        compiler_params=pltpu.CompilerParams(vmem_limit_bytes=VMEM),
        cost_estimate=takes(5),
    )(place.g[None], weight, cosine, sine, x, gain[None], middle, *dqs, *dkvs)


def middle_kernel(
    here, x_ref, grad_ref, w_ref, gain_ref, router_ref, pick0, pick1, seat0, seat1, *refs,
):
    groups = 4
    o_refs = refs[:groups]
    low_ref, middle_ref, mixed_ref, gate_ref = refs[groups : groups + 4]
    sent = refs[groups + 4 : -2]
    o_all, gather = refs[-2:]
    count = len(sent) // 2
    half, three = x_ref.shape[0] // 2, 3 * HEAD_DIM
    for d in range(groups):
        o_all[here[0] ^ d] = o_refs[d][...].astype(F32)
    for g in range(groups):
        at = g * three
        gather[:half, at : at + 128] = o_all[g, :, 0:128]
        gather[half:, at : at + 128] = o_all[g, :, 128:256]
        gather[:half, at + 128 : at + three] = o_all[g, :, 256:320]
        gather[half:, at + 128 : at + three] = o_all[g, :, 320:384]
    low = gather[...].astype(BF16)
    low_ref[...] = low
    middle = x_ref[...].astype(F32) + nn(low, w_ref[...])
    middle_ref[...] = middle
    mixed = (middle * rms_scale(middle) * gain_ref[...]).astype(BF16)
    mixed_ref[...] = mixed
    scores = nn(mixed, router_ref[...])
    picked = [jnp.sum(scores * p[...], axis=1, keepdims=True) for p in (pick0, pick1)]
    largest = jnp.maximum(*picked)
    powers = [jnp.exp(p - largest) for p in picked]
    gates = [p / (powers[0] + powers[1]) for p in powers]
    gate_ref[...] = jnp.concatenate(gates, axis=1)
    seats = (seat0[...], seat1[...])
    held = jnp.zeros((seats[0].shape[0], 1), F32)
    for seat, gate in zip(seats, gates):
        high = gate.astype(BF16)
        rest = (gate - high.astype(F32)).astype(BF16)
        held = held + jnp.sum(nn(seat, jnp.concatenate([high, rest], axis=1)), axis=1, keepdims=True)
    every = seats[0] + seats[1]
    rows = nn(every, mixed).astype(BF16)
    grads = (nn(every, grad_ref[...]) * held).astype(BF16)
    capacity = sent[0].shape[1]
    for d in range(count):
        for e in range(sent[0].shape[0]):
            at = (e * count + d) * capacity
            sent[d][e] = rows[at : at + capacity]
            sent[count + d][e] = grads[at : at + capacity]


def middle_part(place, capacity, outs, x, grad, weight, gain, router, picks, seats):
    rows, width = x.shape
    groups, count = place.groups, place.experts
    local = router.shape[1] // count
    vmem = pl.BlockSpec(memory_space=pltpu.VMEM)
    sds = jax.ShapeDtypeStruct
    low, middle, mixed, gates, *sent = pl.pallas_call(
        middle_kernel,
        out_shape=(
            sds((rows, width), BF16),
            sds((rows, width), F32),
            sds((rows, width), BF16),
            sds((rows, TOP), F32),
        )
        + (sds((local, capacity, width), BF16),) * (2 * count),
        in_specs=[pl.BlockSpec(memory_space=pltpu.SMEM)] + [vmem] * (9 + groups),
        out_specs=(vmem,) * (4 + 2 * count),
        scratch_shapes=[
            pltpu.VMEM((groups, rows // 2, 384), F32),
            pltpu.VMEM((rows, width), F32),
        ],
        compiler_params=pltpu.CompilerParams(vmem_limit_bytes=VMEM),
        cost_estimate=takes(4),
    )(place.g[None], x, grad, weight, gain[None], router, *picks, *seats, *outs)
    return low, middle, mixed, gates, sent[:count], sent[count:]


def trade(parts, axis):
    size = lax.axis_size(axis)
    return [parts[0]] + [
        lax.ppermute(parts[d], axis, [(i, i ^ d) for i in range(size)]) for d in range(1, size)
    ]


def ffn_kernel(shared, count, dp, experts, table, *refs):
    x_refs, dy_refs, (gate_ref, up_ref, down_ref) = refs[:count], refs[count : 2 * count], refs[2 * count : 2 * count + 3]
    refs = refs[2 * count + 3 :]
    if shared:
        result, back, in_keep, in_send, out_keep, out_send, stage, turned, turned_dy = refs
        x_ref, dy_ref = x_refs[0], dy_refs[0]
    else:
        both, refs = refs[:count], refs[count:]
        gate_keep, gate_send, up_keep, up_send, out_keep, out_send = refs[:6]
        in_keep, in_send = (gate_keep, up_keep), (gate_send, up_send)
        stage, turned, result, back, x_ref, dy_ref = refs[6:]
    step = pl.program_id(0)
    width = x_ref.shape[1]
    rows = x_ref.shape[0]

    @pl.when(step == 0)
    def _():
        if not shared:
            part = rows // count
            for d in range(count):
                x_ref[d * part : (d + 1) * part] = x_refs[d][0]
                dy_ref[d * part : (d + 1) * part] = dy_refs[d][0]
        whole = x_ref[...].astype(F32).T
        block = width // dp
        for b in range(dp):
            start = pl.multiple_of(table[2 * STEPS + b], 8)
            stage[pl.ds(start, block), :] = whole[b * block : (b + 1) * block]
        turned[...] = stage[...].astype(BF16)
        if shared:
            whole = dy_ref[...].astype(F32).T
            block = width // experts
            for e in range(experts):
                start = pl.multiple_of(table[2 * STEPS + dp + e], 8)
                stage[pl.ds(start, block), :] = whole[e * block : (e + 1) * block]
            turned_dy[...] = stage[...].astype(BF16)
        result[...] = jnp.zeros_like(result)
        back[...] = jnp.zeros_like(back)

    x, dy = x_ref[...], dy_ref[...]
    w_gate, w_up, w_down = gate_ref[0], up_ref[0], down_ref[0]
    gate, up = nn(x, w_gate), nn(x, w_up)
    grad = nt(dy, w_down)
    sig = jax.nn.sigmoid(gate)
    silu = gate * sig
    act = (silu * up).astype(BF16)
    grad_gate = (grad * up * (sig * (1.0 + gate * (1.0 - sig)))).astype(BF16)
    grad_up = (grad * silu).astype(BF16)
    result[...] += nn(act, w_down)
    back[...] += nt(grad_gate, w_gate) + nt(grad_up, w_up)
    xt = turned[...]
    half = width // 2
    for k, upper in enumerate((grad_gate, grad_up)):
        grad_in = nn(xt, upper).astype(BF16)
        if shared:

            @pl.when(step < STEPS // 2)
            def _():
                in_keep[k] = grad_in

            @pl.when(step >= STEPS // 2)
            def _():
                in_send[k] = grad_in

        else:
            in_keep[k][...] = grad_in[:half]
            in_send[k][...] = grad_in[half:]
    if shared:
        grad_out = nn(turned_dy[...], act).astype(BF16)
        out_keep[...] = grad_out[:half]
        out_send[...] = grad_out[half:]
    else:
        grad_out = lax.dot_general(
            act, dy, (((0,), (0,)), ((), ())), preferred_element_type=F32
        ).astype(BF16)

        @pl.when(step < STEPS // 2)
        def _():
            out_keep[...] = grad_out

        @pl.when(step >= STEPS // 2)
        def _():
            out_send[...] = grad_out

        @pl.when(step == STEPS - 1)
        def _():
            part = rows // count
            for d in range(count):
                both[d][:, :width] = result[d * part : (d + 1) * part].astype(BF16)
                both[d][:, width:] = back[d * part : (d + 1) * part].astype(BF16)


def ffn(shared, place, table, xs, dys, w_in, w_out, e):
    count = len(xs)
    part, width = xs[0].shape[-2:]
    rows = part * count
    if shared:
        given = pl.BlockSpec((rows, width), lambda i, t: (0, 0))
    else:
        given = pl.BlockSpec((1, part, width), lambda i, t: (e, 0, 0))
    hidden = w_out.shape[1]
    chunk = hidden // STEPS
    near, far = STEPS // 2 - 1, STEPS // 2
    sds = jax.ShapeDtypeStruct
    first = lambda i, t: (0, 0, jnp.minimum(i, near))
    second = lambda i, t: (0, 0, jnp.maximum(i - far, 0))
    if shared:
        out_shape = (
            sds((rows, width), F32),
            sds((rows, width), F32),
            sds((2, width, hidden // 2), BF16),
            sds((2, width, hidden // 2), BF16),
            sds((width // 2, hidden), BF16),
            sds((width // 2, hidden), BF16),
        )
        out_specs = (
            pl.BlockSpec((rows, width), lambda i, t: (0, 0)),
            pl.BlockSpec((rows, width), lambda i, t: (0, 0)),
            pl.BlockSpec((2, width, chunk), first),
            pl.BlockSpec((2, width, chunk), second),
            pl.BlockSpec((width // 2, chunk), lambda i, t: (0, t[STEPS + i])),
            pl.BlockSpec((width // 2, chunk), lambda i, t: (0, t[STEPS + i])),
        )
        extra = [pltpu.VMEM((width, rows), BF16)]
    else:
        out_shape = (
            *[sds((part, 2 * width), BF16)] * count,
            *[sds((width // 2, hidden), BF16)] * 4,
            sds((hidden // 2, width), BF16),
            sds((hidden // 2, width), BF16),
        )
        out_specs = (
            *[pl.BlockSpec((part, 2 * width), lambda i, t: (0, 0))] * count,
            *[pl.BlockSpec((width // 2, chunk), lambda i, t: (0, t[i]))] * 4,
            pl.BlockSpec((chunk, width), lambda i, t: (jnp.minimum(i, near), 0)),
            pl.BlockSpec((chunk, width), lambda i, t: (jnp.maximum(i - far, 0), 0)),
        )
        extra = [pltpu.VMEM((rows, width), F32)] * 2 + [pltpu.VMEM((rows, width), BF16)] * 2
    return pl.pallas_call(
        functools.partial(ffn_kernel, shared, count, place.dp, place.experts),
        out_shape=out_shape,
        grid_spec=pltpu.PrefetchScalarGridSpec(
            num_scalar_prefetch=1,
            grid=(STEPS,),
            in_specs=[
                *[given] * (2 * count),
                pl.BlockSpec((1, width, chunk), lambda i, t: (e, 0, t[i])),
                pl.BlockSpec((1, width, chunk), lambda i, t: (e, 0, STEPS + t[i])),
                pl.BlockSpec((1, chunk, width), lambda i, t: (e, t[i], 0)),
            ],
            out_specs=out_specs,
            scratch_shapes=[pltpu.VMEM((width, rows), F32), pltpu.VMEM((width, rows), BF16)]
            + extra,
        ),
        compiler_params=pltpu.CompilerParams(vmem_limit_bytes=VMEM),
        cost_estimate=takes(18),
    )(table, *xs, *dys, w_in, w_in, w_out)


def swap(a, axis, bit=1):
    size = lax.axis_size(axis)
    return lax.ppermute(a, axis, [(i, i ^ bit) for i in range(size)])


def add(a, b, kind=BF16):
    return a + b if kind == BF16 else a.astype(F32) + b.astype(F32)


def half_of(a, dim, index):
    size = a.shape[dim] // 2
    return lax.dynamic_slice_in_dim(a, index * size, size, dim)


def exchange(keep, came, dim, mine):
    return [add(half_of(keep, dim, i), half_of(came, dim, i)) for i in (mine, 1 - mine)]


def scatter(a, axis, dim):
    return lax.psum_scatter(a, axis, scatter_dimension=dim, tiled=True)


def reduce_experts(place, keep, send):
    came = swap(send, "g", 1)
    keep, send = exchange(keep, came, 0, place.high)
    return scatter(add(keep, swap(send, "g", 2)), "r", 0).astype(F32)


def after(x, *values):
    return lax.optimization_barrier((x, *values))[0]


def reduce_tokens(place, keep, came, dim):
    keep, send = exchange(keep, came, dim, place.low)
    came = swap(send, "g", 1)
    keep, send = exchange(keep, came, dim, place.high)
    came = swap(send, "g", 2)
    return scatter(add(keep, came), "r", dim).astype(F32)


def reduce_shared_in(place, keep, send):
    total = add(keep, swap(send, "c"))
    two, width, columns = total.shape
    parts = place.rows_y // 2
    total = total.reshape(two, width, parts, columns // parts).transpose(0, 2, 1, 3)
    mine = scatter(total.reshape(two * parts, width, columns // parts), "y", 0)[0]
    return reduce_tokens(place, mine, jnp.zeros_like(mine), 0)


def reduce_shared_out(place, keep, send):
    mine = scatter(add(keep, swap(send, "c")), "y", 0)
    return reduce_tokens(place, mine, jnp.zeros_like(mine), 1)


def to_flat(place, x):
    rows, width = x.shape
    x = x.reshape(rows, 2, 2, place.lanes, width // place.dp)
    order = (0, 3, 2, 1, 4) if place.lanes == 2 else (0, 2, 1, 3, 4)
    return x.transpose(order).reshape(rows, width)


def weight_grad(place, left, right, extra):
    rows, columns = right.shape
    width = left.shape[1]
    own = columns // place.experts
    parts = right.reshape(rows, place.rows_y, 2, own)
    extra = extra.reshape(width, place.rows_y, 2, extra.shape[-1]).astype(BF16)
    keep, send = [
        jnp.concatenate(
            [
                lax.dot_general(
                    left,
                    lax.dynamic_index_in_dim(parts, i, 2, False).reshape(rows, columns // 2),
                    (((0,), (0,)), ((), ())),
                    preferred_element_type=F32,
                )
                .astype(BF16)
                .reshape(width, place.rows_y, own),
                lax.dynamic_index_in_dim(extra, i, 2, False),
            ],
            axis=2,
        ).transpose(1, 0, 2)
        for i in (place.c, 1 - place.c)
    ]
    return keep, send


def reduce_weight(place, keep, send):
    mine = scatter(add(keep, swap(send, "c")), "y", 0)[0]
    return reduce_tokens(place, mine, jnp.zeros_like(mine), 0)


def in_two(vector):
    high = vector.astype(BF16).astype(F32)
    return [high, vector - high]


def beside(place, columns, experts_of):
    width = columns[0].shape[0]
    every = jnp.stack(columns, axis=1)[:, None, :]
    every = jnp.broadcast_to(every, (width, place.experts, len(columns)))
    parts = [every] if experts_of is None else [every, experts_of]
    used = sum(p.shape[2] for p in parts)
    return jnp.concatenate(parts + [jnp.zeros((width, place.experts, 64 - used), F32)], axis=2)


def combine_kernel(
    here, hot0, hot1, gate_ref, pick0, pick1, grad_ref, middle_ref,
    shared_ref, back_ref, mixed_in_ref, router_ref, gain_ref, w_ref, *refs,
):
    output_ref, middle_grad_ref, low_ref, *head_refs = refs[-11:-4]
    norm_ref, router_grad_ref, returned, heads = refs[-4:]
    ret_refs = refs[:-11]
    width = grad_ref.shape[1]
    part = ret_refs[0].shape[0]
    for i, ref in enumerate(ret_refs):
        returned[i * part : (i + 1) * part] = ref[...]
    hots = (hot0[...], hot1[...])
    grad = grad_ref[...].astype(F32)
    middle = middle_ref[...]
    backs = [nn(h, returned[:, :width]) for h in hots]
    gates = [gate_ref[:, k : k + 1] for k in range(TOP)]
    routed = sum(gates[k] * backs[k] for k in range(TOP))
    output_ref[...] = (middle + routed + shared_ref[...]).astype(BF16)
    slopes = [jnp.sum(b * grad, axis=1, keepdims=True) for b in backs]
    inner = sum(gates[k] * slopes[k] for k in range(TOP))
    logits = sum(
        pick[...] * (gates[k] * (slopes[k] - inner)) for k, pick in enumerate((pick0, pick1))
    ).astype(BF16)
    router_grad_ref[...] = lax.dot_general(
        logits, mixed_in_ref[...], (((0,), (0,)), ((), ())), preferred_element_type=F32
    )
    mixed = back_ref[...] + nn(logits, router_ref[...]) + nn(hots[0] + hots[1], returned[:, width:])
    scale = rms_scale(middle)
    norm_ref[...] = jnp.sum(mixed * middle * scale, axis=0, keepdims=True)
    middle_grad = grad + rms_back(middle, scale, gain_ref[...], mixed)
    middle_grad_ref[...] = middle_grad
    low = middle_grad.astype(BF16)
    low_ref[...] = low
    pack_heads(nt(low, w_ref[...]), heads)
    for d, ref in enumerate(head_refs):
        ref[...] = heads[here[0] ^ d]


def combine(place, hots, rets, gates, picks, grad, middle, shared, back, mixed_in, router, gain, weight):
    rows, width = grad.shape
    vmem = pl.BlockSpec(memory_space=pltpu.VMEM)
    sds = jax.ShapeDtypeStruct
    output, middle_grad, low, *heads, norm, router_grad = pl.pallas_call(
        combine_kernel,
        out_shape=(
            sds((rows, width), BF16),
            sds((rows, width), F32),
            sds((rows, width), BF16),
        )
        + (sds((rows // 2, 384), BF16),) * place.groups
        + (
            sds((1, width), F32),
            sds((router.shape[1], width), F32),
        ),
        in_specs=[pl.BlockSpec(memory_space=pltpu.SMEM)] + [vmem] * (13 + len(rets)),
        out_specs=(vmem,) * (5 + place.groups),
        scratch_shapes=[
            pltpu.VMEM((hots[0].shape[1], 2 * width), BF16),
            pltpu.VMEM((place.groups, rows // 2, 384), BF16),
        ],
        compiler_params=pltpu.CompilerParams(vmem_limit_bytes=VMEM),
        cost_estimate=takes(5),
    )(
        place.g[None], *hots, gates, *picks, grad, middle, shared, back, mixed_in,
        router.T, gain[None], weight, *rets,
    )
    return output, middle_grad, low, heads, norm, router_grad


class Sum:
    def __init__(self, keep, send, stages, direct=None):
        self.keep, self.send, self.stages, self.came = keep, send, list(stages), None
        self.direct = direct

    def begin(self, *behind):
        send = after(self.send, *behind) if behind else self.send
        if self.stages:
            axis, bit, *self.split = self.stages.pop(0)
            self.came = swap(send, axis, bit)
        else:
            self.came = trade([self.keep] + send, "g")[1:]
        return self

    def end(self, *until):
        came = after(self.came, *until) if until else self.came
        self.came = None
        if isinstance(came, list):
            self.keep, self.direct = sum(a.astype(F32) for a in [self.keep, *came]), None
        elif self.split[0] is not None:
            self.keep, self.send = exchange(self.keep, came, *self.split)
        elif self.direct is None:
            self.keep = add(self.keep, came, F32)
        else:
            size = self.keep.shape[1] // 4
            self.keep, *self.send = [
                add(*(lax.dynamic_slice_in_dim(a, at * size, size, 1) for a in (self.keep, came)))
                for at in self.direct
            ]
        return self

    def finish(self):
        if self.came is not None:
            self.end()
        while self.stages or self.direct is not None:
            self.begin().end()
        return self.keep


def expert_sum(place, keep, send, lead):
    if lead == "r":
        near = [("r", 1, 0, place.low), ("g", 1, 0, place.high)]
    else:
        near = [("g", 1, 0, place.r), ("r", 1, 0, place.high)]
    return Sum(keep, send, near + [("g", 2, None, None)])


def direct_sum(place, keep, send):
    owners = [place.g ^ d for d in range(4)]
    return Sum(
        keep,
        send,
        [("c", 1, 0, place.y), ("y", 1, 1, place.r), ("r", 1, None, None)],
        [g % 2 * 2 + g // 2 for g in owners],
    )


def every_sum(place, keep, send, dim):
    return Sum(
        keep,
        send,
        [
            ("c", 1, 0, place.y),
            ("y", 1, dim, place.r),
            ("r", 1, dim, place.low),
            ("g", 1, dim, place.high),
            ("g", 2, None, None),
        ],
    )


def local(
    tokens,
    norm_attn,
    query_key_value_weight,
    attention_output_weight,
    norm_ffn,
    router,
    expert_in,
    expert_out,
    shared_gate_up_weight,
    shared_down_weight,
    block_lengths,
    routes,
    cotangent,
):
    place = Place()
    fast = place.lanes == 2 and place.rows_y == 2
    _, row_count, model_width = tokens.shape
    shard_index = lax.axis_index(DP)
    length = row_count * place.dp
    positions = shard_index * row_count + jnp.arange(row_count, dtype=jnp.int32)
    bounds = jnp.cumsum(block_lengths[0])
    cosine, sine = rope_table(positions)
    experts_total = router.shape[1]
    local_experts = expert_in.shape[1]
    groups = place.experts
    capacity = row_count * TOP * 5 // (4 * experts_total)
    chosen = routes[0]
    column = jnp.arange(experts_total, dtype=jnp.int32)
    picks = [(chosen[:, k : k + 1] == column[None, :]).astype(F32) for k in range(TOP)]
    flat_routes = chosen.reshape(row_count * TOP)
    route_hot = (flat_routes[:, None] == column[None, :]).astype(jnp.int32)
    earlier = jnp.cumsum(route_hot, axis=0) - route_hot
    slot_index = jnp.sum(earlier * route_hot, axis=1)
    partner = (flat_routes // local_experts) ^ lax.axis_index(EX)
    target = jnp.where(
        slot_index < capacity,
        (flat_routes % local_experts * groups + partner) * capacity + slot_index,
        -1,
    ).reshape(row_count, TOP)
    seats = jnp.arange(experts_total * capacity, dtype=jnp.int32)
    hots = [(target[:, k : k + 1] == seats[None, :]).astype(BF16) for k in range(TOP)]
    seated = [(target[:, k][None, :] == seats[:, None]).astype(BF16) for k in range(TOP)]
    upstream = cotangent[0]

    normalized_rows, own_q, own_kv = project(
        place, tokens[0], norm_attn, query_key_value_weight, cosine, sine
    )
    kv = trade(own_kv, "g")
    q = trade(own_q, "g")
    expert_in = jnp.transpose(expert_in, (1, 0, 2))
    expert_out = jnp.transpose(expert_out, (1, 0, 2))
    kv[1], expert_in, expert_out = lax.optimization_barrier((kv[1], expert_in, expert_out))
    if fast:
        kvs = kv + [swap(a, "r") for a in kv]
        lanes_of = [place.r, 1 - place.r]
    else:
        every_kv = [lax.all_gather(a, "r", axis=0, tiled=False) for a in kv]
        kvs = [a[i] for i in range(place.lanes) for a in every_kv]
        lanes_of = [jnp.int32(i) for i in range(place.lanes)]
    starts = (jnp.arange(place.groups, dtype=jnp.int32) * place.lanes + place.r) * row_count
    query_places = starts[:, None] + jnp.arange(row_count, dtype=jnp.int32)[None, :]
    limit = jnp.min(
        jnp.where(bounds[None, None, :] > query_places[:, :, None], bounds, length), axis=-1
    )
    span = row_count * place.lanes
    info = jnp.concatenate(
        [place.g[None], (jnp.max(limit, axis=1) + span - 1) // span, jnp.stack(lanes_of)]
    ).astype(jnp.int32)
    limit = limit[:, None, :]
    tables = [place.expert_table(model_width, lead) for lead in LEADS]
    shared_order = place.shared_table(model_width)
    q[0], *tables = lax.optimization_barrier((q[0], *tables, shared_order))
    *tables, shared_order = tables
    own_out, lse = attend(place, info, limit, q, kvs)
    traded_out = trade(own_out, "g")
    attended_low, middle, mixed_in, gates, send_rows, send_grads = middle_part(
        place,
        capacity,
        traded_out,
        tokens[0],
        upstream,
        attention_output_weight,
        norm_ffn,
        router,
        picks,
        seated,
    )
    arrived = trade(send_rows, EX)
    grad_arrived = trade(send_grads, EX)
    shared_result, shared_back, *shared_grads = ffn(
        True,
        place,
        shared_order,
        [mixed_in],
        [upstream],
        shared_gate_up_weight[None],
        shared_down_weight[None],
        0,
    )
    came_back, parts = [], []
    behind = [shared_result]
    if fast:
        shared_in = every_sum(place, *shared_grads[:2], 1)
        shared_out = every_sum(place, *shared_grads[2:], 1)
    for e in range(local_experts):
        own = [after(arrived[0], *behind)] + arrived[1:]
        results = ffn(
            False,
            place,
            tables[e],
            own,
            grad_arrived,
            expert_in,
            expert_out,
            e,
        )
        behind = [results[0]]
        came_back.append(trade(results[:groups], EX))
        parts.append(results[groups:])
    rets = [a for back in came_back for a in back]
    if fast:
        sums = [
            [expert_sum(place, *parts[e][k : k + 2], "r") for k in (0, 2)]
            + [expert_sum(place, *parts[e][4:], LEADS[e])]
            for e in range(local_experts)
        ]
        (first, second, third), (fourth, fifth, sixth) = sums
        both_done = parts[-1][0]
        first.begin()
        third.begin()
        second.begin(both_done)
        sixth.begin(both_done)
        shared_out.begin().end(both_done)
        shared_in.begin().end(both_done)
        first.end(both_done)
        third.end(both_done)
        shared_out.begin(rets[-1])
        shared_in.begin(rets[-1])
        rets[-1] = after(rets[-1], first.keep, third.keep, shared_in.keep, shared_out.keep)
    output, grad_middle, grad_attn_low, own_grad, grad_norm_ffn, grad_router = combine(
        place,
        hots,
        rets,
        gates,
        picks,
        upstream,
        middle,
        shared_result,
        shared_back,
        mixed_in,
        router,
        norm_ffn,
        attention_output_weight,
    )
    flat = lambda x: to_flat(place, x)
    own_grad = trade(own_grad, "g")
    if fast:
        third.begin()
        first.begin(own_grad[1])
        sixth.end(grad_middle).begin()
        second.end(grad_middle).begin(own_grad[1])
        own_grad[0] = after(own_grad[0], second.send, sixth.keep, shared_out.came)
    own_dq, own_dkv = attend_back(place, info, limit, lse, q, own_out, own_grad, kvs)
    dq = trade(own_dq, "g")
    grad_attn_low, own_dq[0] = lax.optimization_barrier((grad_attn_low, own_dq[0]))
    extra = beside(
        place,
        in_two(flat(grad_norm_ffn)[0]),
        flat(grad_router).T.reshape(model_width, groups, local_experts),
    )
    sides_out = weight_grad(place, flat(attended_low), grad_attn_low, extra)
    if fast:
        went_back = own_dkv[0]
        came = swap(after(own_dkv[1], first.came), "r")
        first.end(went_back).begin(dq[2], dq[3])
        third.end(went_back)
        sixth.end(went_back)
        came = after(came, second.came, sixth.send, third.send, first.send, *dq[1:])
        fourth.begin(came)
        fifth.begin(came)
        dkv = [add(own_dkv[0][d], came[d]) for d in range(place.groups)]
    else:
        dkv = [
            scatter(jnp.stack([a[d] for a in own_dkv]), "r", 0)[0] for d in range(place.groups)
        ]
    dkv = trade(dkv, "g")
    if fast:
        sum_out = direct_sum(place, *sides_out).begin()
        sixth.begin(dkv[1])
        third.begin(dkv[1])
        second.end(dkv[1]).begin()
        dkv[0] = after(dkv[0], fourth.came, first.came, shared_in.came, sum_out.came)
    grad_projected, grad_input, grad_norm_attn = finish(
        place,
        dq,
        dkv,
        query_key_value_weight,
        cosine,
        sine,
        tokens[0],
        norm_attn,
        grad_middle,
    )
    extra = beside(place, in_two(flat(grad_norm_attn)[0]), None)
    right = grad_projected
    if fast:
        fourth.end(grad_projected).begin()
        shared_in.end(grad_projected)
        shared_out.end(grad_projected)
        sum_out.end(grad_projected).begin()
        right = after(
            grad_projected, fifth.came, fourth.send, shared_in.send, shared_out.send, sum_out.came,
            sixth.came, second.came,
        )
    sides_qkv = weight_grad(place, flat(normalized_rows), right, extra)
    if fast:
        sum_qkv = direct_sum(place, *sides_qkv).begin()
        shared_in.begin()
        shared_out.begin(shared_in.send)
        sum_out.end(right).begin()
        fifth.end(right).begin()
        sum_qkv.end(right).begin()
        fourth.end(sum_qkv.send).begin()
        for chunk in (first, second, third, sixth):
            chunk.end(sum_qkv.send)
        sum_out.end(sum_qkv.send).begin()
        sum_qkv.end(shared_in.came).begin(shared_out.came, fourth.came)
        for chunk in (fifth, shared_in, shared_out):
            chunk.end(sum_qkv.send).begin()
        sum_qkv.end().begin(fifth.came, shared_in.came, shared_out.came)
        for chunk in (shared_in, shared_out):
            chunk.end(sum_qkv.send[0]).begin()
        for chunk in (fourth, fifth, sum_out):
            chunk.end(*sum_qkv.came)
        in_grads = [[s.finish() for s in row[:2]] for row in sums]
        out_grads = [row[2].finish() for row in sums]
        sum_shared_in, sum_shared_out = shared_in.finish()[0], shared_out.finish()
        sum_out, sum_qkv = sum_out.finish()[0], sum_qkv.finish()[0]
    else:
        in_grads = [
            [reduce_experts(place, *part[k : k + 2]) for k in (0, 2)] for part in parts
        ]
        out_grads = [reduce_experts(place, *part[4:]) for part in parts]
        sum_shared_in = reduce_shared_in(place, *shared_grads[:2])
        sum_shared_out = reduce_shared_out(place, *shared_grads[2:])
        sum_out, sum_qkv = reduce_weight(place, *sides_out), reduce_weight(place, *sides_qkv)
    own = model_width // place.experts
    sum_out, small = sum_out[:, :own], sum_out[:, own:]
    sum_norm_ffn, sum_router = small[:, 0] + small[:, 1], small[:, 2 : 2 + local_experts]
    sum_qkv, small = sum_qkv[:, : 3 * own], sum_qkv[:, 3 * own :]
    sum_norm_attn = small[:, 0] + small[:, 1]
    part_in = jnp.stack([jnp.concatenate(g, axis=1) for g in in_grads], axis=1)
    part_out = jnp.stack(out_grads, axis=1)
    return (
        output[None],
        grad_input[None],
        sum_norm_attn,
        sum_qkv,
        sum_out,
        sum_norm_ffn,
        sum_router,
        part_in,
        part_out,
        sum_shared_in,
        sum_shared_out.T,
    )


def solution(mesh):
    dp, experts = mesh.shape["dp"], mesh.shape["expert"]
    finer = Mesh(mesh.devices.reshape(4, dp // 4, experts // 2, 2), ("g", "r", "y", "c"))
    whole = P()
    return jax.shard_map(
        local,
        mesh=finer,
        in_specs=(
            P(EX, DP, None),
            whole,
            whole,
            whole,
            whole,
            whole,
            P(None, EX, None),
            P(None, EX, None),
            whole,
            whole,
            P(EX, None),
            P(EX, DP, None),
            P(EX, DP, None),
        ),
        out_specs=(
            P(EX, DP, None),
            P(EX, DP, None),
            P(DP),
            P(DP, EX),
            P(DP, EX),
            P(DP),
            P(DP, EX),
            P(DP, EX, None),
            P(DP, EX, None),
            P(DP, EX),
            P(DP, EX),
        ),
        check_vma=False,
    )
```
